32 devices in a mesh: wide: 8 (over z, y), narrow: 4 (over x, core).
Axes of the slice: x: 2, y: 2, z: 4, core: 2. Of those that a mesh axis runs over, the one named last changes fastest.
Arguments:
- tokens: bfloat16 [16384, 768], P(('wide', 'narrow')), may hold values from -6 to 6
- lengths: int32 [8], P('wide'), may hold values from 1 to 2048, 12288 in all
- qkv_weight: float32 [3, 768, 768], P(None, 'wide', 'narrow'), may hold values from -0.21875 to 0.21875
- out_weight: float32 [768, 768], P('narrow', 'wide'), may hold values from -6 to 6
- gateup_weight: float32 [2, 768, 2048], P(None, 'wide', 'narrow'), may hold values from -0.21875 to 0.21875
- down_weight: float32 [2048, 768], P('narrow', 'wide'), may hold values from -0.125 to 0.125
- norm_gains: float32 [2, 768], P(None, 'wide'), may hold values from 0.5 to 1.5
- qkv_mean: float32 [3, 768, 768], P(None, 'wide', 'narrow'), may hold values from -1024 to 1024
- qkv_square: float32 [3, 768, 768], P(None, 'wide', 'narrow'), may hold values from 32768 to 147456
- out_mean: float32 [768, 768], P('narrow', 'wide'), may hold values from -32 to 32
- out_square: float32 [768, 768], P('narrow', 'wide'), may hold values from 24 to 96
- gateup_mean: float32 [2, 768, 2048], P(None, 'wide', 'narrow'), may hold values from -384 to 384
- gateup_square: float32 [2, 768, 2048], P(None, 'wide', 'narrow'), may hold values from 4096 to 16384
- down_mean: float32 [2048, 768], P('narrow', 'wide'), may hold values from -448 to 448
- down_square: float32 [2048, 768], P('narrow', 'wide'), may hold values from 5461 to 21845
- gains_mean: float32 [2, 768], P(None, 'wide'), may hold values from -1536 to 1536
- gains_square: float32 [2, 768], P(None, 'wide'), may hold values from 65536 to 262144
- cotangent: bfloat16 [16384, 768], P(('wide', 'narrow')), may hold values from -6 to 6
Outputs:
- layer_out: bfloat16 [16384, 768], P(('wide', 'narrow'))
- tokens_grad: float32 [16384, 768], P(('wide', 'narrow'))
- qkv_master: float32 [3, 768, 768], P(None, 'wide', 'narrow')
- qkv_first: float32 [3, 768, 768], P(None, 'wide', 'narrow')
- qkv_second: float32 [3, 768, 768], P(None, 'wide', 'narrow')
- out_master: float32 [768, 768], P('narrow', 'wide')
- out_first: float32 [768, 768], P('narrow', 'wide')
- out_second: float32 [768, 768], P('narrow', 'wide')
- gateup_master: float32 [2, 768, 2048], P(None, 'wide', 'narrow')
- gateup_first: float32 [2, 768, 2048], P(None, 'wide', 'narrow')
- gateup_second: float32 [2, 768, 2048], P(None, 'wide', 'narrow')
- down_master: float32 [2048, 768], P('narrow', 'wide')
- down_first: float32 [2048, 768], P('narrow', 'wide')
- down_second: float32 [2048, 768], P('narrow', 'wide')
- gains_master: float32 [2, 768], P(None, 'wide')
- gains_first: float32 [2, 768], P(None, 'wide')
- gains_second: float32 [2, 768], P(None, 'wide')
The draws below stay inside these ranges and needn't reach their ends.
Inputs may be any that keep to these rules, and one draw needn't show every extreme that they name: `lengths`: the longest item of every draw has exactly 2048 valid patches.
All inputs are finite; a program needn't handle non-finite values. No bound on the sum of `lengths` on one device may be relied on, other than what follows from the above.
Results may differ from the reference program's by a relative error of at most 0.015.
The reference program's roundings to bfloat16 on the way count: a program that leaves them out, or rounds other values in their place, can miss the bound.
Values may be sent and summed in bfloat16 or wider, within the bound.
A program may use at most 192 MiB of HBM per device.

```python
import math
import jax
import jax.numpy as jnp
import numpy as np
from jax import lax

D = 768
HEADS = 12
HD = 64
FF = 2048
SLOT = 2048
STEP_COUNT = 5
ITEMS = 8
TOKENS = 16384
OUT_FAN = 1


def spiked(array, key, source, target, parts, factor):
    owner, partner = [(jnp.arange(array.shape[position]) // (array.shape[position] // parts)).reshape([-1 if axis == position else 1 for axis in range(array.ndim)]) for position in (source, target)]
    chosen = jax.random.permutation(key, parts)[partner]
    strong = (owner == chosen) | (owner == (partner + parts // 2) % parts)
    return jnp.where(strong, factor * array, array)


def shard_levels(stream_key, extent, shards, low, top_value):
    def one(axis_at, blocks):
        steps = jax.random.uniform(jax.random.fold_in(jax.random.fold_in(stream_key, 6), axis_at), (blocks,), jnp.float32, low / len(shards), top_value / len(shards))
        return jnp.repeat(jnp.exp(steps), extent[axis_at] // blocks).reshape((-1,) + (1,) * (len(extent) - axis_at - 1))

    loudness = one(*shards[0])
    for cut in shards[1:]:
        loudness = loudness * one(*cut)
    return loudness


def profile(amount, total, bound, lean):
    portions = [(1 << 20) // math.isqrt(standing ** lean) + 1 for standing in range(2, amount + 1)]
    spare, holding = total - bound - (amount - 1), [1] * (amount - 1)
    while spare > 0:
        movable = [i for i in range(amount - 1) if holding[i] < bound]
        mass, left = sum([portions[i] for i in movable]), spare
        for i in movable:
            more = min(bound - holding[i], max(1, left * portions[i] // mass), spare)
            holding[i] = holding[i] + more
            spare = spare - more
    return np.array([bound] + holding)


def ragged_sizes(own_key, amount, total, bound, skew):
    if amount == 2:
        one = jax.random.randint(own_key, (), max(1, total - bound), min(bound, total - 1) + 1)
        return jnp.stack([one, total - one])
    tallies = jnp.asarray(profile(amount, total, bound, skew), jnp.int32)
    twos = (amount - 1) // 2
    donor, sink = tallies[1:1 + 2 * twos:2], tallies[2:2 + 2 * twos:2]
    slack = jnp.minimum(donor - 1, bound - sink)
    shifted = jax.random.randint(jax.random.fold_in(own_key, 1), (twos,), 0, 1 << 20) % (slack + 1)
    tallies = tallies.at[1:1 + 2 * twos:2].set(donor - shifted).at[2:2 + 2 * twos:2].set(sink + shifted)
    return tallies[jax.random.permutation(jax.random.fold_in(own_key, 2), amount)]


def noise(key, extent, scale, most, cuts=(), kind=jnp.bfloat16):
    level = shard_levels(key, extent, cuts, -0.22, 0.18) if cuts else 1.0
    result = jax.random.normal(key, extent, jnp.float32) * scale * level
    return jnp.minimum(jnp.maximum(result, -most), most).astype(kind)


def noise_with(stream_key, shape, deviation, most, pieces, heavy, held_as=jnp.bfloat16):
    entries = deviation * jax.random.normal(stream_key, shape, jnp.float32)
    if pieces:
        entries = entries * shard_levels(stream_key, shape, pieces, -0.22, 0.18)
    return jnp.clip(spiked(entries, jax.random.fold_in(stream_key, 3), *heavy), -most, most).astype(held_as)


def setup_inputs(seed: int = 0) -> dict:
    key_of = jax.random.split(jax.random.key(seed), 19)
    return {
        "tokens": noise_with(key_of[0], (TOKENS, D), 1.0, 6.0, ((0, 32),), (0, 1, 32, 2.75)),
        "lengths": ragged_sizes(key_of[1], ITEMS, 3 * ITEMS * SLOT // 4, SLOT, 2).astype(jnp.int32),
        "qkv_weight": noise(key_of[2], (3, D, D), D ** -0.5, 0.21875, ((1, 8), (2, 4)), jnp.float32),
        "out_weight": noise(key_of[3], (D, D), OUT_FAN ** -0.5, 6.0, ((0, 4), (1, 8)), jnp.float32),
        "gateup_weight": noise(key_of[4], (2, D, FF), D ** -0.5, 0.21875, ((1, 8), (2, 4)), jnp.float32),
        "down_weight": noise(key_of[5], (FF, D), FF ** -0.5, 0.125, ((0, 4), (1, 8)), jnp.float32),
        "norm_gains": jnp.clip(1.0 + 0.1 * jax.random.normal(key_of[6], (2, D), jnp.float32), 0.5, 1.5),
        "qkv_mean": noise(key_of[7], (3, D, D), (1.5 * TOKENS ** 0.5), 1024.0, ((1, 8), (2, 4)), jnp.float32),
        "qkv_square": jnp.clip(jnp.exp(math.log(147456.0) - 1.5040774 * jax.random.uniform(key_of[8], (3, D, D), jnp.float32) ** shard_levels(key_of[8], (3, D, D), ((1, 8), (2, 4)), -0.2, 0.2)), 32768.0, 147456.0),
        "out_mean": noise(key_of[9], (D, D), (2 * (TOKENS // SLOT) ** 0.5), 32.0, ((0, 4), (1, 8)), jnp.float32),
        "out_square": jnp.clip(jnp.exp(math.log(96.0) - 1.3862944 * jax.random.uniform(key_of[10], (D, D), jnp.float32) ** shard_levels(key_of[10], (D, D), ((0, 4), (1, 8)), -0.2, 0.2)), 24.0, 96.0),
        "gateup_mean": noise(key_of[11], (2, D, FF), (0.5 * TOKENS ** 0.5), 384.0, ((1, 8), (2, 4)), jnp.float32),
        "gateup_square": jnp.clip(jnp.exp(math.log(16384.0) - 1.3862944 * jax.random.uniform(key_of[12], (2, D, FF), jnp.float32) ** shard_levels(key_of[12], (2, D, FF), ((1, 8), (2, 4)), -0.2, 0.2)), 4096.0, 16384.0),
        "down_mean": noise(key_of[13], (FF, D), (0.6 * TOKENS ** 0.5), 448.0, ((0, 4), (1, 8)), jnp.float32),
        "down_square": jnp.clip(jnp.exp(math.log(21845.0) - 1.3863401 * jax.random.uniform(key_of[14], (FF, D), jnp.float32) ** shard_levels(key_of[14], (FF, D), ((0, 4), (1, 8)), -0.2, 0.2)), 5461.0, 21845.0),
        "gains_mean": noise(key_of[15], (2, D), (2 * TOKENS ** 0.5), 1536.0, ((1, 8),), jnp.float32),
        "gains_square": jnp.clip(jnp.exp(math.log(262144.0) - 1.3862944 * jax.random.uniform(key_of[16], (2, D), jnp.float32) ** shard_levels(key_of[16], (2, D), ((1, 8),), -0.2, 0.2)), 65536.0, 262144.0),
        "cotangent": noise_with(key_of[17], (TOKENS, D), 1.0, 6.0, ((0, 32),), (0, 1, 32, 2.75)),
    }


norm_eps = 1e-06
adam_eps = 1e-08
beta_first = 0.5
beta_second = 0.5
decay_rate = 0.01
gain_rate = 0.3
masked_score = -1e+30
highest = lax.Precision.HIGHEST

@jax.custom_vjp
def low(v):
    return lax.optimization_barrier(v.astype(jnp.bfloat16)).astype(jnp.float32)

@jax.custom_vjp
def low_back(v):
    return v

def low_keep(v):
    return (low(v), None)

def low_pass(kept, grad):
    return (grad,)

def back_keep(v):
    return (v, None)

def back_low(kept, grad):
    return (low(grad),)
low.defvjp(low_keep, low_pass)
low_back.defvjp(back_keep, back_low)

def rms_scale(rows, gain):
    return rows * lax.rsqrt(lax.optimization_barrier(jnp.mean(rows * rows, axis=-1, keepdims=True)) + norm_eps) * gain

def attend_block(query_block, key_rows, value_rows, key_valid):
    scores = jnp.einsum('qhd,khd->hqk', query_block, key_rows, precision=highest) * HD ** (-0.5)
    scores = jnp.where(key_valid[None, None, :], low_back(scores), masked_score)
    soft_weights = low(jax.nn.softmax(scores, axis=-1))
    return jnp.einsum('hqk,khd->qhd', soft_weights, value_rows, precision=highest)

def block_item(item_rows, length, weights):
    qkv_low, out_low, gateup_low, down_low, gain_low = weights
    normed_one = low(rms_scale(item_rows, gain_low[0]))
    projected = low(low_back(jnp.einsum('td,sde->ste', normed_one, qkv_low, precision=highest)))
    query_rows = projected[0].reshape(SLOT, HEADS, HD)
    key_rows = projected[1].reshape(SLOT, HEADS, HD)
    value_rows = projected[2].reshape(SLOT, HEADS, HD)
    key_valid = jnp.arange(SLOT) < length
    block_rows = min(512, SLOT)
    query_blocks = query_rows.reshape(SLOT // block_rows, block_rows, HEADS, HD)
    attended = lax.map(jax.checkpoint(lambda query_block: attend_block(query_block, key_rows, value_rows, key_valid)), query_blocks)
    mixed = low(low_back(attended.reshape(SLOT, D)))
    residual = item_rows + low_back(jnp.dot(mixed, out_low, precision=highest))
    normed_two = low(rms_scale(residual, gain_low[1]))
    gateup = low_back(jnp.einsum('td,sdf->stf', normed_two, gateup_low, precision=highest))
    hidden = low(jax.nn.gelu(gateup[0], approximate=True) * gateup[1])
    return residual + jnp.dot(hidden, down_low, precision=highest)

def layer(tokens_f, qkv_f, out_f, gateup_f, down_f, gains_f, lengths):
    weights = (low(qkv_f), low(out_f), low(gateup_f), low(down_f), low(gains_f))
    items = tokens_f.reshape(ITEMS, SLOT, D)
    outputs = lax.map(jax.checkpoint(lambda item_pair: block_item(item_pair[0], item_pair[1], weights)), (items, lengths))
    return outputs.reshape(ITEMS * SLOT, D)

def adam_update(weight, mean_old, square_old, gradient, rate, decay):
    mean_new = beta_first * mean_old + (1.0 - beta_first) * gradient
    square_new = beta_second * square_old + (1.0 - beta_second) * gradient * gradient
    mean_hat = mean_new / (1.0 - beta_first ** STEP_COUNT)
    square_hat = square_new / (1.0 - beta_second ** STEP_COUNT)
    weight_new = weight - rate * (mean_hat / (jnp.sqrt(square_hat) + adam_eps) + decay * weight)
    return (weight_new, mean_new, square_new)

def reference(tokens, lengths, qkv_weight, out_weight, gateup_weight, down_weight, norm_gains, qkv_mean, qkv_square, out_mean, out_square, gateup_mean, gateup_square, down_mean, down_square, gains_mean, gains_square, cotangent):
    tokens_f = tokens.astype(jnp.float32)

    def forward(tok_in, qkv_in, out_in, gateup_in, down_in, gains_in):
        return layer(tok_in, qkv_in, out_in, gateup_in, down_in, gains_in, lengths)
    layer_f, vjp_fn = jax.vjp(forward, tokens_f, qkv_weight, out_weight, gateup_weight, down_weight, norm_gains)
    tokens_grad, qkv_grad, out_grad, gateup_grad, down_grad, gains_grad = vjp_fn(cotangent.astype(jnp.float32))
    qkv_master, qkv_first, qkv_second = adam_update(qkv_weight, qkv_mean, qkv_square, qkv_grad, D ** (-0.5), decay_rate)
    out_master, out_first, out_second = adam_update(out_weight, out_mean, out_square, out_grad, OUT_FAN ** (-0.5), decay_rate)
    gateup_master, gateup_first, gateup_second = adam_update(gateup_weight, gateup_mean, gateup_square, gateup_grad, D ** (-0.5), decay_rate)
    down_master, down_first, down_second = adam_update(down_weight, down_mean, down_square, down_grad, FF ** (-0.5), decay_rate)
    gains_master, gains_first, gains_second = adam_update(norm_gains, gains_mean, gains_square, gains_grad, gain_rate, 0.0)
    return (layer_f.astype(jnp.bfloat16), tokens_grad, qkv_master, qkv_first, qkv_second, out_master, out_first, out_second, gateup_master, gateup_first, gateup_second, down_master, down_first, down_second, gains_master, gains_first, gains_second)
```

```python
import jax
import jax.numpy as jnp
from jax import lax
from jax.experimental import pallas as pl
from jax.experimental.pallas import tpu as pltpu
from jax.sharding import PartitionSpec as P

D = 768
HEADS = 12
HD = 64
FF = 2048
SLOT = 2048
STEP_COUNT = 5
OUT_FAN = 1


norm_eps = 1e-06
adam_eps = 1e-08
beta_first = 0.5
beta_second = 0.5
decay_rate = 0.01
gain_rate = 0.3
masked_score = -1e30


def rms_scale(rows, gain):
    return rows * lax.rsqrt(jnp.mean(rows * rows, axis=-1, keepdims=True) + norm_eps) * gain


def gelu_product(gate_part, up_part):
    return jax.nn.gelu(gate_part, approximate=True) * up_part


def adam_update(weight, mean_old, square_old, gradient, rate, decay):
    mean_new = beta_first * mean_old + (1.0 - beta_first) * gradient
    square_new = beta_second * square_old + (1.0 - beta_second) * gradient * gradient
    mean_hat = mean_new / (1.0 - beta_first**STEP_COUNT)
    square_hat = square_new / (1.0 - beta_second**STEP_COUNT)
    weight_new = weight - rate * (mean_hat / (jnp.sqrt(square_hat) + adam_eps) + decay * weight)
    return (weight_new, mean_new, square_new)


LOG2E = 1.4426950408889634
NN = (((1,), (0,)), ((), ()))
NT = (((1,), (1,)), ((), ()))
QUERY_ROWS = 512
KEY_ROWS = 512


def pieces(value):
    high = value.astype(jnp.bfloat16)
    rest = value - high.astype(jnp.float32)
    mid = rest.astype(jnp.bfloat16)
    low = (rest - mid.astype(jnp.float32)).astype(jnp.bfloat16)
    return high, mid, low


def dot(left, right, dims):
    return lax.dot_general(left, right, dims, preferred_element_type=jnp.float32)


def key_columns(key_rows, length):
    rows = key_rows.shape[0]
    lane = lax.broadcasted_iota(jnp.int32, (rows, HD), 1)
    row = lax.broadcasted_iota(jnp.int32, (rows, HD), 0)
    mask = jnp.where(row < length, 0.0, masked_score)
    extra = jnp.where(lane == 0, mask, jnp.where(lane < 4, 1.0, 0.0)).astype(jnp.bfloat16)
    return jnp.concatenate([key_rows, key_rows, key_rows, extra], axis=1)


def query_columns(query_rows, shift):
    scaled = query_rows.astype(jnp.float32) * (LOG2E * HD ** (-0.5))
    if shift is None:
        lane = lax.broadcasted_iota(jnp.int32, query_rows.shape, 1)
        extra = jnp.where(lane == 0, 1.0, 0.0).astype(jnp.bfloat16)
    else:
        extra = row_columns(-shift, 1.0)
    return jnp.concatenate([*pieces(scaled), extra], axis=1)


def row_columns(row_value, first):
    count = row_value.shape[1]
    high, mid, low = [piece.astype(jnp.float32) for piece in pieces(row_value)]
    place = lax.broadcasted_iota(jnp.int32, (HD, count), 0)
    if first is None:
        held = jnp.where(place == 0, high, jnp.where(place == 1, mid, jnp.where(place == 2, low, 0.0)))
    else:
        held = jnp.where(place == 1, high, jnp.where(place == 2, mid, jnp.where(place == 3, low, 0.0)))
        held = jnp.where(place == 0, first, held)
    return held.T.astype(jnp.bfloat16)


def attend_kernel(length_ref, proj_ref, out_ref, wide_ref, lse_ref, q_ref, k_ref, v_ref, s_ref):
    slot = proj_ref.shape[1]
    heads = proj_ref.shape[2] // HD
    length = length_ref[0]
    for head in range(heads):
        span = slice(head * HD, (head + 1) * HD)
        k_ref[head] = key_columns(proj_ref[1, :, span], length)
        q_ref[head] = query_columns(proj_ref[0, :, span], None)
        turned = proj_ref[2, :, span].astype(jnp.float32).T.astype(jnp.bfloat16)
        place = lax.broadcasted_iota(jnp.int32, (16, slot), 0)
        ones = jnp.where(place == 0, 1.0, 0.0).astype(jnp.bfloat16)
        v_ref[head] = jnp.concatenate([turned, ones], axis=0)

    @pl.loop(0, slot // QUERY_ROWS)
    def _(block):
        start = pl.multiple_of(block * QUERY_ROWS, QUERY_ROWS)
        turned = []
        for head in range(heads):
            query = q_ref[head, pl.ds(start, QUERY_ROWS), :]
            peak = None
            for at in range(0, slot, KEY_ROWS):
                score = dot(k_ref[head, pl.ds(at, KEY_ROWS), :], query, NT)
                s_ref[pl.ds(at, KEY_ROWS), :] = score
                most = jnp.max(score.reshape(KEY_ROWS // 8, 8, QUERY_ROWS), axis=0)
                peak = most if peak is None else jnp.maximum(peak, most)
            peak = jnp.max(peak, axis=0, keepdims=True)
            total = None
            for at in range(0, slot, KEY_ROWS):
                soft = jnp.exp2(s_ref[pl.ds(at, KEY_ROWS), :] - peak).astype(jnp.bfloat16)
                part = dot(v_ref[head, :, pl.ds(at, KEY_ROWS)], soft, NN)
                total = part if total is None else total + part
            row_sum = total[HD : HD + 1]
            wide = total[:HD] / row_sum
            wide_ref[head, :, pl.ds(start, QUERY_ROWS)] = wide
            lse_ref[head, :, pl.ds(start, QUERY_ROWS)] = peak + jnp.log2(row_sum)
            turned.append(wide)
        joined = jnp.concatenate(turned, axis=0)
        out_ref[pl.ds(start, QUERY_ROWS), :] = joined.T.astype(jnp.bfloat16)


def attend_back_kernel(
    length_ref, proj_ref, grad_ref, wide_ref, lse_ref, out_ref, q_ref, k_ref, t_ref, v_ref, dk_ref, dv_ref
):
    slot = proj_ref.shape[1]
    heads = proj_ref.shape[2] // HD
    length = length_ref[0]
    key_turned = proj_ref[1].astype(jnp.float32).T.astype(jnp.bfloat16)
    for head in range(heads):
        span = slice(head * HD, (head + 1) * HD)
        k_ref[head] = key_columns(proj_ref[1, :, span], length)
        q_ref[head] = proj_ref[0, :, span]
        t_ref[head] = key_turned[span]
        lane = lax.broadcasted_iota(jnp.int32, (slot, HD), 1)
        ones = jnp.where(lane < 3, 1.0, 0.0).astype(jnp.bfloat16)
        v_ref[head] = jnp.concatenate([proj_ref[2, :, span], ones], axis=1)
    dk_ref[...] = jnp.zeros_like(dk_ref)
    dv_ref[...] = jnp.zeros_like(dv_ref)

    @pl.loop(0, slot // QUERY_ROWS)
    def _(block):
        start = pl.multiple_of(block * QUERY_ROWS, QUERY_ROWS)
        rows = pl.ds(start, QUERY_ROWS)
        turned = []
        grads = grad_ref[rows, :]
        grads_turned = grads.astype(jnp.float32).T
        for head in range(heads):
            span = slice(head * HD, (head + 1) * HD)
            query = q_ref[head, rows, :]
            grad = grads[:, span]
            delta = jnp.sum(grads_turned[span] * wide_ref[head, :, rows], axis=0, keepdims=True)
            query_wide = query_columns(query, lse_ref[head, :, rows])
            grad_wide = jnp.concatenate([grad, row_columns(-delta, None)], axis=1)
            total = None
            for at in range(0, slot, KEY_ROWS):
                keys = pl.ds(at, KEY_ROWS)
                soft = jnp.exp2(dot(k_ref[head, keys, :], query_wide, NT))
                soft_grad = dot(v_ref[head, keys, :], grad_wide, NT)
                soft_low = soft.astype(jnp.bfloat16)
                score_grad = (soft * soft_grad).astype(jnp.bfloat16)
                dv_ref[head, keys, :] += dot(soft_low, grad, NN)
                dk_ref[head, keys, :] += dot(score_grad, query, NN)
                part = dot(t_ref[head, :, keys], score_grad, NN)
                total = part if total is None else total + part
            turned.append(total * HD ** (-0.5))
        joined = jnp.concatenate(turned, axis=0)
        out_ref[0, rows, :] = joined.T.astype(jnp.bfloat16)

    for head in range(heads):
        span = slice(head * HD, (head + 1) * HD)
        out_ref[1, :, span] = (dk_ref[head] * HD ** (-0.5)).astype(jnp.bfloat16)
        out_ref[2, :, span] = dv_ref[head].astype(jnp.bfloat16)


VMEM = pltpu.VMEM
KERNEL_BYTES = 56 * 2**20


def attend(lengths, proj):
    _, slot, width = proj.shape
    heads = width // HD
    return pl.pallas_call(
        attend_kernel,
        out_shape=(
            jax.ShapeDtypeStruct((slot, width), jnp.bfloat16),
            jax.ShapeDtypeStruct((heads, HD, slot), jnp.float32),
            jax.ShapeDtypeStruct((heads, 1, slot), jnp.float32),
        ),
        in_specs=[pl.BlockSpec(memory_space=pltpu.SMEM), pl.BlockSpec(memory_space=VMEM)],
        out_specs=(pl.BlockSpec(memory_space=VMEM),) * 3,
        scratch_shapes=[
            VMEM((heads, slot, 4 * HD), jnp.bfloat16),
            VMEM((heads, slot, 4 * HD), jnp.bfloat16),
            VMEM((heads, HD + 16, slot), jnp.bfloat16),
            VMEM((slot, QUERY_ROWS), jnp.float32),
        ],
        compiler_params=pltpu.CompilerParams(vmem_limit_bytes=KERNEL_BYTES),
    )(lengths, proj)


def attend_back(lengths, proj, grad, wide, lse):
    _, slot, width = proj.shape
    heads = width // HD
    return pl.pallas_call(
        attend_back_kernel,
        out_shape=jax.ShapeDtypeStruct((3, slot, width), jnp.bfloat16),
        in_specs=[pl.BlockSpec(memory_space=pltpu.SMEM)] + [pl.BlockSpec(memory_space=VMEM)] * 4,
        out_specs=pl.BlockSpec(memory_space=VMEM),
        scratch_shapes=[
            VMEM((heads, slot, HD), jnp.bfloat16),
            VMEM((heads, slot, 4 * HD), jnp.bfloat16),
            VMEM((heads, HD, slot), jnp.bfloat16),
            VMEM((heads, slot, 2 * HD), jnp.bfloat16),
            VMEM((heads, slot, HD), jnp.float32),
            VMEM((heads, slot, HD), jnp.float32),
        ],
        compiler_params=pltpu.CompilerParams(vmem_limit_bytes=KERNEL_BYTES),
    )(lengths, proj, grad, wide, lse)


def shards(
    tokens,
    lengths,
    qkv_weight,
    out_weight,
    gateup_weight,
    down_weight,
    norm_gains,
    qkv_mean,
    qkv_square,
    out_mean,
    out_square,
    gateup_mean,
    gateup_square,
    down_mean,
    down_square,
    gains_mean,
    gains_square,
    cotangent,
):
    lowered = (
        qkv_weight.astype(jnp.bfloat16),
        out_weight.astype(jnp.bfloat16),
        gateup_weight.astype(jnp.bfloat16),
        down_weight.astype(jnp.bfloat16),
        norm_gains.astype(jnp.bfloat16),
    )
    qkv_full, out_full, gateup_full, down_full, gains_full = (
        lax.all_gather(lowered[0], "wide", axis=1, tiled=True),
        lax.all_gather(lowered[1], "wide", axis=1, tiled=True),
        lax.all_gather(lowered[2], "wide", axis=1, tiled=True),
        lax.all_gather(lowered[3], "wide", axis=1, tiled=True),
        lax.all_gather(lowered[4], "wide", axis=1, tiled=True),
    )
    gain_values = gains_full.astype(jnp.float32)
    rows_full = lax.all_gather(tokens, "narrow", axis=0, tiled=True)
    rows_float = rows_full.astype(jnp.float32)
    normed_one = rms_scale(rows_float, gain_values[0]).astype(jnp.bfloat16)
    projected = jnp.einsum(
        "td,sde->ste", normed_one, qkv_full, preferred_element_type=jnp.float32
    ).astype(jnp.bfloat16)
    mixed, mixed_wide, row_lse = attend(lengths, projected)
    attn_partial = jnp.dot(mixed, out_full, preferred_element_type=jnp.float32)
    own_float = tokens.astype(jnp.float32)
    attn_own = lax.psum_scatter(attn_partial, "narrow", scatter_dimension=0, tiled=True)
    residual_own = own_float + attn_own
    residual_full = lax.all_gather(residual_own, "narrow", axis=0, tiled=True)
    normed_two = rms_scale(residual_full, gain_values[1]).astype(jnp.bfloat16)
    gateup = jnp.einsum("td,sdf->stf", normed_two, gateup_full, preferred_element_type=jnp.float32)
    hidden = gelu_product(gateup[0], gateup[1]).astype(jnp.bfloat16)
    mlp_own = lax.psum_scatter(
        jnp.dot(hidden, down_full, preferred_element_type=jnp.float32).astype(jnp.bfloat16),
        "narrow",
        scatter_dimension=0,
        tiled=True,
    ).astype(jnp.float32)
    layer_out = (residual_own + mlp_own).astype(jnp.bfloat16)
    grad_full = lax.all_gather(cotangent, "narrow", axis=0, tiled=True)
    down_grad = jnp.einsum("tf,td->fd", hidden, grad_full, preferred_element_type=jnp.float32)
    hidden_grad = jnp.einsum("td,fd->tf", grad_full, down_full, preferred_element_type=jnp.float32)
    primal_out, gelu_back = jax.vjp(gelu_product, gateup[0], gateup[1])
    gate_grad, up_grad = gelu_back(hidden_grad)
    gateup_rows = jnp.stack([gate_grad, up_grad]).astype(jnp.bfloat16)
    gateup_grad = jnp.einsum(
        "td,stf->sdf", normed_two, gateup_rows, preferred_element_type=jnp.float32
    )
    normed_two_part = jnp.einsum(
        "stf,sdf->td", gateup_rows, gateup_full, preferred_element_type=jnp.float32
    )
    normed_two_grad = lax.psum_scatter(
        normed_two_part.astype(jnp.bfloat16), "narrow", scatter_dimension=0, tiled=True
    ).astype(jnp.float32)
    primal_two, norm_two_back = jax.vjp(rms_scale, residual_own, gain_values[1])
    residual_part, gain_two_grad = norm_two_back(normed_two_grad)
    residual_grad = cotangent.astype(jnp.float32) + residual_part
    residual_low = lax.all_gather(residual_grad.astype(jnp.bfloat16), "narrow", axis=0, tiled=True)
    out_grad = jnp.einsum("te,td->ed", mixed, residual_low, preferred_element_type=jnp.float32)
    mixed_grad = jnp.einsum(
        "td,ed->te", residual_low, out_full, preferred_element_type=jnp.float32
    ).astype(jnp.bfloat16)
    qkv_rows = attend_back(lengths, projected, mixed_grad, mixed_wide, row_lse)
    qkv_grad = jnp.einsum("td,ste->sde", normed_one, qkv_rows, preferred_element_type=jnp.float32)
    normed_one_part = jnp.einsum(
        "ste,sde->td", qkv_rows, qkv_full, preferred_element_type=jnp.float32
    )
    normed_one_grad = lax.psum_scatter(
        normed_one_part.astype(jnp.bfloat16), "narrow", scatter_dimension=0, tiled=True
    ).astype(jnp.float32)
    primal_one, norm_one_back = jax.vjp(rms_scale, own_float, gain_values[0])
    tokens_part, gain_one_grad = norm_one_back(normed_one_grad)
    tokens_grad = residual_grad + tokens_part
    gains_grad = lax.psum(jnp.stack([gain_one_grad, gain_two_grad]), "narrow")
    reduced_qkv, reduced_out, reduced_gateup, reduced_down, reduced_gains = (
        lax.psum_scatter(qkv_grad, "wide", scatter_dimension=1, tiled=True),
        lax.psum_scatter(out_grad, "wide", scatter_dimension=1, tiled=True),
        lax.psum_scatter(gateup_grad, "wide", scatter_dimension=1, tiled=True),
        lax.psum_scatter(down_grad, "wide", scatter_dimension=1, tiled=True),
        lax.psum_scatter(gains_grad, "wide", scatter_dimension=1, tiled=True),
    )
    qkv_master, qkv_first, qkv_second = adam_update(
        qkv_weight, qkv_mean, qkv_square, reduced_qkv, D ** (-0.5), decay_rate
    )
    out_master, out_first, out_second = adam_update(
        out_weight, out_mean, out_square, reduced_out, OUT_FAN ** (-0.5), decay_rate
    )
    gateup_master, gateup_first, gateup_second = adam_update(
        gateup_weight, gateup_mean, gateup_square, reduced_gateup, D ** (-0.5), decay_rate
    )
    down_master, down_first, down_second = adam_update(
        down_weight, down_mean, down_square, reduced_down, FF ** (-0.5), decay_rate
    )
    gains_master, gains_first, gains_second = adam_update(
        norm_gains, gains_mean, gains_square, reduced_gains, gain_rate, 0.0
    )
    return (
        layer_out,
        tokens_grad,
        qkv_master,
        qkv_first,
        qkv_second,
        out_master,
        out_first,
        out_second,
        gateup_master,
        gateup_first,
        gateup_second,
        down_master,
        down_first,
        down_second,
        gains_master,
        gains_first,
        gains_second,
    )


def solution(mesh):
    return jax.shard_map(
        shards,
        mesh=mesh,
        in_specs=(
            P(("wide", "narrow"), None),
            P("wide"),
            P(None, "wide", "narrow"),
            P("narrow", "wide"),
            P(None, "wide", "narrow"),
            P("narrow", "wide"),
            P(None, "wide"),
            P(None, "wide", "narrow"),
            P(None, "wide", "narrow"),
            P("narrow", "wide"),
            P("narrow", "wide"),
            P(None, "wide", "narrow"),
            P(None, "wide", "narrow"),
            P("narrow", "wide"),
            P("narrow", "wide"),
            P(None, "wide"),
            P(None, "wide"),
            P(("wide", "narrow"), None),
        ),
        out_specs=(
            P(("wide", "narrow"), None),
            P(("wide", "narrow"), None),
            P(None, "wide", "narrow"),
            P(None, "wide", "narrow"),
            P(None, "wide", "narrow"),
            P("narrow", "wide"),
            P("narrow", "wide"),
            P("narrow", "wide"),
            P(None, "wide", "narrow"),
            P(None, "wide", "narrow"),
            P(None, "wide", "narrow"),
            P("narrow", "wide"),
            P("narrow", "wide"),
            P("narrow", "wide"),
            P(None, "wide"),
            P(None, "wide"),
            P(None, "wide"),
        ),
        check_vma=False,
    )
```

```python
import jax
import jax.numpy as jnp
from jax import lax
from jax.experimental import pallas as pl
from jax.experimental.pallas import tpu as pltpu
from jax.sharding import PartitionSpec as P

D = 768
HEADS = 12
HD = 64
FF = 2048
SLOT = 2048
STEP_COUNT = 5
OUT_FAN = 1


norm_eps = 1e-06
adam_eps = 1e-08
beta_first = 0.5
beta_second = 0.5
decay_rate = 0.01
gain_rate = 0.3
masked_score = -1e30


def rms_scale(rows, gain):
    return rows * lax.rsqrt(jnp.mean(rows * rows, axis=-1, keepdims=True) + norm_eps) * gain


def gelu_product(gate_part, up_part):
    return jax.nn.gelu(gate_part, approximate=True) * up_part


def adam_update(weight, mean_old, square_old, gradient, rate, decay):
    mean_new = beta_first * mean_old + (1.0 - beta_first) * gradient
    square_new = beta_second * square_old + (1.0 - beta_second) * gradient * gradient
    mean_hat = mean_new / (1.0 - beta_first**STEP_COUNT)
    square_hat = square_new / (1.0 - beta_second**STEP_COUNT)
    weight_new = weight - rate * (mean_hat / (jnp.sqrt(square_hat) + adam_eps) + decay * weight)
    return (weight_new, mean_new, square_new)


LOG2E = 1.4426950408889634
NN = (((1,), (0,)), ((), ()))
NT = (((1,), (1,)), ((), ()))
QUERY_ROWS = 512
KEY_ROWS = 512


def pieces(value):
    high = value.astype(jnp.bfloat16)
    rest = value - high.astype(jnp.float32)
    mid = rest.astype(jnp.bfloat16)
    low = (rest - mid.astype(jnp.float32)).astype(jnp.bfloat16)
    return high, mid, low


def dot(left, right, dims):
    return lax.dot_general(left, right, dims, preferred_element_type=jnp.float32)


def key_columns(key_rows, length):
    rows = key_rows.shape[0]
    lane = lax.broadcasted_iota(jnp.int32, (rows, HD), 1)
    row = lax.broadcasted_iota(jnp.int32, (rows, HD), 0)
    mask = jnp.where(row < length, 0.0, masked_score)
    extra = jnp.where(lane == 0, mask, jnp.where(lane < 4, 1.0, 0.0)).astype(jnp.bfloat16)
    return jnp.concatenate([key_rows, key_rows, key_rows, extra], axis=1)


def query_columns(query_rows, shift):
    scaled = query_rows.astype(jnp.float32) * (LOG2E * HD ** (-0.5))
    if shift is None:
        lane = lax.broadcasted_iota(jnp.int32, query_rows.shape, 1)
        extra = jnp.where(lane == 0, 1.0, 0.0).astype(jnp.bfloat16)
    else:
        extra = row_columns(-shift, 1.0)
    return jnp.concatenate([*pieces(scaled), extra], axis=1)


def row_columns(row_value, first):
    count = row_value.shape[1]
    high, mid, low = [piece.astype(jnp.float32) for piece in pieces(row_value)]
    place = lax.broadcasted_iota(jnp.int32, (HD, count), 0)
    if first is None:
        held = jnp.where(place == 0, high, jnp.where(place == 1, mid, jnp.where(place == 2, low, 0.0)))
    else:
        held = jnp.where(place == 1, high, jnp.where(place == 2, mid, jnp.where(place == 3, low, 0.0)))
        held = jnp.where(place == 0, first, held)
    return held.T.astype(jnp.bfloat16)


def attend_kernel(length_ref, proj_ref, out_ref, wide_ref, lse_ref, q_ref, k_ref, v_ref, s_ref):
    slot = proj_ref.shape[1]
    heads = proj_ref.shape[2] // HD
    length = length_ref[0]
    for head in range(heads):
        span = slice(head * HD, (head + 1) * HD)
        k_ref[head] = key_columns(proj_ref[1, :, span], length)
        q_ref[head] = query_columns(proj_ref[0, :, span], None)
        turned = proj_ref[2, :, span].astype(jnp.float32).T.astype(jnp.bfloat16)
        place = lax.broadcasted_iota(jnp.int32, (16, slot), 0)
        ones = jnp.where(place == 0, 1.0, 0.0).astype(jnp.bfloat16)
        v_ref[head] = jnp.concatenate([turned, ones], axis=0)

    @pl.loop(0, slot // QUERY_ROWS)
    def _(block):
        start = pl.multiple_of(block * QUERY_ROWS, QUERY_ROWS)
        turned = []
        for head in range(heads):
            query = q_ref[head, pl.ds(start, QUERY_ROWS), :]
            peak = None
            for at in range(0, slot, KEY_ROWS):
                score = dot(k_ref[head, pl.ds(at, KEY_ROWS), :], query, NT)
                s_ref[pl.ds(at, KEY_ROWS), :] = score
                most = jnp.max(score.reshape(KEY_ROWS // 8, 8, QUERY_ROWS), axis=0)
                peak = most if peak is None else jnp.maximum(peak, most)
            peak = jnp.max(peak, axis=0, keepdims=True)
            total = None
            for at in range(0, slot, KEY_ROWS):
                soft = jnp.exp2(s_ref[pl.ds(at, KEY_ROWS), :] - peak).astype(jnp.bfloat16)
                part = dot(v_ref[head, :, pl.ds(at, KEY_ROWS)], soft, NN)
                total = part if total is None else total + part
            row_sum = total[HD : HD + 1]
            wide = total[:HD] / row_sum
            wide_ref[head, :, pl.ds(start, QUERY_ROWS)] = wide
            lse_ref[head, :, pl.ds(start, QUERY_ROWS)] = peak + jnp.log2(row_sum)
            turned.append(wide)
        joined = jnp.concatenate(turned, axis=0)
        out_ref[pl.ds(start, QUERY_ROWS), :] = joined.T.astype(jnp.bfloat16)


def attend_back_kernel(
    length_ref, proj_ref, grad_ref, wide_ref, lse_ref, out_ref, q_ref, k_ref, t_ref, v_ref, dk_ref, dv_ref
):
    slot = proj_ref.shape[1]
    heads = proj_ref.shape[2] // HD
    length = length_ref[0]
    key_turned = proj_ref[1].astype(jnp.float32).T.astype(jnp.bfloat16)
    for head in range(heads):
        span = slice(head * HD, (head + 1) * HD)
        k_ref[head] = key_columns(proj_ref[1, :, span], length)
        q_ref[head] = proj_ref[0, :, span]
        t_ref[head] = key_turned[span]
        lane = lax.broadcasted_iota(jnp.int32, (slot, HD), 1)
        ones = jnp.where(lane < 3, 1.0, 0.0).astype(jnp.bfloat16)
        v_ref[head] = jnp.concatenate([proj_ref[2, :, span], ones], axis=1)
    dk_ref[...] = jnp.zeros_like(dk_ref)
    dv_ref[...] = jnp.zeros_like(dv_ref)

    @pl.loop(0, slot // QUERY_ROWS)
    def _(block):
        start = pl.multiple_of(block * QUERY_ROWS, QUERY_ROWS)
        rows = pl.ds(start, QUERY_ROWS)
        turned = []
        grads = grad_ref[rows, :]
        grads_turned = grads.astype(jnp.float32).T
        for head in range(heads):
            span = slice(head * HD, (head + 1) * HD)
            query = q_ref[head, rows, :]
            grad = grads[:, span]
            delta = jnp.sum(grads_turned[span] * wide_ref[head, :, rows], axis=0, keepdims=True)
            query_wide = query_columns(query, lse_ref[head, :, rows])
            grad_wide = jnp.concatenate([grad, row_columns(-delta, None)], axis=1)
            total = None
            for at in range(0, slot, KEY_ROWS):
                keys = pl.ds(at, KEY_ROWS)
                soft = jnp.exp2(dot(k_ref[head, keys, :], query_wide, NT))
                soft_grad = dot(v_ref[head, keys, :], grad_wide, NT)
                soft_low = soft.astype(jnp.bfloat16)
                score_grad = (soft * soft_grad).astype(jnp.bfloat16)
                dv_ref[head, keys, :] += dot(soft_low, grad, NN)
                dk_ref[head, keys, :] += dot(score_grad, query, NN)
                part = dot(t_ref[head, :, keys], score_grad, NN)
                total = part if total is None else total + part
            turned.append(total * HD ** (-0.5))
        joined = jnp.concatenate(turned, axis=0)
        out_ref[0, rows, :] = joined.T.astype(jnp.bfloat16)

    for head in range(heads):
        span = slice(head * HD, (head + 1) * HD)
        out_ref[1, :, span] = (dk_ref[head] * HD ** (-0.5)).astype(jnp.bfloat16)
        out_ref[2, :, span] = dv_ref[head].astype(jnp.bfloat16)


VMEM = pltpu.VMEM
KERNEL_BYTES = 56 * 2**20


def attend(lengths, proj):
    _, slot, width = proj.shape
    heads = width // HD
    return pl.pallas_call(
        attend_kernel,
        out_shape=(
            jax.ShapeDtypeStruct((slot, width), jnp.bfloat16),
            jax.ShapeDtypeStruct((heads, HD, slot), jnp.float32),
            jax.ShapeDtypeStruct((heads, 1, slot), jnp.float32),
        ),
        in_specs=[pl.BlockSpec(memory_space=pltpu.SMEM), pl.BlockSpec(memory_space=VMEM)],
        out_specs=(pl.BlockSpec(memory_space=VMEM),) * 3,
        scratch_shapes=[
            VMEM((heads, slot, 4 * HD), jnp.bfloat16),
            VMEM((heads, slot, 4 * HD), jnp.bfloat16),
            VMEM((heads, HD + 16, slot), jnp.bfloat16),
            VMEM((slot, QUERY_ROWS), jnp.float32),
        ],
        compiler_params=pltpu.CompilerParams(vmem_limit_bytes=KERNEL_BYTES),
    )(lengths, proj)


def attend_back(lengths, proj, grad, wide, lse):
    _, slot, width = proj.shape
    heads = width // HD
    return pl.pallas_call(
        attend_back_kernel,
        out_shape=jax.ShapeDtypeStruct((3, slot, width), jnp.bfloat16),
        in_specs=[pl.BlockSpec(memory_space=pltpu.SMEM)] + [pl.BlockSpec(memory_space=VMEM)] * 4,
        out_specs=pl.BlockSpec(memory_space=VMEM),
        scratch_shapes=[
            VMEM((heads, slot, HD), jnp.bfloat16),
            VMEM((heads, slot, 4 * HD), jnp.bfloat16),
            VMEM((heads, HD, slot), jnp.bfloat16),
            VMEM((heads, slot, 2 * HD), jnp.bfloat16),
            VMEM((heads, slot, HD), jnp.float32),
            VMEM((heads, slot, HD), jnp.float32),
        ],
        compiler_params=pltpu.CompilerParams(vmem_limit_bytes=KERNEL_BYTES),
    )(lengths, proj, grad, wide, lse)


MESH = pl.DeviceIdType.MESH
TN = (((0,), (0,)), ((), ()))
GATE_AT, UP_AT, DOWN_AT, OUT_AT, ALL_AT = 0, 512, 1024, 1536, 1792


class Place:
    def __init__(self):
        self.w = lax.axis_index("wide")
        self.n = lax.axis_index("narrow")
        self.c = lax.rem(self.n, 2)
        self.x = lax.div(self.n, 2)
        self.levels = lax.axis_size("wide").bit_length() - 1
        self.bits = [lax.rem(lax.div(self.w, 2**k), 2) for k in range(self.levels)]
        self.spot = tuple(self.bits[::-1])
        self.core_n = self.n + 1 - 2 * self.c
        self.cross_n = self.n + 2 - 4 * self.x
        self.diag_n = 3 - self.n
        self.core = (self.w, self.core_n)
        self.cross = (self.w, self.cross_n)
        self.diag = (self.w, self.diag_n)

    def wide(self, k):
        return (self.w + 2**k * (1 - 2 * self.bits[k]), self.n)

    def known(self, k):
        return (slice(None),) * (self.levels - 1 - k) + self.spot[self.levels - 1 - k :]


def enter(devices):
    barrier = pltpu.get_barrier_semaphore()
    for device in devices:
        pl.semaphore_signal(barrier, inc=1, device_id=device, device_id_type=MESH)
    pl.semaphore_wait(barrier, len(devices))


class Links:
    def __init__(self, send, recv, local):
        self.send, self.recv, self.local = send, recv, local
        self.sent = self.copied = 0

    def remote(self, source, target, device):
        i = self.sent
        self.sent += 1
        return pltpu.make_async_remote_copy(
            src_ref=source,
            dst_ref=target,
            send_sem=self.send.at[i],
            recv_sem=self.recv.at[i],
            device_id=device,
            device_id_type=MESH,
        )

    def copy(self, source, target):
        i = self.copied
        self.copied += 1
        return pltpu.make_async_copy(source, target, self.local.at[i])


class Chain:
    def __init__(self, transfers):
        self.transfers = transfers
        self.at = 0

    def step(self):
        if self.at > 0:
            self.transfers[self.at - 1].wait()
        if self.at < len(self.transfers):
            self.transfers[self.at].start()
        self.at += 1

    def finish(self):
        while self.at <= len(self.transfers):
            self.step()


def norm_rows(rows):
    scale = lax.rsqrt(jnp.mean(rows * rows, axis=-1, keepdims=True) + norm_eps)
    return scale, rows * scale


def front_kernel(
    length_ref, tok, cot, qkv_ref, gateup_ref, down_ref, out_ref, gains_ref,
    p_out, turned_out, wide_out, lse_out, mixed_out, w_out, wo_out, wq_out, xs_out, ds_out, gain_out,
    rows_ref, norm_ref, wq_ref, gain_ref, shard_ref, proj_ref, q_ref, k_ref, v_ref, s_ref,
    wide_ref, lse_ref, mixed_ref, turned_ref, send, recv, local,
):
    me = Place()
    links = Links(send, recv, local)
    rows, width = tok.shape
    heads = qkv_ref.shape[2] // HD
    half = rows // 2
    top = me.levels - 1
    everyone = [me.core, me.cross] + [me.wide(k) for k in range(me.levels)]
    wide_count = lax.axis_size("wide")
    slice_rows = width // wide_count

    wq_ref[(slice(None), *me.spot)] = qkv_ref[...].astype(jnp.bfloat16)
    gain_ref[me.spot] = jnp.zeros((8, 128), jnp.float32)
    gain_ref[(*me.spot, slice(0, 2), slice(0, slice_rows))] = gains_ref[...]
    own_rows = links.copy(tok, rows_ref.at[me.n])
    own_rows.start()
    enter(everyone)

    cross_rows, core_rows, forward_rows = [], [], []
    for part in range(2):
        piece = pl.ds(part * half, half)
        cross_rows.append(links.remote(tok.at[piece], rows_ref.at[me.n, piece], me.cross))
        core_rows.append(links.remote(tok.at[piece], rows_ref.at[me.n, piece], me.core))
        forward_rows.append(
            links.remote(rows_ref.at[me.cross_n, piece], rows_ref.at[me.cross_n, piece], me.core)
        )
    for copy in cross_rows + core_rows:
        copy.start()
    gain_chain = Chain(
        [links.remote(gain_ref.at[me.known(k)], gain_ref.at[me.known(k)], me.wide(k)) for k in range(top, -1, -1)]
    )
    wq_chain = Chain(
        [
            links.remote(
                wq_ref.at[(slice(None), *me.known(k))], wq_ref.at[(slice(None), *me.known(k))], me.wide(k)
            )
            for k in range(top, -1, -1)
        ]
    )
    gain_chain.step()
    wq_chain.step()
    shard_ref[:, GATE_AT:UP_AT] = gateup_ref[0].astype(jnp.bfloat16)
    shard_ref[:, UP_AT:DOWN_AT] = gateup_ref[1].astype(jnp.bfloat16)
    shard_ref[:, DOWN_AT:OUT_AT] = down_ref[...].T.astype(jnp.bfloat16)
    pad = jnp.zeros((slice_rows, ALL_AT - OUT_AT - out_ref.shape[0]), jnp.float32)
    shard_ref[:, OUT_AT:ALL_AT] = jnp.concatenate([out_ref[...].T, pad], axis=1).astype(jnp.bfloat16)
    own_shard = links.copy(shard_ref, w_out.at[(me.x, *me.spot)])
    own_shard.start()
    to_core_cot = links.remote(cot, ds_out.at[0], me.core)
    to_core_tok = links.remote(tok, xs_out.at[0], me.core)
    to_core_cot.start()
    to_core_tok.start()
    own_cot = links.copy(cot, ds_out.at[1])
    own_tok = links.copy(tok, xs_out.at[1])
    own_cot.start()
    own_tok.start()

    def weight_chain(start, count, cross_first):
        lanes = (slice(None), pl.ds(start, count))
        steps = []
        for k in range(top, 0, -1):
            spot = w_out.at[(me.x, *me.known(k), *lanes)]
            source = shard_ref.at[lanes] if k == top else spot
            steps.append(links.remote(source, spot, me.wide(k)))
        if cross_first:
            spot = w_out.at[(me.x, *me.known(0), *lanes)]
            steps.append(links.remote(spot, spot, me.cross))
            spot = w_out.at[(slice(None), *me.known(0), *lanes)]
            steps.append(links.remote(spot, spot, me.wide(0)))
        else:
            spot = w_out.at[(me.x, *me.known(0), *lanes)]
            steps.append(links.remote(spot, spot, me.wide(0)))
            spot = w_out.at[(me.x, *(slice(None),) * me.levels, *lanes)]
            steps.append(links.remote(spot, spot, me.cross))
        return Chain(steps)

    chains = [
        weight_chain(OUT_AT, ALL_AT - OUT_AT, False),
        weight_chain(GATE_AT, UP_AT - GATE_AT, True),
        weight_chain(UP_AT, DOWN_AT - UP_AT, False),
        weight_chain(DOWN_AT, OUT_AT - DOWN_AT, True),
    ]
    out_lanes = (*(slice(None),) * (me.levels + 2), pl.ds(OUT_AT, ALL_AT - OUT_AT))
    to_core_out = links.remote(w_out.at[out_lanes], wo_out, me.core)

    for _ in range(top):
        gain_chain.step()
        wq_chain.step()
    own_shard.wait()
    for chain in chains:
        chain.step()
    gain_chain.finish()
    gain_row = jnp.zeros((8, width), jnp.float32)
    for w in range(wide_count):
        bits = tuple((w >> k) & 1 for k in range(top, -1, -1))
        lane = lax.broadcasted_iota(jnp.int32, (128, width), 0)
        column = lax.broadcasted_iota(jnp.int32, (128, width), 1)
        select = jnp.where((column == lane + w * slice_rows) & (lane < slice_rows), 1.0, 0.0)
        gain_row = gain_row + dot(gain_ref[bits].astype(jnp.bfloat16), select.astype(jnp.bfloat16), NN)
    gain_out[...] = gain_row
    gain_one = gain_row[0:1]

    def project(block):
        values = norm_rows(rows_ref[block].astype(jnp.float32))[1] * gain_one
        norm_ref[block] = values.astype(jnp.bfloat16)

    def project_more(block):
        start = pl.multiple_of(block * rows, rows)
        normed = norm_ref[block]
        turned_ref[:, pl.ds(start, rows)] = normed.T
        for s in range(3):
            weights = wq_ref[s].reshape(width, heads * HD)
            proj_ref[s, pl.ds(start, rows), :] = dot(normed, weights, NN).astype(jnp.bfloat16)

    own_rows.wait()
    project(me.n)
    for copy in core_rows:
        copy.wait()
    project(me.core_n)
    for part in range(2):
        cross_rows[part].wait()
        forward_rows[part].start()
    project(me.cross_n)
    for part in range(2):
        forward_rows[part].wait()
    project(me.diag_n)
    wq_chain.finish()
    out_wq = links.copy(wq_ref, wq_out)
    out_wq.start()

    @pl.loop(0, 4)
    def _(block):
        project_more(block)

    out_proj = links.copy(proj_ref, p_out)
    out_turned = links.copy(turned_ref, turned_out)
    out_proj.start()
    out_turned.start()

    length = length_ref[0]
    slot = 4 * rows
    for head in range(heads):
        span = slice(head * HD, (head + 1) * HD)
        k_ref[head] = key_columns(proj_ref[1, :, span], length)
        q_ref[head] = query_columns(proj_ref[0, :, span], None)
        turned = proj_ref[2, :, span].astype(jnp.float32).T.astype(jnp.bfloat16)
        place = lax.broadcasted_iota(jnp.int32, (16, slot), 0)
        ones = jnp.where(place == 0, 1.0, 0.0).astype(jnp.bfloat16)
        v_ref[head] = jnp.concatenate([turned, ones], axis=0)
    for chain in chains:
        chain.step()

    to_cross = [
        links.remote(mixed_ref.at[0], mixed_out.at[me.n, me.c], me.cross),
        links.remote(mixed_ref.at[1], mixed_out.at[me.n, 1 - me.c], me.cross),
    ]
    to_core = [
        links.remote(mixed_ref.at[2], mixed_out.at[me.n, 1 - me.c], me.core),
        links.remote(mixed_ref.at[3], mixed_out.at[me.n, me.c], me.core),
    ]
    own_mixed = [
        links.copy(mixed_ref.at[2], mixed_out.at[me.n, 1 - me.c]),
        links.copy(mixed_ref.at[3], mixed_out.at[me.n, me.c]),
    ]
    pass_on = links.remote(mixed_out.at[me.cross_n], mixed_out.at[me.cross_n], me.core)

    def attend_head(start, head):
        query = q_ref[head, pl.ds(start, rows), :]
        peak = None
        for at in range(0, slot, KEY_ROWS):
            score = dot(k_ref[head, pl.ds(at, KEY_ROWS), :], query, NT)
            s_ref[pl.ds(at, KEY_ROWS), :] = score
            most = jnp.max(score.reshape(KEY_ROWS // 8, 8, rows), axis=0)
            peak = most if peak is None else jnp.maximum(peak, most)
        peak = jnp.max(peak, axis=0, keepdims=True)
        total = None
        for at in range(0, slot, KEY_ROWS):
            soft = jnp.exp2(s_ref[pl.ds(at, KEY_ROWS), :] - peak).astype(jnp.bfloat16)
            part = dot(v_ref[head, :, pl.ds(at, KEY_ROWS)], soft, NN)
            total = part if total is None else total + part
        row_sum = total[HD : HD + 1]
        wide = total[:HD] / row_sum
        wide_ref[head, :, pl.ds(start, rows)] = wide
        lse_ref[head, :, pl.ds(start, rows)] = peak + jnp.log2(row_sum)
        return wide

    @pl.loop(0, 4)
    def _(turn):
        other = 1 - lax.div(turn, 2)
        flip = lax.rem(lax.rem(turn, 2) + lax.div(turn, 2), 2)
        block = 2 * (me.x + (1 - 2 * me.x) * other) + me.c + (1 - 2 * me.c) * flip
        start = pl.multiple_of(block * rows, rows)
        turned = [attend_head(start, head) for head in range(heads)]
        mixed_ref[turn] = jnp.concatenate(turned, axis=0).T.astype(jnp.bfloat16)

        @pl.when(turn == 0)
        def _():
            to_cross[0].start()
            for chain in chains:
                chain.step()

        @pl.when(turn == 1)
        def _():
            to_cross[1].start()

        @pl.when(turn == 2)
        def _():
            to_core[0].start()
            own_mixed[0].start()
            for chain in chains:
                chain.step()

        @pl.when(turn == 3)
        def _():
            to_core[1].start()
            own_mixed[1].start()

    out_wide = links.copy(wide_ref, wide_out)
    out_lse = links.copy(lse_ref, lse_out)
    out_wide.start()
    out_lse.start()
    for copy in to_cross:
        copy.wait()
    pass_on.start()
    chains[0].finish()
    to_core_out.start()
    for chain in chains[1:]:
        chain.finish()
    for copy in to_core + own_mixed + [pass_on, to_core_out, to_core_cot, to_core_tok, own_cot, own_tok]:
        copy.wait()
    for copy in [out_wq, out_proj, out_turned, out_wide, out_lse]:
        copy.wait()


def middle_kernel(
    mixed_ref, w_ref, wo_ref, xs_ref, ds_ref, gain_ref,
    layer_out, dx_out, do_out, dw_out,
    h_ref, dg_ref, du_ref, h2_ref, x1_ref, dh2_ref, mlp_ref, send_dh2, send_mlp, got_dh2, got_mlp,
    dxb_ref, do_ref, turn_ref, send, recv, local,
):
    me = Place()
    links = Links(send, recv, local)
    rows, width = layer_out.shape
    block_rows = 256
    hidden = UP_AT - GATE_AT
    head_width = mixed_ref.shape[3]
    gain_two = gain_ref[1:2, :]
    enter([me.core, me.cross, me.diag])

    to_core_dh2 = links.remote(send_dh2, got_dh2, me.core)
    to_core_mlp = links.remote(send_mlp, got_mlp, me.core)
    to_core_dx = links.remote(dxb_ref.at[1], dxb_ref.at[0], me.core)
    to_grads = [
        links.remote(do_ref.at[me.cross_n], do_out.at[me.n], me.cross),
        links.remote(do_ref.at[me.diag_n], do_out.at[me.n], me.diag),
        links.remote(do_ref.at[me.core_n], do_out.at[me.n], me.core),
    ]
    own_grad = links.copy(do_ref.at[me.n], do_out.at[me.n])

    def feed(own):
        side = me.c if own else 1 - me.c

        @pl.loop(0, rows // block_rows)
        def _(step):
            at = pl.ds(pl.multiple_of(step * block_rows, block_rows), block_rows)
            at_all = pl.ds(pl.multiple_of(own * rows + step * block_rows, block_rows), block_rows)
            attn = jnp.zeros((block_rows, width), jnp.float32)
            for x in range(2):
                attn += dot(mixed_ref[2 * x + me.c, side, at, :], w_ref[x, :, OUT_AT : OUT_AT + head_width], NT)
                attn += dot(mixed_ref[2 * x + 1 - me.c, side, at, :], wo_ref[x, :, :head_width], NT)
            x1 = xs_ref[own, at, :].astype(jnp.float32) + attn
            h2 = (norm_rows(x1)[1] * gain_two).astype(jnp.bfloat16)
            h2_ref[at_all, :] = h2
            dy = ds_ref[own, at, :]
            dh2 = jnp.zeros((block_rows, width), jnp.float32)
            mlp = jnp.zeros((block_rows, width), jnp.float32)
            for x in range(2):
                gate = dot(h2, w_ref[x, :, GATE_AT:UP_AT], NN)
                up = dot(h2, w_ref[x, :, UP_AT:DOWN_AT], NN)
                dh = dot(dy, w_ref[x, :, DOWN_AT:OUT_AT], NN)
                square = gate * gate
                turn = jnp.tanh(gate * (0.7978845608028654 + 0.035677408136300125 * square))
                share = 0.5 + 0.5 * turn
                gelu = gate * share
                slope = share + 0.5 * gate * (1.0 - turn * turn) * (
                    0.7978845608028654 + 0.10703222440890037 * square
                )
                h = (gelu * up).astype(jnp.bfloat16)
                dup = (dh * gelu).astype(jnp.bfloat16)
                dgate = (dh * up * slope).astype(jnp.bfloat16)
                h_ref[x, at_all, :] = h
                du_ref[x, at_all, :] = dup
                dg_ref[x, at_all, :] = dgate
                mlp += dot(h, w_ref[x, :, DOWN_AT:OUT_AT], NT)
                dh2 += dot(dgate, w_ref[x, :, GATE_AT:UP_AT], NT)
                dh2 += dot(dup, w_ref[x, :, UP_AT:DOWN_AT], NT)
            if own:
                x1_ref[at, :] = x1
                dh2_ref[at, :] = dh2
                mlp_ref[at, :] = mlp
            else:
                send_dh2[at, :] = dh2.astype(jnp.bfloat16)
                send_mlp[at, :] = mlp.astype(jnp.bfloat16)

    feed(0)
    to_core_dh2.start()
    to_core_mlp.start()
    feed(1)
    to_core_dh2.wait()
    to_core_mlp.wait()

    @pl.loop(0, rows // block_rows)
    def _(step):
        at = pl.ds(pl.multiple_of(step * block_rows, block_rows), block_rows)
        x1 = x1_ref[at, :]
        layer_out[at, :] = (x1 + mlp_ref[at, :] + got_mlp[at, :].astype(jnp.float32)).astype(jnp.bfloat16)
        dh2 = dh2_ref[at, :] + got_dh2[at, :].astype(jnp.float32)
        scale, n2 = norm_rows(x1)
        e2 = dh2 * gain_two
        dx = ds_ref[1, at, :].astype(jnp.float32) + scale * (e2 - n2 * jnp.mean(e2 * n2, axis=-1, keepdims=True))
        dx_out[at, :] = dx
        low = dx.astype(jnp.bfloat16)
        dxb_ref[1, at, :] = low
        for x in range(2):
            do_ref[2 * x + me.c, at, :] = dot(low, w_ref[x, :, OUT_AT : OUT_AT + head_width], NN).astype(
                jnp.bfloat16
            )
            do_ref[2 * x + 1 - me.c, at, :] = dot(low, wo_ref[x, :, :head_width], NN).astype(jnp.bfloat16)

    to_core_dx.start()
    for copy in to_grads:
        copy.start()
    own_grad.start()

    for own in range(2):
        turn_ref[:, own * rows : (own + 1) * rows] = h2_ref[own * rows : (own + 1) * rows, :].T

    def weight_grad(lanes, right):
        @pl.loop(0, width // 256)
        def _(step):
            at = pl.ds(pl.multiple_of(step * 256, 256), 256)
            left = turn_ref[at, :]
            for x in range(2):
                dw_out[x, at, lanes] = dot(left, right(x), NN).astype(jnp.bfloat16)

    weight_grad(slice(GATE_AT, UP_AT), lambda x: dg_ref[x])
    weight_grad(slice(UP_AT, DOWN_AT), lambda x: du_ref[x])
    for own in range(2):
        turn_ref[:, own * rows : (own + 1) * rows] = ds_ref[own].T
    weight_grad(slice(DOWN_AT, OUT_AT), lambda x: h_ref[x])
    to_core_dx.wait()
    for own in range(2):
        turn_ref[:, own * rows : (own + 1) * rows] = dxb_ref[own].T
    dw_out[:, :, OUT_AT:ALL_AT] = jnp.zeros((2, width, ALL_AT - OUT_AT), jnp.bfloat16)

    @pl.loop(0, width // 256)
    def _(step):
        at = pl.ds(pl.multiple_of(step * 256, 256), 256)
        for x in range(2):
            total = jnp.zeros((256, head_width), jnp.float32)
            for own in range(2):
                side = me.c if own else 1 - me.c
                left = turn_ref[at, own * rows : (own + 1) * rows]
                total += dot(left, mixed_ref[2 * x + me.c, side], NN)
            dw_out[x, at, OUT_AT : OUT_AT + head_width] = total.astype(jnp.bfloat16)

    for copy in to_grads + [own_grad]:
        copy.wait()


def back_kernel(
    length_ref, proj_ref, grad_ref, wide_ref, lse_ref, dw_ref, turned_hbm, wq_ref, tok_ref, dx_ref, gain_ref,
    gateup_ref, qkv_ref,
    dtok_out, red_out, redq_out, gsum_out,
    q_ref, k_ref, t_ref, v_ref, dk_ref, dv_ref, dp_ref, turned_ref,
    a1, a2, b1, b2, a3, b3, a4, b4, dq_ref, q1, q2, q3, pair_ref, got_ref, cross_ref, own_ref,
    gsend, gcore, gcross, send, recv, local,
):
    me = Place()
    links = Links(send, recv, local)
    slot = proj_ref.shape[1]
    heads = proj_ref.shape[2] // HD
    rows, width = tok_ref.shape
    length = length_ref[0]
    full = (slice(None),) * (me.levels - 1)
    y = me.bits[0]
    edge = ALL_AT // 2
    lane_a, lane_b = (slice(None), pl.ds(0, edge)), (slice(None), pl.ds(edge, edge))
    load_turned = links.copy(turned_hbm, turned_ref)
    load_turned.start()
    enter([me.core, me.cross] + [me.wide(k) for k in range(me.levels)])

    first_a = links.remote(dw_ref.at[(1 - me.x, *full, slice(None), *lane_a)], a1, me.cross)
    first_b = links.remote(dw_ref.at[(slice(None), *full, 1 - y, *lane_b)], b1, me.wide(0))
    second_a = links.remote(a1.at[(*full, 1 - y)], a2, me.wide(0))
    second_b = links.remote(b1.at[1 - me.x], b2, me.cross)
    first_a.start()
    first_b.start()

    def add(target, other):
        target[...] = (target[...].astype(jnp.float32) + other.astype(jnp.float32)).astype(jnp.bfloat16)

    def after_first():
        first_a.wait()
        first_b.wait()
        add(a1, dw_ref[(me.x, *full, slice(None), *lane_a)])
        add(b1, dw_ref[(slice(None), *full, y, *lane_b)])
        second_a.start()
        second_b.start()

    def after_second():
        second_a.wait()
        second_b.wait()
        add(a2, a1[(*full, y)])
        add(b2, b1[me.x])

    def left_index(k, bit):
        return (slice(None),) * (me.levels - 1 - k) + (bit,)

    for head in range(heads):
        span = slice(head * HD, (head + 1) * HD)
        k_ref[head] = key_columns(proj_ref[1, :, span], length)
        q_ref[head] = proj_ref[0, :, span]
        lane = lax.broadcasted_iota(jnp.int32, (slot, HD), 1)
        ones = jnp.where(lane < 3, 1.0, 0.0).astype(jnp.bfloat16)
        v_ref[head] = jnp.concatenate([proj_ref[2, :, span], ones], axis=1)
    key_turned = proj_ref[1].astype(jnp.float32).T.astype(jnp.bfloat16)
    for head in range(heads):
        t_ref[head] = key_turned[head * HD : (head + 1) * HD]
    dk_ref[...] = jnp.zeros_like(dk_ref)
    dv_ref[...] = jnp.zeros_like(dv_ref)

    @pl.loop(0, slot // QUERY_ROWS)
    def _(block):
        start = pl.multiple_of(block * QUERY_ROWS, QUERY_ROWS)
        at_rows = pl.ds(start, QUERY_ROWS)
        turned = []
        grads = grad_ref[at_rows, :]
        grads_turned = grads.astype(jnp.float32).T
        for head in range(heads):
            span = slice(head * HD, (head + 1) * HD)
            query = q_ref[head, at_rows, :]
            grad = grads[:, span]
            delta = jnp.sum(grads_turned[span] * wide_ref[head, :, at_rows], axis=0, keepdims=True)
            query_wide = query_columns(query, lse_ref[head, :, at_rows])
            grad_wide = jnp.concatenate([grad, row_columns(-delta, None)], axis=1)
            total = None
            for at in range(0, slot, KEY_ROWS):
                keys = pl.ds(at, KEY_ROWS)
                soft = jnp.exp2(dot(k_ref[head, keys, :], query_wide, NT))
                soft_grad = dot(v_ref[head, keys, :], grad_wide, NT)
                soft_low = soft.astype(jnp.bfloat16)
                score_grad = (soft * soft_grad).astype(jnp.bfloat16)
                dv_ref[head, keys, :] += dot(soft_low, grad, NN)
                dk_ref[head, keys, :] += dot(score_grad, query, NN)
                part = dot(t_ref[head, :, keys], score_grad, NN)
                total = part if total is None else total + part
            turned.append(total * HD ** (-0.5))
        dp_ref[0, at_rows, :] = jnp.concatenate(turned, axis=0).T.astype(jnp.bfloat16)

        @pl.when(block == 2)
        def _():
            after_first()

    for head in range(heads):
        span = slice(head * HD, (head + 1) * HD)
        dp_ref[1, :, span] = (dk_ref[head] * HD ** (-0.5)).astype(jnp.bfloat16)
        dp_ref[2, :, span] = dv_ref[head].astype(jnp.bfloat16)

    def input_grad(block):
        at = pl.ds(pl.multiple_of(block * rows, rows), rows)
        total = jnp.zeros((rows, width), jnp.float32)
        for s in range(3):
            total += dot(dp_ref[s, at, :], wq_ref[s], NT)
        return total

    to_core = [links.remote(pair_ref.at[i], got_ref.at[i], me.core) for i in range(2)]
    to_cross = links.remote(pair_ref.at[2], cross_ref, me.cross)
    pair_ref[0] = input_grad(me.diag_n).astype(jnp.bfloat16)
    to_core[0].start()
    kept = input_grad(me.cross_n)
    to_core[0].wait()
    pair_ref[2] = (kept + got_ref[0].astype(jnp.float32)).astype(jnp.bfloat16)
    to_cross.start()

    after_second()
    load_turned.wait()
    for s in range(3):
        grads = dot(turned_ref[...], dp_ref[s], NN).astype(jnp.bfloat16)
        dq_ref[s] = grads.reshape(dq_ref.shape[1:])
    q_first = links.remote(dq_ref.at[(slice(None), *left_index(0, 1 - y))], q1, me.wide(0))
    q_first.start()
    a_third = links.remote(a2.at[left_index(1, 1 - me.bits[1])], a3, me.wide(1))
    b_third = links.remote(b2.at[left_index(1, 1 - me.bits[1])], b3, me.wide(1))
    a_third.start()
    b_third.start()
    pair_ref[1] = input_grad(me.core_n).astype(jnp.bfloat16)
    to_core[1].start()
    own_ref[...] = input_grad(me.n)
    a_third.wait()
    b_third.wait()
    add(a3, a2[left_index(1, me.bits[1])])
    add(b3, b2[left_index(1, me.bits[1])])
    a_fourth = links.remote(a3.at[1 - me.bits[2]], a4, me.wide(2))
    b_fourth = links.remote(b3.at[1 - me.bits[2]], b4, me.wide(2))
    q_first.wait()
    add(q1, dq_ref[(slice(None), *left_index(0, y))])
    q_second = links.remote(q1.at[(slice(None), *left_index(1, 1 - me.bits[1]))], q2, me.wide(1))
    q_second.start()
    a_fourth.start()
    b_fourth.start()
    q_second.wait()
    add(q2, q1[(slice(None), *left_index(1, me.bits[1]))])
    q_third = links.remote(q2.at[(slice(None), 1 - me.bits[2])], q3, me.wide(2))
    q_third.start()

    to_core[1].wait()
    to_cross.wait()
    gain_one = gain_ref[0:1, :]
    block_rows = 256

    @pl.loop(0, rows // block_rows)
    def _(step):
        at = pl.ds(pl.multiple_of(step * block_rows, block_rows), block_rows)
        dh1 = own_ref[at, :] + got_ref[1, at, :].astype(jnp.float32) + cross_ref[at, :].astype(jnp.float32)
        scale, n1 = norm_rows(tok_ref[at, :].astype(jnp.float32))
        e1 = dh1 * gain_one
        dtok_out[at, :] = dx_ref[at, :] + scale * (e1 - n1 * jnp.mean(e1 * n1, axis=-1, keepdims=True))

    a_fourth.wait()
    b_fourth.wait()
    red_out[:, :edge] = a4[...].astype(jnp.float32) + a3[me.bits[2]].astype(jnp.float32)
    red_out[:, edge:] = b4[...].astype(jnp.float32) + b3[me.bits[2]].astype(jnp.float32)
    two = jnp.zeros((red_out.shape[0], 1), jnp.float32)
    for s in range(2):
        weight = gateup_ref[s].astype(jnp.bfloat16).astype(jnp.float32)
        two += jnp.sum(weight * red_out[:, s * UP_AT : (s + 1) * UP_AT], axis=-1, keepdims=True)
    q_third.wait()
    one = jnp.zeros((red_out.shape[0], 1), jnp.float32)
    for s in range(3):
        grad = q3[s].astype(jnp.float32) + q2[s, me.bits[2]].astype(jnp.float32)
        redq_out[s] = grad
        weight = qkv_ref[s].astype(jnp.bfloat16).astype(jnp.float32)
        one += jnp.sum(weight * grad, axis=-1, keepdims=True)
    lane = lax.broadcasted_iota(jnp.int32, gsend.shape[1:], 1)
    gsend[0] = jnp.where(lane == 0, one, jnp.where(lane == 1, two, 0.0))
    core_sum = links.remote(gsend.at[0], gcore, me.core)
    core_sum.start()
    core_sum.wait()
    gsend[1] = gsend[0] + gcore[...]
    cross_sum = links.remote(gsend.at[1], gcross, me.cross)
    cross_sum.start()
    cross_sum.wait()
    gsum_out[...] = gsend[1] + gcross[...]


def update_kernel(
    red_ref, redq_ref, gsum_ref,
    qkv_w, out_w, gateup_w, down_w, gains_w,
    qkv_m, qkv_s, out_m, out_s, gateup_m, gateup_s, down_m, down_s, gains_m, gains_s,
    *outs,
):
    def put(at, weight, mean, square, gradient, rate, decay):
        results = adam_update(weight[...], mean[...], square[...], gradient, rate, decay)
        for ref, value in zip(outs[3 * at : 3 * at + 3], results):
            ref[...] = value

    slice_rows = red_ref.shape[0]
    put(0, qkv_w, qkv_m, qkv_s, redq_ref[...], D ** (-0.5), decay_rate)
    heads_width = out_w.shape[0]
    put(1, out_w, out_m, out_s, red_ref[:, OUT_AT : OUT_AT + heads_width].T, OUT_FAN ** (-0.5), decay_rate)
    both = jnp.stack([red_ref[:, GATE_AT:UP_AT], red_ref[:, UP_AT:DOWN_AT]])
    put(2, gateup_w, gateup_m, gateup_s, both, D ** (-0.5), decay_rate)
    put(3, down_w, down_m, down_s, red_ref[:, DOWN_AT:OUT_AT].T, FF ** (-0.5), decay_rate)
    gain = gains_w[...].astype(jnp.bfloat16).astype(jnp.float32)
    gain_grad = gsum_ref[...].T[0:2, :slice_rows] / gain
    put(4, gains_w, gains_m, gains_s, gain_grad, gain_rate, 0.0)


ANY = pl.BlockSpec(memory_space=pl.ANY)
IN_VMEM = pl.BlockSpec(memory_space=pltpu.VMEM)
IN_SMEM = pl.BlockSpec(memory_space=pltpu.SMEM)


def sems(remote, local):
    return [pltpu.SemaphoreType.DMA((remote,)), pltpu.SemaphoreType.DMA((remote,)), pltpu.SemaphoreType.DMA((local,))]


def shards_fast(
    tokens, lengths, qkv_weight, out_weight, gateup_weight, down_weight, norm_gains,
    qkv_mean, qkv_square, out_mean, out_square, gateup_mean, gateup_square, down_mean, down_square,
    gains_mean, gains_square, cotangent,
):
    low, wide_type = jnp.bfloat16, jnp.float32
    shape = jax.ShapeDtypeStruct
    rows, width = tokens.shape
    slot = 4 * rows
    count = lax.axis_size("wide")
    levels = count.bit_length() - 1
    bits = (2,) * levels
    part = width // count
    heads = qkv_weight.shape[2] // HD
    head_width = heads * HD
    hidden = gateup_weight.shape[2]
    tail = ALL_AT - OUT_AT

    def params(group):
        return pltpu.CompilerParams(collective_id=group, has_side_effects=True, vmem_limit_bytes=KERNEL_BYTES)

    proj, turned, wide, lse, mixed, w_all, wo_all, wq_all, xs, ds, gain = pl.pallas_call(
        front_kernel,
        out_shape=(
            shape((3, slot, head_width), low),
            shape((width, slot), low),
            shape((heads, HD, slot), wide_type),
            shape((heads, 1, slot), wide_type),
            shape((4, 2, rows, head_width), low),
            shape((2, *bits, part, ALL_AT), low),
            shape((2, *bits, part, tail), low),
            shape((3, *bits, part, head_width), low),
            shape((2, rows, width), low),
            shape((2, rows, width), low),
            shape((8, width), wide_type),
        ),
        in_specs=[IN_SMEM, ANY, ANY] + [IN_VMEM] * 5,
        out_specs=(ANY,) * 10 + (IN_VMEM,),
        scratch_shapes=[
            VMEM((4, rows, width), low),
            VMEM((4, rows, width), low),
            VMEM((3, *bits, part, head_width), low),
            VMEM((*bits, 8, 128), wide_type),
            VMEM((part, ALL_AT), low),
            VMEM((3, slot, head_width), low),
            VMEM((heads, slot, 4 * HD), low),
            VMEM((heads, slot, 4 * HD), low),
            VMEM((heads, HD + 16, slot), low),
            VMEM((slot, rows), wide_type),
            VMEM((heads, HD, slot), wide_type),
            VMEM((heads, 1, slot), wide_type),
            VMEM((4, rows, head_width), low),
            VMEM((width, slot), low),
            *sems(14 + 2 * levels + 4 * (levels + 1), 16),
        ],
        compiler_params=params(1),
    )(lengths, tokens, cotangent, qkv_weight, gateup_weight, down_weight, out_weight, norm_gains)

    layer_out, dx, do, dw = pl.pallas_call(
        middle_kernel,
        out_shape=(
            shape((rows, width), low),
            shape((rows, width), wide_type),
            shape((4, rows, head_width), low),
            shape((2, width, ALL_AT), low),
        ),
        in_specs=[IN_VMEM] * 6,
        out_specs=(IN_VMEM, IN_VMEM, ANY, IN_VMEM),
        scratch_shapes=[
            VMEM((2, 2 * rows, hidden), low),
            VMEM((2, 2 * rows, hidden), low),
            VMEM((2, 2 * rows, hidden), low),
            VMEM((2 * rows, width), low),
            VMEM((rows, width), wide_type),
            VMEM((rows, width), wide_type),
            VMEM((rows, width), wide_type),
            VMEM((rows, width), low),
            VMEM((rows, width), low),
            VMEM((rows, width), low),
            VMEM((rows, width), low),
            VMEM((2, rows, width), low),
            VMEM((4, rows, head_width), low),
            VMEM((width, 2 * rows), low),
            *sems(8, 2),
        ],
        compiler_params=params(2),
    )(
        mixed,
        w_all.reshape(2, width, ALL_AT),
        wo_all.reshape(2, width, tail),
        xs,
        ds,
        gain,
    )

    edge = ALL_AT // 2
    dtok, red, redq, gsum = pl.pallas_call(
        back_kernel,
        out_shape=(
            shape((rows, width), wide_type),
            shape((part, ALL_AT), wide_type),
            shape((3, part, head_width), wide_type),
            shape((part, 128), wide_type),
        ),
        in_specs=[IN_SMEM] + [IN_VMEM] * 5 + [ANY] + [IN_VMEM] * 6,
        out_specs=(IN_VMEM,) * 4,
        scratch_shapes=[
            VMEM((heads, slot, HD), low),
            VMEM((heads, slot, 4 * HD), low),
            VMEM((heads, HD, slot), low),
            VMEM((heads, slot, 2 * HD), low),
            VMEM((heads, slot, HD), wide_type),
            VMEM((heads, slot, HD), wide_type),
            VMEM((3, slot, head_width), low),
            VMEM((width, slot), low),
            VMEM((*bits, part, edge), low),
            VMEM((*bits[1:], part, edge), low),
            VMEM((2, *bits[1:], part, edge), low),
            VMEM((*bits[1:], part, edge), low),
            VMEM((*bits[2:], part, edge), low),
            VMEM((*bits[2:], part, edge), low),
            VMEM((part, edge), low),
            VMEM((part, edge), low),
            VMEM((3, *bits, part, head_width), low),
            VMEM((3, *bits[1:], part, head_width), low),
            VMEM((3, *bits[2:], part, head_width), low),
            VMEM((3, part, head_width), low),
            VMEM((3, rows, width), low),
            VMEM((2, rows, width), low),
            VMEM((rows, width), low),
            VMEM((rows, width), wide_type),
            VMEM((2, part, 128), wide_type),
            VMEM((part, 128), wide_type),
            VMEM((part, 128), wide_type),
            *sems(20, 2),
        ],
        compiler_params=params(3),
    )(
        lengths,
        proj,
        do.reshape(slot, head_width),
        wide,
        lse,
        dw.reshape(2, *bits, part, ALL_AT),
        turned,
        wq_all.reshape(3, width, head_width),
        tokens,
        dx,
        gain,
        gateup_weight,
        qkv_weight,
    )

    weights = (qkv_weight, out_weight, gateup_weight, down_weight, norm_gains)
    moments = (
        qkv_mean, qkv_square, out_mean, out_square, gateup_mean, gateup_square, down_mean, down_square,
        gains_mean, gains_square,
    )
    updated = pl.pallas_call(
        update_kernel,
        out_shape=tuple(shape(w.shape, wide_type) for w in weights for _ in range(3)),
        in_specs=[IN_VMEM] * 18,
        out_specs=(IN_VMEM,) * 15,
        compiler_params=pltpu.CompilerParams(vmem_limit_bytes=KERNEL_BYTES),
    )(red, redq, gsum, *weights, *moments)
    return (layer_out, dtok, *updated)


def shards(
    tokens,
    lengths,
    qkv_weight,
    out_weight,
    gateup_weight,
    down_weight,
    norm_gains,
    qkv_mean,
    qkv_square,
    out_mean,
    out_square,
    gateup_mean,
    gateup_square,
    down_mean,
    down_square,
    gains_mean,
    gains_square,
    cotangent,
):
    lowered = (
        qkv_weight.astype(jnp.bfloat16),
        out_weight.astype(jnp.bfloat16),
        gateup_weight.astype(jnp.bfloat16),
        down_weight.astype(jnp.bfloat16),
        norm_gains.astype(jnp.bfloat16),
    )
    qkv_full, out_full, gateup_full, down_full, gains_full = (
        lax.all_gather(lowered[0], "wide", axis=1, tiled=True),
        lax.all_gather(lowered[1], "wide", axis=1, tiled=True),
        lax.all_gather(lowered[2], "wide", axis=1, tiled=True),
        lax.all_gather(lowered[3], "wide", axis=1, tiled=True),
        lax.all_gather(lowered[4], "wide", axis=1, tiled=True),
    )
    gain_values = gains_full.astype(jnp.float32)
    rows_full = lax.all_gather(tokens, "narrow", axis=0, tiled=True)
    rows_float = rows_full.astype(jnp.float32)
    normed_one = rms_scale(rows_float, gain_values[0]).astype(jnp.bfloat16)
    projected = jnp.einsum(
        "td,sde->ste", normed_one, qkv_full, preferred_element_type=jnp.float32
    ).astype(jnp.bfloat16)
    mixed, mixed_wide, row_lse = attend(lengths, projected)
    attn_partial = jnp.dot(mixed, out_full, preferred_element_type=jnp.float32)
    own_float = tokens.astype(jnp.float32)
    attn_own = lax.psum_scatter(attn_partial, "narrow", scatter_dimension=0, tiled=True)
    residual_own = own_float + attn_own
    residual_full = lax.all_gather(residual_own, "narrow", axis=0, tiled=True)
    normed_two = rms_scale(residual_full, gain_values[1]).astype(jnp.bfloat16)
    gateup = jnp.einsum("td,sdf->stf", normed_two, gateup_full, preferred_element_type=jnp.float32)
    hidden = gelu_product(gateup[0], gateup[1]).astype(jnp.bfloat16)
    mlp_own = lax.psum_scatter(
        jnp.dot(hidden, down_full, preferred_element_type=jnp.float32).astype(jnp.bfloat16),
        "narrow",
        scatter_dimension=0,
        tiled=True,
    ).astype(jnp.float32)
    layer_out = (residual_own + mlp_own).astype(jnp.bfloat16)
    grad_full = lax.all_gather(cotangent, "narrow", axis=0, tiled=True)
    down_grad = jnp.einsum("tf,td->fd", hidden, grad_full, preferred_element_type=jnp.float32)
    hidden_grad = jnp.einsum("td,fd->tf", grad_full, down_full, preferred_element_type=jnp.float32)
    primal_out, gelu_back = jax.vjp(gelu_product, gateup[0], gateup[1])
    gate_grad, up_grad = gelu_back(hidden_grad)
    gateup_rows = jnp.stack([gate_grad, up_grad]).astype(jnp.bfloat16)
    gateup_grad = jnp.einsum(
        "td,stf->sdf", normed_two, gateup_rows, preferred_element_type=jnp.float32
    )
    normed_two_part = jnp.einsum(
        "stf,sdf->td", gateup_rows, gateup_full, preferred_element_type=jnp.float32
    )
    normed_two_grad = lax.psum_scatter(
        normed_two_part.astype(jnp.bfloat16), "narrow", scatter_dimension=0, tiled=True
    ).astype(jnp.float32)
    primal_two, norm_two_back = jax.vjp(rms_scale, residual_own, gain_values[1])
    residual_part, gain_two_grad = norm_two_back(normed_two_grad)
    residual_grad = cotangent.astype(jnp.float32) + residual_part
    residual_low = lax.all_gather(residual_grad.astype(jnp.bfloat16), "narrow", axis=0, tiled=True)
    out_grad = jnp.einsum("te,td->ed", mixed, residual_low, preferred_element_type=jnp.float32)
    mixed_grad = jnp.einsum(
        "td,ed->te", residual_low, out_full, preferred_element_type=jnp.float32
    ).astype(jnp.bfloat16)
    qkv_rows = attend_back(lengths, projected, mixed_grad, mixed_wide, row_lse)
    qkv_grad = jnp.einsum("td,ste->sde", normed_one, qkv_rows, preferred_element_type=jnp.float32)
    normed_one_part = jnp.einsum(
        "ste,sde->td", qkv_rows, qkv_full, preferred_element_type=jnp.float32
    )
    normed_one_grad = lax.psum_scatter(
        normed_one_part.astype(jnp.bfloat16), "narrow", scatter_dimension=0, tiled=True
    ).astype(jnp.float32)
    primal_one, norm_one_back = jax.vjp(rms_scale, own_float, gain_values[0])
    tokens_part, gain_one_grad = norm_one_back(normed_one_grad)
    tokens_grad = residual_grad + tokens_part
    gains_grad = lax.psum(jnp.stack([gain_one_grad, gain_two_grad]), "narrow")
    reduced_qkv, reduced_out, reduced_gateup, reduced_down, reduced_gains = (
        lax.psum_scatter(qkv_grad, "wide", scatter_dimension=1, tiled=True),
        lax.psum_scatter(out_grad, "wide", scatter_dimension=1, tiled=True),
        lax.psum_scatter(gateup_grad, "wide", scatter_dimension=1, tiled=True),
        lax.psum_scatter(down_grad, "wide", scatter_dimension=1, tiled=True),
        lax.psum_scatter(gains_grad, "wide", scatter_dimension=1, tiled=True),
    )
    qkv_master, qkv_first, qkv_second = adam_update(
        qkv_weight, qkv_mean, qkv_square, reduced_qkv, D ** (-0.5), decay_rate
    )
    out_master, out_first, out_second = adam_update(
        out_weight, out_mean, out_square, reduced_out, OUT_FAN ** (-0.5), decay_rate
    )
    gateup_master, gateup_first, gateup_second = adam_update(
        gateup_weight, gateup_mean, gateup_square, reduced_gateup, D ** (-0.5), decay_rate
    )
    down_master, down_first, down_second = adam_update(
        down_weight, down_mean, down_square, reduced_down, FF ** (-0.5), decay_rate
    )
    gains_master, gains_first, gains_second = adam_update(
        norm_gains, gains_mean, gains_square, reduced_gains, gain_rate, 0.0
    )
    return (
        layer_out,
        tokens_grad,
        qkv_master,
        qkv_first,
        qkv_second,
        out_master,
        out_first,
        out_second,
        gateup_master,
        gateup_first,
        gateup_second,
        down_master,
        down_first,
        down_second,
        gains_master,
        gains_first,
        gains_second,
    )


def solution(mesh):
    part = D // mesh.shape["wide"]
    fits = mesh.shape["narrow"] == 4 and mesh.shape["wide"] == 8 and part % 16 == 0
    return jax.shard_map(
        shards_fast if fits else shards,
        mesh=mesh,
        in_specs=(
            P(("wide", "narrow"), None),
            P("wide"),
            P(None, "wide", "narrow"),
            P("narrow", "wide"),
            P(None, "wide", "narrow"),
            P("narrow", "wide"),
            P(None, "wide"),
            P(None, "wide", "narrow"),
            P(None, "wide", "narrow"),
            P("narrow", "wide"),
            P("narrow", "wide"),
            P(None, "wide", "narrow"),
            P(None, "wide", "narrow"),
            P("narrow", "wide"),
            P("narrow", "wide"),
            P(None, "wide"),
            P(None, "wide"),
            P(("wide", "narrow"), None),
        ),
        out_specs=(
            P(("wide", "narrow"), None),
            P(("wide", "narrow"), None),
            P(None, "wide", "narrow"),
            P(None, "wide", "narrow"),
            P(None, "wide", "narrow"),
            P("narrow", "wide"),
            P("narrow", "wide"),
            P("narrow", "wide"),
            P(None, "wide", "narrow"),
            P(None, "wide", "narrow"),
            P(None, "wide", "narrow"),
            P("narrow", "wide"),
            P("narrow", "wide"),
            P("narrow", "wide"),
            P(None, "wide"),
            P(None, "wide"),
            P(None, "wide"),
        ),
        check_vma=False,
    )
```

```python
import jax
import jax.numpy as jnp
from jax import lax
from jax.experimental import pallas as pl
from jax.experimental.pallas import tpu as pltpu
from jax.sharding import PartitionSpec as P

D = 768
HEADS = 12
HD = 64
FF = 2048
SLOT = 2048
STEP_COUNT = 5
OUT_FAN = 1


norm_eps = 1e-06
adam_eps = 1e-08
beta_first = 0.5
beta_second = 0.5
decay_rate = 0.01
gain_rate = 0.3
masked_score = -1e30


def rms_scale(rows, gain):
    return rows * lax.rsqrt(jnp.mean(rows * rows, axis=-1, keepdims=True) + norm_eps) * gain


def gelu_product(gate_part, up_part):
    return jax.nn.gelu(gate_part, approximate=True) * up_part


def adam_update(weight, mean_old, square_old, gradient, rate, decay):
    mean_new = beta_first * mean_old + (1.0 - beta_first) * gradient
    square_new = beta_second * square_old + (1.0 - beta_second) * gradient * gradient
    mean_hat = mean_new / (1.0 - beta_first**STEP_COUNT)
    square_hat = square_new / (1.0 - beta_second**STEP_COUNT)
    weight_new = weight - rate * (mean_hat / (jnp.sqrt(square_hat) + adam_eps) + decay * weight)
    return (weight_new, mean_new, square_new)


LOG2E = 1.4426950408889634
NN = (((1,), (0,)), ((), ()))
NT = (((1,), (1,)), ((), ()))
QUERY_ROWS = 512
KEY_ROWS = 512


def pieces(value):
    high = value.astype(jnp.bfloat16)
    rest = value - high.astype(jnp.float32)
    mid = rest.astype(jnp.bfloat16)
    low = (rest - mid.astype(jnp.float32)).astype(jnp.bfloat16)
    return high, mid, low


def dot(left, right, dims):
    return lax.dot_general(left, right, dims, preferred_element_type=jnp.float32)


def key_columns(key_rows, length):
    rows = key_rows.shape[0]
    lane = lax.broadcasted_iota(jnp.int32, (rows, HD), 1)
    row = lax.broadcasted_iota(jnp.int32, (rows, HD), 0)
    mask = jnp.where(row < length, 0.0, masked_score)
    extra = jnp.where(lane == 0, mask, jnp.where(lane < 4, 1.0, 0.0)).astype(jnp.bfloat16)
    return jnp.concatenate([key_rows, key_rows, key_rows, extra], axis=1)


def query_columns(query_rows, shift):
    scaled = query_rows.astype(jnp.float32) * (LOG2E * HD ** (-0.5))
    if shift is None:
        lane = lax.broadcasted_iota(jnp.int32, query_rows.shape, 1)
        extra = jnp.where(lane == 0, 1.0, 0.0).astype(jnp.bfloat16)
    else:
        extra = row_columns(-shift, 1.0)
    return jnp.concatenate([*pieces(scaled), extra], axis=1)


def row_columns(row_value, first):
    count = row_value.shape[1]
    high, mid, low = [piece.astype(jnp.float32) for piece in pieces(row_value)]
    place = lax.broadcasted_iota(jnp.int32, (HD, count), 0)
    if first is None:
        held = jnp.where(place == 0, high, jnp.where(place == 1, mid, jnp.where(place == 2, low, 0.0)))
    else:
        held = jnp.where(place == 1, high, jnp.where(place == 2, mid, jnp.where(place == 3, low, 0.0)))
        held = jnp.where(place == 0, first, held)
    return held.T.astype(jnp.bfloat16)


def attend_kernel(length_ref, proj_ref, out_ref, wide_ref, lse_ref, q_ref, k_ref, v_ref, s_ref):
    slot = proj_ref.shape[1]
    heads = proj_ref.shape[2] // HD
    length = length_ref[0]
    for head in range(heads):
        span = slice(head * HD, (head + 1) * HD)
        k_ref[head] = key_columns(proj_ref[1, :, span], length)
        q_ref[head] = query_columns(proj_ref[0, :, span], None)
        turned = proj_ref[2, :, span].astype(jnp.float32).T.astype(jnp.bfloat16)
        place = lax.broadcasted_iota(jnp.int32, (16, slot), 0)
        ones = jnp.where(place == 0, 1.0, 0.0).astype(jnp.bfloat16)
        v_ref[head] = jnp.concatenate([turned, ones], axis=0)

    @pl.loop(0, slot // QUERY_ROWS)
    def _(block):
        start = pl.multiple_of(block * QUERY_ROWS, QUERY_ROWS)
        turned = []
        for head in range(heads):
            query = q_ref[head, pl.ds(start, QUERY_ROWS), :]
            peak = None
            for at in range(0, slot, KEY_ROWS):
                score = dot(k_ref[head, pl.ds(at, KEY_ROWS), :], query, NT)
                s_ref[pl.ds(at, KEY_ROWS), :] = score
                most = jnp.max(score.reshape(KEY_ROWS // 8, 8, QUERY_ROWS), axis=0)
                peak = most if peak is None else jnp.maximum(peak, most)
            peak = jnp.max(peak, axis=0, keepdims=True)
            total = None
            for at in range(0, slot, KEY_ROWS):
                soft = jnp.exp2(s_ref[pl.ds(at, KEY_ROWS), :] - peak).astype(jnp.bfloat16)
                part = dot(v_ref[head, :, pl.ds(at, KEY_ROWS)], soft, NN)
                total = part if total is None else total + part
            row_sum = total[HD : HD + 1]
            wide = total[:HD] / row_sum
            wide_ref[head, :, pl.ds(start, QUERY_ROWS)] = wide
            lse_ref[head, :, pl.ds(start, QUERY_ROWS)] = peak + jnp.log2(row_sum)
            turned.append(wide)
        joined = jnp.concatenate(turned, axis=0)
        out_ref[pl.ds(start, QUERY_ROWS), :] = joined.T.astype(jnp.bfloat16)


def attend_back_kernel(
    length_ref, proj_ref, grad_ref, wide_ref, lse_ref, out_ref, q_ref, k_ref, t_ref, v_ref, dk_ref, dv_ref
):
    slot = proj_ref.shape[1]
    heads = proj_ref.shape[2] // HD
    length = length_ref[0]
    key_turned = proj_ref[1].astype(jnp.float32).T.astype(jnp.bfloat16)
    for head in range(heads):
        span = slice(head * HD, (head + 1) * HD)
        k_ref[head] = key_columns(proj_ref[1, :, span], length)
        q_ref[head] = proj_ref[0, :, span]
        t_ref[head] = key_turned[span]
        lane = lax.broadcasted_iota(jnp.int32, (slot, HD), 1)
        ones = jnp.where(lane < 3, 1.0, 0.0).astype(jnp.bfloat16)
        v_ref[head] = jnp.concatenate([proj_ref[2, :, span], ones], axis=1)
    dk_ref[...] = jnp.zeros_like(dk_ref)
    dv_ref[...] = jnp.zeros_like(dv_ref)

    @pl.loop(0, slot // QUERY_ROWS)
    def _(block):
        start = pl.multiple_of(block * QUERY_ROWS, QUERY_ROWS)
        rows = pl.ds(start, QUERY_ROWS)
        turned = []
        grads = grad_ref[rows, :]
        grads_turned = grads.astype(jnp.float32).T
        for head in range(heads):
            span = slice(head * HD, (head + 1) * HD)
            query = q_ref[head, rows, :]
            grad = grads[:, span]
            delta = jnp.sum(grads_turned[span] * wide_ref[head, :, rows], axis=0, keepdims=True)
            query_wide = query_columns(query, lse_ref[head, :, rows])
            grad_wide = jnp.concatenate([grad, row_columns(-delta, None)], axis=1)
            total = None
            for at in range(0, slot, KEY_ROWS):
                keys = pl.ds(at, KEY_ROWS)
                soft = jnp.exp2(dot(k_ref[head, keys, :], query_wide, NT))
                soft_grad = dot(v_ref[head, keys, :], grad_wide, NT)
                soft_low = soft.astype(jnp.bfloat16)
                score_grad = (soft * soft_grad).astype(jnp.bfloat16)
                dv_ref[head, keys, :] += dot(soft_low, grad, NN)
                dk_ref[head, keys, :] += dot(score_grad, query, NN)
                part = dot(t_ref[head, :, keys], score_grad, NN)
                total = part if total is None else total + part
            turned.append(total * HD ** (-0.5))
        joined = jnp.concatenate(turned, axis=0)
        out_ref[0, rows, :] = joined.T.astype(jnp.bfloat16)

    for head in range(heads):
        span = slice(head * HD, (head + 1) * HD)
        out_ref[1, :, span] = (dk_ref[head] * HD ** (-0.5)).astype(jnp.bfloat16)
        out_ref[2, :, span] = dv_ref[head].astype(jnp.bfloat16)


VMEM = pltpu.VMEM
KERNEL_BYTES = 62 * 2**20


def attend(lengths, proj):
    _, slot, width = proj.shape
    heads = width // HD
    return pl.pallas_call(
        attend_kernel,
        out_shape=(
            jax.ShapeDtypeStruct((slot, width), jnp.bfloat16),
            jax.ShapeDtypeStruct((heads, HD, slot), jnp.float32),
            jax.ShapeDtypeStruct((heads, 1, slot), jnp.float32),
        ),
        in_specs=[pl.BlockSpec(memory_space=pltpu.SMEM), pl.BlockSpec(memory_space=VMEM)],
        out_specs=(pl.BlockSpec(memory_space=VMEM),) * 3,
        scratch_shapes=[
            VMEM((heads, slot, 4 * HD), jnp.bfloat16),
            VMEM((heads, slot, 4 * HD), jnp.bfloat16),
            VMEM((heads, HD + 16, slot), jnp.bfloat16),
            VMEM((slot, QUERY_ROWS), jnp.float32),
        ],
        compiler_params=pltpu.CompilerParams(vmem_limit_bytes=KERNEL_BYTES),
    )(lengths, proj)


def attend_back(lengths, proj, grad, wide, lse):
    _, slot, width = proj.shape
    heads = width // HD
    return pl.pallas_call(
        attend_back_kernel,
        out_shape=jax.ShapeDtypeStruct((3, slot, width), jnp.bfloat16),
        in_specs=[pl.BlockSpec(memory_space=pltpu.SMEM)] + [pl.BlockSpec(memory_space=VMEM)] * 4,
        out_specs=pl.BlockSpec(memory_space=VMEM),
        scratch_shapes=[
            VMEM((heads, slot, HD), jnp.bfloat16),
            VMEM((heads, slot, 4 * HD), jnp.bfloat16),
            VMEM((heads, HD, slot), jnp.bfloat16),
            VMEM((heads, slot, 2 * HD), jnp.bfloat16),
            VMEM((heads, slot, HD), jnp.float32),
            VMEM((heads, slot, HD), jnp.float32),
        ],
        compiler_params=pltpu.CompilerParams(vmem_limit_bytes=KERNEL_BYTES),
    )(lengths, proj, grad, wide, lse)


MESH = pl.DeviceIdType.MESH
GATE_AT, UP_AT, DOWN_AT, OUT_AT, ALL_AT = 0, 512, 1024, 1536, 1792
AXES = ("x", "z1", "z0", "y")
SPANS = {
    "out": (OUT_AT, ALL_AT - OUT_AT),
    "gate": (GATE_AT, UP_AT - GATE_AT),
    "up": (UP_AT, DOWN_AT - UP_AT),
    "down": (DOWN_AT, OUT_AT - DOWN_AT),
}
GATHER = {
    "out": ("z1", "z0", "y", "x"),
    "gate": ("z1", "z0", "x", "y"),
    "up": ("z1", "x", "y", "z0"),
    "down": ("z1", "x", "y", "z0"),
}
REDUCE = {
    "down": ("y", "x", "z0", "z1"),
    "gate": ("z0", "y", "x", "z1"),
    "up": ("z0", "y", "x", "z1"),
    "out": ("y", "x", "z0", "z1"),
}
QUERY_GATHER = (("z1", "z0", "y"), ("z1", "y", "z0"))
QUERY_REDUCE = (("y", "z0", "z1"), ("z0", "y", "z1"))
FULL = slice(None)


class Place:
    def __init__(self):
        self.w = lax.axis_index("wide")
        self.n = lax.axis_index("narrow")
        self.c = lax.rem(self.n, 2)
        self.x = lax.div(self.n, 2)
        y, z0, z1 = [lax.rem(lax.div(self.w, 2**k), 2) for k in range(3)]
        self.spot = {"x": self.x, "z1": z1, "z0": z0, "y": y}
        self.core_n = self.n + 1 - 2 * self.c
        self.cross_n = self.n + 2 - 4 * self.x
        self.diag_n = 3 - self.n
        self.core = (self.w, self.core_n)
        self.cross = (self.w, self.cross_n)
        self.diag = (self.w, self.diag_n)
        self.to = {
            "x": self.cross,
            "y": (self.w + 1 - 2 * y, self.n),
            "z0": (self.w + 2 - 4 * z0, self.n),
            "z1": (self.w + 4 - 8 * z1, self.n),
        }


def enter(devices):
    barrier = pltpu.get_barrier_semaphore()
    for device in devices:
        pl.semaphore_signal(barrier, inc=1, device_id=device, device_id_type=MESH)
    pl.semaphore_wait(barrier, len(devices))


class Links:
    def __init__(self, send, recv):
        self.send, self.recv = send, recv
        self.sent = 0

    def remote(self, source, target, device):
        i = self.sent
        self.sent += 1
        return pltpu.make_async_remote_copy(
            src_ref=source,
            dst_ref=target,
            send_sem=self.send.at[i],
            recv_sem=self.recv.at[i],
            device_id=device,
            device_id_type=MESH,
        )


class Gather:
    def __init__(self, links, me, room, axes, order, lead=(), tail=()):
        self.transfers = []
        known = set()
        for axis in order:
            spot = room.at[(*lead, *(FULL if a in known else me.spot[a] for a in axes), *tail)]
            self.transfers.append(links.remote(spot, spot, me.to[axis]))
            known.add(axis)
        self.at = 0

    def step(self):
        if self.at > 0:
            self.transfers[self.at - 1].wait()
        if self.at < len(self.transfers):
            self.transfers[self.at].start()
        self.at += 1

    def finish(self):
        while self.at <= len(self.transfers):
            self.step()


class Reduce:
    def __init__(self, links, me, start, rooms, axes, order, lead=(), tail=()):
        self.values, self.stages = [start, *rooms], []
        axes = list(axes)
        for room, axis in zip(rooms, order):
            before = (FULL,) * axes.index(axis)
            after = ((FULL,) * (len(axes) - 1 - len(before)) + tail) if not self.stages else ()
            theirs = (*lead, *before, 1 - me.spot[axis], *after)
            mine = (*lead, *before, me.spot[axis], *after)
            source = self.values[len(self.stages)]
            self.stages.append((links.remote(source.at[theirs], room, me.to[axis]), mine))
            axes.remove(axis)
        self.at = 0

    def take(self):
        copy, mine = self.stages[self.at - 1]
        copy.wait()
        before, into = self.values[self.at - 1 : self.at + 1]
        return into[...].astype(jnp.float32) + before[mine].astype(jnp.float32)

    def step(self):
        if self.at > 0:
            into = self.values[self.at]
            into[...] = self.take().astype(into.dtype)
        self.stages[self.at][0].start()
        self.at += 1

    def close(self):
        while self.at < len(self.stages):
            self.step()
        return self.take()


def reduce_rooms(order, axes, lead, part, lanes):
    left, shapes = list(axes), []
    for axis in order:
        left.remove(axis)
        shapes.append((*lead, *(2,) * len(left), part, lanes))
    return shapes


def norm_rows(rows):
    scale = lax.rsqrt(jnp.mean(rows * rows, axis=-1, keepdims=True) + norm_eps)
    return scale, rows * scale


def layer_kernel(
    length_ref, tok_ref, cot_ref, qkv_ref, gateup_ref, down_ref, out_ref, gains_ref,
    layer_out, dtok_out, red_out, redq_out, gsum_out,
    rows_ref, wq_ref, gain_ref, w_ref, wo_ref, k_ref, q_ref, v_ref, wide_ref, lse_ref, turned_ref, mixed_ref,
    xs_ref, ds_ref, got_ref, dxb_ref, do_ref, cross_ref, gsend, ggot, *rest,
):
    *rooms, send, recv, local = rest
    me = Place()
    links = Links(send, recv)
    rows, width = tok_ref.shape
    heads = qkv_ref.shape[2] // HD
    head_width = heads * HD
    slot = 4 * rows
    half = rows // 2
    part = qkv_ref.shape[1]
    cut = part // 2
    wide_axes = AXES[1:]
    low = jnp.bfloat16
    length = length_ref[0]
    own_w = tuple(me.spot[a] for a in wide_axes)
    step_rows = 256

    def rows_of(block):
        return pl.ds(pl.multiple_of(block * rows, rows), rows)

    def weight(x, name, count=None):
        start, lanes = SPANS[name]
        lanes = lanes if count is None else count
        return w_ref[x, :, :, :, :, start : start + lanes].reshape(width, lanes)

    def other_out(x):
        return wo_ref[x, :, :, :, :, :head_width].reshape(width, head_width)

    wq_ref[(FULL, *own_w)] = qkv_ref[...].astype(low)
    gain_ref[own_w] = jnp.zeros((8, 128), jnp.float32)
    gain_ref[(*own_w, slice(0, 2), slice(0, part))] = gains_ref[...]
    own_rows = pltpu.make_async_copy(tok_ref, rows_ref.at[me.n], local.at[0])
    own_rows.start()
    enter([me.core, me.cross, me.diag, me.to["y"], me.to["z0"], me.to["z1"]])
    cross_rows, core_rows, forward_rows = [], [], []
    for i in range(2):
        piece = pl.ds(i * half, half)
        cross_rows.append(links.remote(tok_ref.at[piece], rows_ref.at[me.n, piece], me.cross))
        core_rows.append(links.remote(tok_ref.at[piece], rows_ref.at[me.n, piece], me.core))
        there = rows_ref.at[me.cross_n, piece]
        forward_rows.append(links.remote(there, there, me.core))
    cross_rows[0].start()
    core_rows[0].start()
    core_rows[1].start()
    gain_chain = Gather(links, me, gain_ref, wide_axes, ("z1", "z0", "y"))
    wq_chains = [
        Gather(links, me, wq_ref, wide_axes, order, (FULL,), (pl.ds(i * cut, cut),))
        for i, order in enumerate(QUERY_GATHER)
    ]
    gain_chain.step()
    for chain in wq_chains:
        chain.step()
    cross_rows[1].start()
    own = (me.x, *own_w, FULL)
    w_ref[(*own, slice(GATE_AT, UP_AT))] = gateup_ref[0].astype(low)
    w_ref[(*own, slice(UP_AT, DOWN_AT))] = gateup_ref[1].astype(low)
    w_ref[(*own, slice(DOWN_AT, OUT_AT))] = down_ref[...].astype(low)
    pad = jnp.zeros((part, ALL_AT - OUT_AT - head_width), jnp.float32)
    w_ref[(*own, slice(OUT_AT, ALL_AT))] = jnp.concatenate([out_ref[...].T, pad], axis=1).astype(low)
    chains = {
        name: Gather(links, me, w_ref, AXES, GATHER[name], (), (FULL, pl.ds(*SPANS[name]))) for name in GATHER
    }
    out_lanes = (FULL,) * 5 + (pl.ds(*SPANS["out"]),)
    to_core_out = links.remote(w_ref.at[out_lanes], wo_ref, me.core)
    to_core_cot = links.remote(cot_ref, ds_ref, me.core)
    to_core_tok = links.remote(tok_ref, xs_ref, me.core)

    gain_chain.step()
    for chain in wq_chains:
        chain.step()
    for name in ("gate", "up"):
        chains[name].step()
    gain_chain.step()
    for chain in wq_chains:
        chain.step()
    for name in ("down", "out"):
        chains[name].step()
    gain_chain.finish()
    gain_row = jnp.zeros((8, width), jnp.float32)
    for w in range(8):
        lane = lax.broadcasted_iota(jnp.int32, (128, width), 0)
        column = lax.broadcasted_iota(jnp.int32, (128, width), 1)
        select = jnp.where((column == lane + w * part) & (lane < part), 1.0, 0.0)
        gain_row = gain_row + dot(gain_ref[w >> 2, (w >> 1) & 1, w & 1].astype(low), select.astype(low), NN)
    gain_one, gain_two = gain_row[0:1], gain_row[1:2]

    def normalize(block):
        values = norm_rows(rows_ref[block].astype(jnp.float32))[1] * gain_one
        normed = values.astype(low)
        rows_ref[block] = normed
        turned_ref[:, rows_of(block)] = normed.T

    own_rows.wait()
    normalize(me.n)
    for copy in core_rows:
        copy.wait()
    normalize(me.core_n)
    to_core_cot.start()
    to_core_tok.start()
    chains["gate"].step()
    for i in range(2):
        cross_rows[i].wait()
        forward_rows[i].start()
    for i in range(2):
        forward_rows[i].wait()
    chains["up"].step()
    chains["down"].step()
    chains["out"].step()
    chains["gate"].step()
    normalize(me.cross_n)
    normalize(me.diag_n)
    for chain in wq_chains:
        chain.finish()

    def attention(proj_ref, qa_ref, vt_ref, s_ref, own_mixed):
        @pl.loop(0, 4)
        def _(block):
            normed = rows_ref[block]
            for s in range(3):
                weights = wq_ref[s].reshape(width, head_width)
                proj_ref[s, rows_of(block), :] = dot(normed, weights, NN).astype(low)

        for head in range(heads):
            span = slice(head * HD, (head + 1) * HD)
            query = proj_ref[0, :, span]
            value = proj_ref[2, :, span]
            k_ref[head] = key_columns(proj_ref[1, :, span], length)
            q_ref[head] = query
            qa_ref[head] = query_columns(query, None)
            lane = lax.broadcasted_iota(jnp.int32, (slot, HD), 1)
            ones = jnp.where(lane < 3, 1.0, 0.0).astype(low)
            v_ref[head] = jnp.concatenate([value, ones], axis=1)
            place = lax.broadcasted_iota(jnp.int32, (16, slot), 0)
            ones = jnp.where(place == 0, 1.0, 0.0).astype(low)
            vt_ref[head] = jnp.concatenate([value.T, ones], axis=0)
        chains["up"].step()
        chains["out"].step()

        to_cross = [
            links.remote(own_mixed.at[0], mixed_ref.at[me.n, me.c], me.cross),
            links.remote(own_mixed.at[1], mixed_ref.at[me.n, 1 - me.c], me.cross),
        ]
        to_core = [
            links.remote(own_mixed.at[2], mixed_ref.at[me.n, 1 - me.c], me.core),
            links.remote(own_mixed.at[3], mixed_ref.at[me.n, me.c], me.core),
        ]
        arrived = mixed_ref.at[me.cross_n]
        pass_on = links.remote(arrived, arrived, me.core)

        def attend_head(at_rows, head):
            query = qa_ref[head, at_rows, :]
            peak = None
            for at in range(0, slot, KEY_ROWS):
                score = dot(k_ref[head, pl.ds(at, KEY_ROWS), :], query, NT)
                s_ref[pl.ds(at, KEY_ROWS), :] = score
                most = jnp.max(score.reshape(KEY_ROWS // 8, 8, rows), axis=0)
                peak = most if peak is None else jnp.maximum(peak, most)
            peak = jnp.max(peak, axis=0, keepdims=True)
            total = None
            for at in range(0, slot, KEY_ROWS):
                soft = jnp.exp2(s_ref[pl.ds(at, KEY_ROWS), :] - peak).astype(low)
                share = dot(vt_ref[head, :, pl.ds(at, KEY_ROWS)], soft, NN)
                total = share if total is None else total + share
            row_sum = total[HD : HD + 1]
            wide = total[:HD] / row_sum
            wide_ref[head, :, at_rows] = wide
            lse_ref[head, :, at_rows] = peak + jnp.log2(row_sum)
            return wide

        @pl.loop(0, 4)
        def _(turn):
            other = 1 - lax.div(turn, 2)
            flip = lax.rem(lax.rem(turn, 2) + lax.div(turn, 2), 2)
            block = 2 * (me.x + (1 - 2 * me.x) * other) + me.c + (1 - 2 * me.c) * flip
            wides = [attend_head(rows_of(block), head) for head in range(heads)]
            own_mixed[turn] = jnp.concatenate(wides, axis=0).T.astype(low)

            @pl.when(turn == 0)
            def _():
                to_cross[0].start()
                chains["down"].step()
                chains["out"].step()

            @pl.when(turn == 1)
            def _():
                to_cross[1].start()
                chains["gate"].step()
                chains["up"].step()

            @pl.when(turn == 2)
            def _():
                to_core[0].start()
                chains["down"].step()
                chains["out"].step()
                to_core_out.start()

            @pl.when(turn == 3)
            def _():
                to_core[1].start()

        mixed_ref[me.n, 1 - me.c] = own_mixed[2]
        mixed_ref[me.n, me.c] = own_mixed[3]
        for copy in to_cross:
            copy.wait()
        pass_on.start()
        for copy in to_core + [to_core_out, to_core_cot, to_core_tok, pass_on]:
            copy.wait()

    pl.run_scoped(
        attention,
        VMEM((3, slot, head_width), low),
        VMEM((heads, slot, 4 * HD), low),
        VMEM((heads, HD + 16, slot), low),
        VMEM((slot, rows), jnp.float32),
        VMEM((4, rows, head_width), low),
    )

    at_room = 0
    reduces = {}
    for name, order in REDUCE.items():
        reduces[name] = Reduce(
            links, me, w_ref, rooms[at_room : at_room + 4], AXES, order, (), (FULL, pl.ds(*SPANS[name]))
        )
        at_room += 4

    def middle(h_ref, dg_ref, du_ref, x1_ref, dh2_ref, mlp_ref, own_do, turn_ref):
        send_dh2, send_mlp = rows_ref.at[2], rows_ref.at[3]
        to_core_dh2 = links.remote(send_dh2, got_ref.at[0], me.core)
        to_core_mlp = links.remote(send_mlp, got_ref.at[1], me.core)
        to_core_dx = links.remote(dxb_ref.at[1], dxb_ref.at[0], me.core)
        to_grads = [
            links.remote(own_do.at[me.cross_n], do_ref.at[me.n], me.cross),
            links.remote(own_do.at[me.diag_n], do_ref.at[me.n], me.diag),
            links.remote(own_do.at[me.core_n], do_ref.at[me.n], me.core),
        ]

        @pl.loop(0, 4)
        def _(step):
            own = lax.div(step, 2)
            side = me.c + (1 - 2 * me.c) * (1 - own)
            at = pl.ds(pl.multiple_of(lax.rem(step, 2) * step_rows, step_rows), step_rows)
            attn = jnp.zeros((step_rows, width), jnp.float32)
            for x in range(2):
                attn += dot(mixed_ref[2 * x + me.c, side, at, :], weight(x, "out", head_width), NT)
                attn += dot(mixed_ref[2 * x + 1 - me.c, side, at, :], other_out(x), NT)

            @pl.when(own == 0)
            def _():
                x1 = xs_ref[at, :].astype(jnp.float32) + attn
                rows_ref[own, at, :] = (norm_rows(x1)[1] * gain_two).astype(low)

            @pl.when(own == 1)
            def _():
                x1 = tok_ref[at, :].astype(jnp.float32) + attn
                x1_ref[at, :] = x1
                rows_ref[own, at, :] = (norm_rows(x1)[1] * gain_two).astype(low)

        for name in ("gate", "up", "down"):
            chains[name].finish()

        def feed(own):
            @pl.loop(0, rows // step_rows)
            def _(step):
                at = pl.ds(pl.multiple_of(step * step_rows, step_rows), step_rows)
                at_all = pl.ds(pl.multiple_of(own * rows + step * step_rows, step_rows), step_rows)
                h2 = rows_ref[own, at, :]
                dy = (cot_ref if own else ds_ref)[at, :]
                dh2 = jnp.zeros((step_rows, width), jnp.float32)
                mlp = jnp.zeros((step_rows, width), jnp.float32)
                for x in range(2):
                    gate = dot(h2, weight(x, "gate"), NN)
                    up = dot(h2, weight(x, "up"), NN)
                    dh = dot(dy, weight(x, "down"), NN)
                    square = gate * gate
                    turn = jnp.tanh(gate * (0.7978845608028654 + 0.035677408136300125 * square))
                    share = 0.5 + 0.5 * turn
                    gelu = gate * share
                    slope = share + 0.5 * gate * (1.0 - turn * turn) * (
                        0.7978845608028654 + 0.10703222440890037 * square
                    )
                    h = (gelu * up).astype(low)
                    dup = (dh * gelu).astype(low)
                    dgate = (dh * up * slope).astype(low)
                    h_ref[x, at_all, :] = h
                    du_ref[x, at_all, :] = dup
                    dg_ref[x, at_all, :] = dgate
                    mlp += dot(h, weight(x, "down"), NT)
                    dh2 += dot(dgate, weight(x, "gate"), NT)
                    dh2 += dot(dup, weight(x, "up"), NT)
                if own:
                    dh2_ref[at, :] = dh2
                    mlp_ref[at, :] = mlp
                else:
                    send_dh2[at, :] = dh2.astype(low)
                    send_mlp[at, :] = mlp.astype(low)

        feed(0)
        to_core_dh2.start()
        to_core_mlp.start()
        feed(1)

        def weight_grad(name, right):
            start, lanes = SPANS[name]

            @pl.loop(0, 4)
            def _(step):
                tile = 2 * part
                left = turn_ref[pl.ds(pl.multiple_of(step * tile, tile), tile), :]
                for x in range(2):
                    value = dot(left, right(x), NN).astype(low).reshape(2, part, lanes)
                    w_ref[x, lax.div(step, 2), lax.rem(step, 2), :, :, start : start + lanes] = value

        turn_ref[:, :rows] = ds_ref[...].T
        turn_ref[:, rows:] = cot_ref[...].T
        weight_grad("down", lambda x: h_ref[x])
        reduces["down"].step()
        to_core_dh2.wait()
        to_core_mlp.wait()
        gsend[0] = jnp.zeros_like(gsend[0])

        @pl.loop(0, rows // step_rows)
        def _(step):
            at = pl.ds(pl.multiple_of(step * step_rows, step_rows), step_rows)
            x1 = x1_ref[at, :]
            layer_out[at, :] = (x1 + mlp_ref[at, :] + got_ref[1, at, :].astype(jnp.float32)).astype(low)
            dh2 = dh2_ref[at, :] + got_ref[0, at, :].astype(jnp.float32)
            scale, n2 = norm_rows(x1)
            gsend[0, 1:2, :] += jnp.sum(dh2 * n2, axis=0, keepdims=True)
            e2 = dh2 * gain_two
            dx = cot_ref[at, :].astype(jnp.float32) + scale * (
                e2 - n2 * jnp.mean(e2 * n2, axis=-1, keepdims=True)
            )
            dtok_out[at, :] = dx
            dx_low = dx.astype(low)
            dxb_ref[1, at, :] = dx_low
            for x in range(2):
                own_do[2 * x + me.c, at, :] = dot(dx_low, weight(x, "out", head_width), NN).astype(low)
                own_do[2 * x + 1 - me.c, at, :] = dot(dx_low, other_out(x), NN).astype(low)

        for copy in to_grads:
            copy.start()
        to_core_dx.start()
        do_ref[me.n] = own_do[me.n]
        for i in range(2):
            turn_ref[:, i * rows : (i + 1) * rows] = rows_ref[i].T
        weight_grad("gate", lambda x: dg_ref[x])
        reduces["gate"].step()
        weight_grad("up", lambda x: du_ref[x])
        to_core_dx.wait()
        for i in range(2):
            turn_ref[:, i * rows : (i + 1) * rows] = dxb_ref[i].T

        @pl.loop(0, 4)
        def _(step):
            tile = 2 * part
            at = pl.ds(pl.multiple_of(step * tile, tile), tile)
            for x in range(2):
                value = dot(turn_ref[at, :rows], mixed_ref[2 * x + me.c, 1 - me.c], NN)
                value += dot(turn_ref[at, rows:], mixed_ref[2 * x + me.c, me.c], NN)
                value = value.astype(low).reshape(2, part, head_width)
                w_ref[x, lax.div(step, 2), lax.rem(step, 2), :, :, OUT_AT : OUT_AT + head_width] = value

        reduces["out"].step()
        for copy in to_grads:
            copy.wait()

    hidden = UP_AT - GATE_AT
    pl.run_scoped(
        middle,
        VMEM((2, 2 * rows, hidden), low),
        VMEM((2, 2 * rows, hidden), low),
        VMEM((2, 2 * rows, hidden), low),
        VMEM((rows, width), jnp.float32),
        VMEM((rows, width), jnp.float32),
        VMEM((rows, width), jnp.float32),
        VMEM((4, rows, head_width), low),
        VMEM((width, 2 * rows), low),
    )

    def back(t_ref, qw_ref, gw_ref, dkv_ref, dp_ref, dq_ref):
        pair_ref = rows_ref
        for head in range(heads):
            t_ref[head] = k_ref[head, :, :HD].T
        dkv_ref[...] = jnp.zeros_like(dkv_ref)
        far = [me.cross_n, me.diag_n]
        near = [me.core_n, me.n]

        def prepare(block):
            at_rows = rows_of(block)
            grads = do_ref[block]
            grads_turned = grads.astype(jnp.float32).T
            for head in range(heads):
                span = slice(head * HD, (head + 1) * HD)
                delta = jnp.sum(grads_turned[span] * wide_ref[head, :, at_rows], axis=0, keepdims=True)
                qw_ref[head, at_rows, :] = query_columns(q_ref[head, at_rows, :], lse_ref[head, :, at_rows])
                gw_ref[head, at_rows, :] = jnp.concatenate([grads[:, span], row_columns(-delta, None)], axis=1)

        def attend_back_rows(at_rows, blocks):
            totals = []
            for head in range(heads):
                query_wide = qw_ref[head, at_rows, :]
                grad_wide = gw_ref[head, at_rows, :]
                query = q_ref[head, at_rows, :]
                grad = grad_wide[:, :HD]
                blank = jnp.zeros_like(query)
                right = jnp.concatenate(
                    [jnp.concatenate([query, blank], axis=1), jnp.concatenate([blank, grad], axis=1)], axis=0
                )
                total = None
                for block in blocks:
                    keys = rows_of(block)
                    soft = jnp.exp2(dot(k_ref[head, keys, :], query_wide, NT))
                    soft_grad = dot(v_ref[head, keys, :], grad_wide, NT)
                    score_grad = (soft * soft_grad).astype(low)
                    left = jnp.concatenate([score_grad, soft.astype(low)], axis=1)
                    dkv_ref[head, keys, :] += dot(left, right, NN)
                    share = dot(t_ref[head, :, keys], score_grad, NN)
                    total = share if total is None else total + share
                totals.append(total)
            return jnp.concatenate(totals, axis=0)

        def pick(pair, step):
            return pair[0] + (pair[1] - pair[0]) * step

        def close_keys(blocks):
            for block in blocks:
                at = rows_of(block)
                for head in range(heads):
                    span = slice(head * HD, (head + 1) * HD)
                    dkv = dkv_ref[head, at, :]
                    dp_ref[1, at, span] = (dkv[:, :HD] * HD ** (-0.5)).astype(low)
                    dp_ref[2, at, span] = dkv[:, HD:].astype(low)

        def input_grad(block):
            at = rows_of(block)
            total = jnp.zeros((rows, width), jnp.float32)
            for s in range(3):
                total += dot(dp_ref[s, at, :], wq_ref[s].reshape(width, head_width), NT)
            return total

        @pl.loop(0, 2)
        def _(step):
            block = pick(far, step)
            prepare(block)
            total = attend_back_rows(rows_of(block), far + near) * HD ** (-0.5)
            dp_ref[0, rows_of(block), :] = total.T.astype(low)

            @pl.when(step == 0)
            def _():
                reduces["down"].step()
                reduces["up"].step()

        reduces["gate"].step()

        @pl.loop(0, 2)
        def _(step):
            block = pick(near, step)
            prepare(block)
            total = attend_back_rows(rows_of(block), far)
            wide_ref[:, :, rows_of(block)] = total.reshape(heads, HD, rows)

            @pl.when(step == 0)
            def _():
                reduces["down"].step()
                reduces["out"].step()

        reduces["gate"].step()
        reduces["up"].step()
        to_core = [links.remote(pair_ref.at[i], got_ref.at[i], me.core) for i in range(2)]
        to_cross = links.remote(pair_ref.at[2], cross_ref, me.cross)
        close_keys(far)
        pair_ref[0] = input_grad(me.diag_n).astype(low)
        to_core[0].start()
        kept = input_grad(me.cross_n)
        to_core[0].wait()
        pair_ref[2] = (kept + got_ref[0].astype(jnp.float32)).astype(low)
        to_cross.start()

        @pl.loop(0, 2)
        def _(step):
            at = rows_of(pick(near, step))
            total = wide_ref[:, :, at].reshape(head_width, rows) + attend_back_rows(at, near)
            total = total * HD ** (-0.5)
            dp_ref[0, at, :] = total.T.astype(low)

            @pl.when(step == 0)
            def _():
                reduces["down"].step()
                reduces["out"].step()

        close_keys(near)
        gain_sum = jnp.zeros((width, 1), jnp.float32)
        for s in range(3):
            total = dot(turned_ref[...], dp_ref[s], NN)
            weights = wq_ref[s].reshape(width, head_width).astype(jnp.float32)
            gain_sum += jnp.sum(total * weights, axis=-1, keepdims=True)
            dq_ref[s] = total.astype(low).reshape(dq_ref.shape[1:])
        sums = []
        for i, order in enumerate(QUERY_REDUCE):
            at = at_room + 3 * i
            tail = (pl.ds(i * cut, cut),)
            sums.append(Reduce(links, me, dq_ref, rooms[at : at + 3], wide_axes, order, (FULL,), tail))
        for item in sums:
            item.step()
        gain_place = lax.broadcasted_iota(jnp.int32, (width, 128), 1)
        gsend[0] = gsend[0] + jnp.where(gain_place == 0, gain_sum, 0.0).T[0:8]
        hops = [me.core, me.cross, me.to["y"], me.to["z0"], me.to["z1"]]
        gains = [links.remote(gsend.at[i], ggot.at[i], device) for i, device in enumerate(hops)]

        def gain_step(i):
            gains[i].wait()
            gsend[i + 1] = gsend[i] + ggot[i]
            if i + 1 < len(gains):
                gains[i + 1].start()

        gains[0].start()
        pair_ref[1] = input_grad(me.core_n).astype(low)
        to_core[1].start()
        gain_step(0)
        pair_ref[3] = input_grad(me.n).astype(low)
        gain_step(1)
        for item in sums:
            item.step()
        reduces["gate"].step()
        reduces["up"].step()
        gain_step(2)
        to_core[1].wait()
        to_cross.wait()

        @pl.loop(0, rows // step_rows)
        def _(step):
            at = pl.ds(pl.multiple_of(step * step_rows, step_rows), step_rows)
            dh1 = pair_ref[3, at, :].astype(jnp.float32) + got_ref[1, at, :].astype(jnp.float32)
            dh1 += cross_ref[at, :].astype(jnp.float32)
            scale, n1 = norm_rows(tok_ref[at, :].astype(jnp.float32))
            e1 = dh1 * gain_one
            dtok_out[at, :] += scale * (e1 - n1 * jnp.mean(e1 * n1, axis=-1, keepdims=True))

        for item in sums:
            item.step()
        gain_step(3)
        for name in ("down", "out", "gate", "up"):
            start, lanes = SPANS[name]
            red_out[:, start : start + lanes] = reduces[name].close()
        gain_step(4)
        redq_out[:, :cut] = sums[0].close()
        redq_out[:, cut:] = sums[1].close()
        own_lane = lax.broadcasted_iota(jnp.int32, (width, 128), 0) == gain_place + me.w * part
        select = jnp.where(own_lane & (gain_place < part), 1.0, 0.0).astype(low)
        held = jnp.zeros((8, 128), jnp.float32)
        for piece in pieces(gsend[len(gains)]):
            held += dot(piece, select, NN)
        gsum_out[...] = held

    pl.run_scoped(
        back,
        VMEM((heads, HD, slot), low),
        VMEM((heads, slot, 4 * HD), low),
        VMEM((heads, slot, 2 * HD), low),
        VMEM((heads, slot, 2 * HD), jnp.float32),
        VMEM((3, slot, head_width), low),
        VMEM((3, 2, 2, 2, part, head_width), low),
    )


def update_kernel(
    red_ref, redq_ref, gsum_ref,
    qkv_w, out_w, gateup_w, down_w, gains_w,
    qkv_m, qkv_s, out_m, out_s, gateup_m, gateup_s, down_m, down_s, gains_m, gains_s,
    *outs,
):
    def put(at, weight, mean, square, gradient, rate, decay):
        results = adam_update(weight[...], mean[...], square[...], gradient, rate, decay)
        for ref, value in zip(outs[3 * at : 3 * at + 3], results):
            ref[...] = value

    slice_rows = red_ref.shape[0]
    put(0, qkv_w, qkv_m, qkv_s, redq_ref[...], D ** (-0.5), decay_rate)
    heads_width = out_w.shape[0]
    put(1, out_w, out_m, out_s, red_ref[:, OUT_AT : OUT_AT + heads_width].T, OUT_FAN ** (-0.5), decay_rate)
    both = jnp.stack([red_ref[:, GATE_AT:UP_AT], red_ref[:, UP_AT:DOWN_AT]])
    put(2, gateup_w, gateup_m, gateup_s, both, D ** (-0.5), decay_rate)
    put(3, down_w, down_m, down_s, red_ref[:, DOWN_AT:OUT_AT], FF ** (-0.5), decay_rate)
    gain = gains_w[...].astype(jnp.bfloat16).astype(jnp.float32)
    gain_grad = gsum_ref[0:2, :slice_rows]
    row = lax.broadcasted_iota(jnp.int32, gain.shape, 0)
    gain_grad = jnp.where(row == 0, gain_grad / gain, gain_grad)
    put(4, gains_w, gains_m, gains_s, gain_grad, gain_rate, 0.0)


IN_VMEM = pl.BlockSpec(memory_space=pltpu.VMEM)
IN_SMEM = pl.BlockSpec(memory_space=pltpu.SMEM)


def shards_fast(
    tokens, lengths, qkv_weight, out_weight, gateup_weight, down_weight, norm_gains,
    qkv_mean, qkv_square, out_mean, out_square, gateup_mean, gateup_square, down_mean, down_square,
    gains_mean, gains_square, cotangent,
):
    low, wide_type = jnp.bfloat16, jnp.float32
    shape = jax.ShapeDtypeStruct
    rows, width = tokens.shape
    slot = 4 * rows
    part = qkv_weight.shape[1]
    heads = qkv_weight.shape[2] // HD
    head_width = heads * HD
    tail = ALL_AT - OUT_AT
    wide_bits = (2, 2, 2)

    rooms = []
    for name, order in REDUCE.items():
        rooms += reduce_rooms(order, AXES, (), part, SPANS[name][1])
    for order in QUERY_REDUCE:
        rooms += reduce_rooms(order, AXES[1:], (3,), part // 2, head_width)
    layer_out, dtok, red, redq, gsum = pl.pallas_call(
        layer_kernel,
        out_shape=(
            shape((rows, width), low),
            shape((rows, width), wide_type),
            shape((part, ALL_AT), wide_type),
            shape((3, part, head_width), wide_type),
            shape((8, 128), wide_type),
        ),
        in_specs=[IN_SMEM] + [IN_VMEM] * 7,
        out_specs=(IN_VMEM,) * 5,
        scratch_shapes=[
            VMEM((4, rows, width), low),
            VMEM((3, *wide_bits, part, head_width), low),
            VMEM((*wide_bits, 8, 128), wide_type),
            VMEM((2, *wide_bits, part, ALL_AT), low),
            VMEM((2, *wide_bits, part, tail), low),
            VMEM((heads, slot, 4 * HD), low),
            VMEM((heads, slot, HD), low),
            VMEM((heads, slot, 2 * HD), low),
            VMEM((heads, HD, slot), wide_type),
            VMEM((heads, 1, slot), wide_type),
            VMEM((width, slot), low),
            VMEM((4, 2, rows, head_width), low),
            VMEM((rows, width), low),
            VMEM((rows, width), low),
            VMEM((2, rows, width), low),
            VMEM((2, rows, width), low),
            VMEM((4, rows, head_width), low),
            VMEM((rows, width), low),
            VMEM((6, 8, width), wide_type),
            VMEM((5, 8, width), wide_type),
            *[VMEM(room, low) for room in rooms],
            pltpu.SemaphoreType.DMA((96,)),
            pltpu.SemaphoreType.DMA((96,)),
            pltpu.SemaphoreType.DMA((1,)),
        ],
        compiler_params=pltpu.CompilerParams(
            collective_id=1, has_side_effects=True, vmem_limit_bytes=KERNEL_BYTES
        ),
    )(lengths, tokens, cotangent, qkv_weight, gateup_weight, down_weight.T, out_weight, norm_gains)

    weights = (qkv_weight, out_weight, gateup_weight, down_weight.T, norm_gains)
    moments = (
        qkv_mean, qkv_square, out_mean, out_square, gateup_mean, gateup_square, down_mean.T, down_square.T,
        gains_mean, gains_square,
    )
    updated = pl.pallas_call(
        update_kernel,
        out_shape=tuple(shape(w.shape, wide_type) for w in weights for _ in range(3)),
        in_specs=[IN_VMEM] * 18,
        out_specs=(IN_VMEM,) * 15,
        compiler_params=pltpu.CompilerParams(vmem_limit_bytes=KERNEL_BYTES),
    )(red, redq, gsum, *weights, *moments)
    down_updated = [value.T for value in updated[9:12]]
    return (layer_out, dtok, *updated[:9], *down_updated, *updated[12:])


def shards(
    tokens,
    lengths,
    qkv_weight,
    out_weight,
    gateup_weight,
    down_weight,
    norm_gains,
    qkv_mean,
    qkv_square,
    out_mean,
    out_square,
    gateup_mean,
    gateup_square,
    down_mean,
    down_square,
    gains_mean,
    gains_square,
    cotangent,
):
    lowered = (
        qkv_weight.astype(jnp.bfloat16),
        out_weight.astype(jnp.bfloat16),
        gateup_weight.astype(jnp.bfloat16),
        down_weight.astype(jnp.bfloat16),
        norm_gains.astype(jnp.bfloat16),
    )
    qkv_full, out_full, gateup_full, down_full, gains_full = (
        lax.all_gather(lowered[0], "wide", axis=1, tiled=True),
        lax.all_gather(lowered[1], "wide", axis=1, tiled=True),
        lax.all_gather(lowered[2], "wide", axis=1, tiled=True),
        lax.all_gather(lowered[3], "wide", axis=1, tiled=True),
        lax.all_gather(lowered[4], "wide", axis=1, tiled=True),
    )
    gain_values = gains_full.astype(jnp.float32)
    rows_full = lax.all_gather(tokens, "narrow", axis=0, tiled=True)
    rows_float = rows_full.astype(jnp.float32)
    normed_one = rms_scale(rows_float, gain_values[0]).astype(jnp.bfloat16)
    projected = jnp.einsum(
        "td,sde->ste", normed_one, qkv_full, preferred_element_type=jnp.float32
    ).astype(jnp.bfloat16)
    mixed, mixed_wide, row_lse = attend(lengths, projected)
    attn_partial = jnp.dot(mixed, out_full, preferred_element_type=jnp.float32)
    own_float = tokens.astype(jnp.float32)
    attn_own = lax.psum_scatter(attn_partial, "narrow", scatter_dimension=0, tiled=True)
    residual_own = own_float + attn_own
    residual_full = lax.all_gather(residual_own, "narrow", axis=0, tiled=True)
    normed_two = rms_scale(residual_full, gain_values[1]).astype(jnp.bfloat16)
    gateup = jnp.einsum("td,sdf->stf", normed_two, gateup_full, preferred_element_type=jnp.float32)
    hidden = gelu_product(gateup[0], gateup[1]).astype(jnp.bfloat16)
    mlp_own = lax.psum_scatter(
        jnp.dot(hidden, down_full, preferred_element_type=jnp.float32).astype(jnp.bfloat16),
        "narrow",
        scatter_dimension=0,
        tiled=True,
    ).astype(jnp.float32)
    layer_out = (residual_own + mlp_own).astype(jnp.bfloat16)
    grad_full = lax.all_gather(cotangent, "narrow", axis=0, tiled=True)
    down_grad = jnp.einsum("tf,td->fd", hidden, grad_full, preferred_element_type=jnp.float32)
    hidden_grad = jnp.einsum("td,fd->tf", grad_full, down_full, preferred_element_type=jnp.float32)
    primal_out, gelu_back = jax.vjp(gelu_product, gateup[0], gateup[1])
    gate_grad, up_grad = gelu_back(hidden_grad)
    gateup_rows = jnp.stack([gate_grad, up_grad]).astype(jnp.bfloat16)
    gateup_grad = jnp.einsum(
        "td,stf->sdf", normed_two, gateup_rows, preferred_element_type=jnp.float32
    )
    normed_two_part = jnp.einsum(
        "stf,sdf->td", gateup_rows, gateup_full, preferred_element_type=jnp.float32
    )
    normed_two_grad = lax.psum_scatter(
        normed_two_part.astype(jnp.bfloat16), "narrow", scatter_dimension=0, tiled=True
    ).astype(jnp.float32)
    primal_two, norm_two_back = jax.vjp(rms_scale, residual_own, gain_values[1])
    residual_part, gain_two_grad = norm_two_back(normed_two_grad)
    residual_grad = cotangent.astype(jnp.float32) + residual_part
    residual_low = lax.all_gather(residual_grad.astype(jnp.bfloat16), "narrow", axis=0, tiled=True)
    out_grad = jnp.einsum("te,td->ed", mixed, residual_low, preferred_element_type=jnp.float32)
    mixed_grad = jnp.einsum(
        "td,ed->te", residual_low, out_full, preferred_element_type=jnp.float32
    ).astype(jnp.bfloat16)
    qkv_rows = attend_back(lengths, projected, mixed_grad, mixed_wide, row_lse)
    qkv_grad = jnp.einsum("td,ste->sde", normed_one, qkv_rows, preferred_element_type=jnp.float32)
    normed_one_part = jnp.einsum(
        "ste,sde->td", qkv_rows, qkv_full, preferred_element_type=jnp.float32
    )
    normed_one_grad = lax.psum_scatter(
        normed_one_part.astype(jnp.bfloat16), "narrow", scatter_dimension=0, tiled=True
    ).astype(jnp.float32)
    primal_one, norm_one_back = jax.vjp(rms_scale, own_float, gain_values[0])
    tokens_part, gain_one_grad = norm_one_back(normed_one_grad)
    tokens_grad = residual_grad + tokens_part
    gains_grad = lax.psum(jnp.stack([gain_one_grad, gain_two_grad]), "narrow")
    reduced_qkv, reduced_out, reduced_gateup, reduced_down, reduced_gains = (
        lax.psum_scatter(qkv_grad, "wide", scatter_dimension=1, tiled=True),
        lax.psum_scatter(out_grad, "wide", scatter_dimension=1, tiled=True),
        lax.psum_scatter(gateup_grad, "wide", scatter_dimension=1, tiled=True),
        lax.psum_scatter(down_grad, "wide", scatter_dimension=1, tiled=True),
        lax.psum_scatter(gains_grad, "wide", scatter_dimension=1, tiled=True),
    )
    qkv_master, qkv_first, qkv_second = adam_update(
        qkv_weight, qkv_mean, qkv_square, reduced_qkv, D ** (-0.5), decay_rate
    )
    out_master, out_first, out_second = adam_update(
        out_weight, out_mean, out_square, reduced_out, OUT_FAN ** (-0.5), decay_rate
    )
    gateup_master, gateup_first, gateup_second = adam_update(
        gateup_weight, gateup_mean, gateup_square, reduced_gateup, D ** (-0.5), decay_rate
    )
    down_master, down_first, down_second = adam_update(
        down_weight, down_mean, down_square, reduced_down, FF ** (-0.5), decay_rate
    )
    gains_master, gains_first, gains_second = adam_update(
        norm_gains, gains_mean, gains_square, reduced_gains, gain_rate, 0.0
    )
    return (
        layer_out,
        tokens_grad,
        qkv_master,
        qkv_first,
        qkv_second,
        out_master,
        out_first,
        out_second,
        gateup_master,
        gateup_first,
        gateup_second,
        down_master,
        down_first,
        down_second,
        gains_master,
        gains_first,
        gains_second,
    )


def solution(mesh):
    part = D // mesh.shape["wide"]
    fits = mesh.shape["narrow"] == 4 and mesh.shape["wide"] == 8 and part % 32 == 0
    return jax.shard_map(
        shards_fast if fits else shards,
        mesh=mesh,
        in_specs=(
            P(("wide", "narrow"), None),
            P("wide"),
            P(None, "wide", "narrow"),
            P("narrow", "wide"),
            P(None, "wide", "narrow"),
            P("narrow", "wide"),
            P(None, "wide"),
            P(None, "wide", "narrow"),
            P(None, "wide", "narrow"),
            P("narrow", "wide"),
            P("narrow", "wide"),
            P(None, "wide", "narrow"),
            P(None, "wide", "narrow"),
            P("narrow", "wide"),
            P("narrow", "wide"),
            P(None, "wide"),
            P(None, "wide"),
            P(("wide", "narrow"), None),
        ),
        out_specs=(
            P(("wide", "narrow"), None),
            P(("wide", "narrow"), None),
            P(None, "wide", "narrow"),
            P(None, "wide", "narrow"),
            P(None, "wide", "narrow"),
            P("narrow", "wide"),
            P("narrow", "wide"),
            P("narrow", "wide"),
            P(None, "wide", "narrow"),
            P(None, "wide", "narrow"),
            P(None, "wide", "narrow"),
            P("narrow", "wide"),
            P("narrow", "wide"),
            P("narrow", "wide"),
            P(None, "wide"),
            P(None, "wide"),
            P(None, "wide"),
        ),
        check_vma=False,
    )
```

```python
import functools

import jax
import jax.numpy as jnp
from jax import lax
from jax.experimental import pallas as pl
from jax.experimental.pallas import tpu as pltpu
from jax.sharding import PartitionSpec as P

D = 768
HEADS = 12
HD = 64
FF = 2048
SLOT = 2048
STEP_COUNT = 5
OUT_FAN = 1


norm_eps = 1e-06
adam_eps = 1e-08
beta_first = 0.5
beta_second = 0.5
decay_rate = 0.01
gain_rate = 0.3
masked_score = -1e30


def rms_scale(rows, gain):
    return rows * lax.rsqrt(jnp.mean(rows * rows, axis=-1, keepdims=True) + norm_eps) * gain


def gelu_product(gate_part, up_part):
    return jax.nn.gelu(gate_part, approximate=True) * up_part


def adam_update(weight, mean_old, square_old, gradient, rate, decay):
    mean_new = beta_first * mean_old + (1.0 - beta_first) * gradient
    square_new = beta_second * square_old + (1.0 - beta_second) * gradient * gradient
    mean_hat = mean_new / (1.0 - beta_first**STEP_COUNT)
    square_hat = square_new / (1.0 - beta_second**STEP_COUNT)
    weight_new = weight - rate * (mean_hat / (jnp.sqrt(square_hat) + adam_eps) + decay * weight)
    return (weight_new, mean_new, square_new)


LOG2E = 1.4426950408889634
NN = (((1,), (0,)), ((), ()))
NT = (((1,), (1,)), ((), ()))
QUERY_ROWS = 512
KEY_ROWS = 512


def pieces(value):
    high = value.astype(jnp.bfloat16)
    rest = value - high.astype(jnp.float32)
    mid = rest.astype(jnp.bfloat16)
    low = (rest - mid.astype(jnp.float32)).astype(jnp.bfloat16)
    return high, mid, low


def dot(left, right, dims):
    return lax.dot_general(left, right, dims, preferred_element_type=jnp.float32)


def key_columns(key_rows, length):
    rows = key_rows.shape[0]
    lane = lax.broadcasted_iota(jnp.int32, (rows, HD), 1)
    row = lax.broadcasted_iota(jnp.int32, (rows, HD), 0)
    mask = jnp.where(row < length, 0.0, masked_score)
    extra = jnp.where(lane == 0, mask, jnp.where(lane < 4, 1.0, 0.0)).astype(jnp.bfloat16)
    return jnp.concatenate([key_rows, key_rows, key_rows, extra], axis=1)


def query_columns(query_rows, shift):
    scaled = query_rows.astype(jnp.float32) * (LOG2E * HD ** (-0.5))
    if shift is None:
        lane = lax.broadcasted_iota(jnp.int32, query_rows.shape, 1)
        extra = jnp.where(lane == 0, 1.0, 0.0).astype(jnp.bfloat16)
    else:
        extra = row_columns(-shift, 1.0)
    return jnp.concatenate([*pieces(scaled), extra], axis=1)


def row_columns(row_value, first):
    count = row_value.shape[1]
    high, mid, low = [piece.astype(jnp.float32) for piece in pieces(row_value)]
    place = lax.broadcasted_iota(jnp.int32, (HD, count), 0)
    if first is None:
        held = jnp.where(place == 0, high, jnp.where(place == 1, mid, jnp.where(place == 2, low, 0.0)))
    else:
        held = jnp.where(place == 1, high, jnp.where(place == 2, mid, jnp.where(place == 3, low, 0.0)))
        held = jnp.where(place == 0, first, held)
    return held.T.astype(jnp.bfloat16)


def attend_kernel(length_ref, proj_ref, out_ref, wide_ref, lse_ref, q_ref, k_ref, v_ref, s_ref):
    slot = proj_ref.shape[1]
    heads = proj_ref.shape[2] // HD
    length = length_ref[0]
    for head in range(heads):
        span = slice(head * HD, (head + 1) * HD)
        k_ref[head] = key_columns(proj_ref[1, :, span], length)
        q_ref[head] = query_columns(proj_ref[0, :, span], None)
        turned = proj_ref[2, :, span].astype(jnp.float32).T.astype(jnp.bfloat16)
        place = lax.broadcasted_iota(jnp.int32, (16, slot), 0)
        ones = jnp.where(place == 0, 1.0, 0.0).astype(jnp.bfloat16)
        v_ref[head] = jnp.concatenate([turned, ones], axis=0)

    @pl.loop(0, slot // QUERY_ROWS)
    def _(block):
        start = pl.multiple_of(block * QUERY_ROWS, QUERY_ROWS)
        turned = []
        for head in range(heads):
            query = q_ref[head, pl.ds(start, QUERY_ROWS), :]
            peak = None
            for at in range(0, slot, KEY_ROWS):
                score = dot(k_ref[head, pl.ds(at, KEY_ROWS), :], query, NT)
                s_ref[pl.ds(at, KEY_ROWS), :] = score
                most = jnp.max(score.reshape(KEY_ROWS // 8, 8, QUERY_ROWS), axis=0)
                peak = most if peak is None else jnp.maximum(peak, most)
            peak = jnp.max(peak, axis=0, keepdims=True)
            total = None
            for at in range(0, slot, KEY_ROWS):
                soft = jnp.exp2(s_ref[pl.ds(at, KEY_ROWS), :] - peak).astype(jnp.bfloat16)
                part = dot(v_ref[head, :, pl.ds(at, KEY_ROWS)], soft, NN)
                total = part if total is None else total + part
            row_sum = total[HD : HD + 1]
            wide = total[:HD] / row_sum
            wide_ref[head, :, pl.ds(start, QUERY_ROWS)] = wide
            lse_ref[head, :, pl.ds(start, QUERY_ROWS)] = peak + jnp.log2(row_sum)
            turned.append(wide)
        joined = jnp.concatenate(turned, axis=0)
        out_ref[pl.ds(start, QUERY_ROWS), :] = joined.T.astype(jnp.bfloat16)


def attend_back_kernel(
    length_ref, proj_ref, grad_ref, wide_ref, lse_ref, out_ref, q_ref, k_ref, t_ref, v_ref, dk_ref, dv_ref
):
    slot = proj_ref.shape[1]
    heads = proj_ref.shape[2] // HD
    length = length_ref[0]
    key_turned = proj_ref[1].astype(jnp.float32).T.astype(jnp.bfloat16)
    for head in range(heads):
        span = slice(head * HD, (head + 1) * HD)
        k_ref[head] = key_columns(proj_ref[1, :, span], length)
        q_ref[head] = proj_ref[0, :, span]
        t_ref[head] = key_turned[span]
        lane = lax.broadcasted_iota(jnp.int32, (slot, HD), 1)
        ones = jnp.where(lane < 3, 1.0, 0.0).astype(jnp.bfloat16)
        v_ref[head] = jnp.concatenate([proj_ref[2, :, span], ones], axis=1)
    dk_ref[...] = jnp.zeros_like(dk_ref)
    dv_ref[...] = jnp.zeros_like(dv_ref)

    @pl.loop(0, slot // QUERY_ROWS)
    def _(block):
        start = pl.multiple_of(block * QUERY_ROWS, QUERY_ROWS)
        rows = pl.ds(start, QUERY_ROWS)
        turned = []
        grads = grad_ref[rows, :]
        grads_turned = grads.astype(jnp.float32).T
        for head in range(heads):
            span = slice(head * HD, (head + 1) * HD)
            query = q_ref[head, rows, :]
            grad = grads[:, span]
            delta = jnp.sum(grads_turned[span] * wide_ref[head, :, rows], axis=0, keepdims=True)
            query_wide = query_columns(query, lse_ref[head, :, rows])
            grad_wide = jnp.concatenate([grad, row_columns(-delta, None)], axis=1)
            total = None
            for at in range(0, slot, KEY_ROWS):
                keys = pl.ds(at, KEY_ROWS)
                soft = jnp.exp2(dot(k_ref[head, keys, :], query_wide, NT))
                soft_grad = dot(v_ref[head, keys, :], grad_wide, NT)
                soft_low = soft.astype(jnp.bfloat16)
                score_grad = (soft * soft_grad).astype(jnp.bfloat16)
                dv_ref[head, keys, :] += dot(soft_low, grad, NN)
                dk_ref[head, keys, :] += dot(score_grad, query, NN)
                part = dot(t_ref[head, :, keys], score_grad, NN)
                total = part if total is None else total + part
            turned.append(total * HD ** (-0.5))
        joined = jnp.concatenate(turned, axis=0)
        out_ref[0, rows, :] = joined.T.astype(jnp.bfloat16)

    for head in range(heads):
        span = slice(head * HD, (head + 1) * HD)
        out_ref[1, :, span] = (dk_ref[head] * HD ** (-0.5)).astype(jnp.bfloat16)
        out_ref[2, :, span] = dv_ref[head].astype(jnp.bfloat16)


VMEM = pltpu.VMEM
KERNEL_BYTES = 62 * 2**20


def attend(lengths, proj):
    _, slot, width = proj.shape
    heads = width // HD
    return pl.pallas_call(
        attend_kernel,
        out_shape=(
            jax.ShapeDtypeStruct((slot, width), jnp.bfloat16),
            jax.ShapeDtypeStruct((heads, HD, slot), jnp.float32),
            jax.ShapeDtypeStruct((heads, 1, slot), jnp.float32),
        ),
        in_specs=[pl.BlockSpec(memory_space=pltpu.SMEM), pl.BlockSpec(memory_space=VMEM)],
        out_specs=(pl.BlockSpec(memory_space=VMEM),) * 3,
        scratch_shapes=[
            VMEM((heads, slot, 4 * HD), jnp.bfloat16),
            VMEM((heads, slot, 4 * HD), jnp.bfloat16),
            VMEM((heads, HD + 16, slot), jnp.bfloat16),
            VMEM((slot, QUERY_ROWS), jnp.float32),
        ],
        compiler_params=pltpu.CompilerParams(vmem_limit_bytes=KERNEL_BYTES),
    )(lengths, proj)


def attend_back(lengths, proj, grad, wide, lse):
    _, slot, width = proj.shape
    heads = width // HD
    return pl.pallas_call(
        attend_back_kernel,
        out_shape=jax.ShapeDtypeStruct((3, slot, width), jnp.bfloat16),
        in_specs=[pl.BlockSpec(memory_space=pltpu.SMEM)] + [pl.BlockSpec(memory_space=VMEM)] * 4,
        out_specs=pl.BlockSpec(memory_space=VMEM),
        scratch_shapes=[
            VMEM((heads, slot, HD), jnp.bfloat16),
            VMEM((heads, slot, 4 * HD), jnp.bfloat16),
            VMEM((heads, HD, slot), jnp.bfloat16),
            VMEM((heads, slot, 2 * HD), jnp.bfloat16),
            VMEM((heads, slot, HD), jnp.float32),
            VMEM((heads, slot, HD), jnp.float32),
        ],
        compiler_params=pltpu.CompilerParams(vmem_limit_bytes=KERNEL_BYTES),
    )(lengths, proj, grad, wide, lse)


MESH = pl.DeviceIdType.MESH
GATE_AT, UP_AT, DOWN_AT, OUT_AT, ALL_AT = 0, 512, 1024, 1536, 1792
AXES = ("x", "z1", "z0", "y")
SPANS = {
    "out": (OUT_AT, ALL_AT - OUT_AT),
    "gate": (GATE_AT, UP_AT - GATE_AT),
    "up": (UP_AT, DOWN_AT - UP_AT),
    "down": (DOWN_AT, OUT_AT - DOWN_AT),
}
GATHER = {
    "gain": ("z1", "z0", "y"),
    "query0": ("z1", "z0", "y"),
    "query1": ("z1", "y", "z0"),
    "out": ("z0", "z1", "x", "y"),
    "gate": ("z1", "x", "y", "z0"),
    "up": ("z1", "x", "z0", "y"),
    "down": ("z1", "y", "z0", "x"),
}
GATHER_POINTS = {
    0: ("query0", "gain", "query1"),
    1: ("gate",),
    2: ("out", "gain", "down"),
    3: ("query0", "gain", "query1"),
    4: ("up", "query0", "query1"),
    5: ("gate",),
    6: ("out", "down"),
    7: ("up",),
    8: ("gate", "down"),
    9: ("up", "out"),
    12: ("out",),
    14: ("gate",),
    17: ("up", "down"),
}
REDUCE = {
    "out": (OUT_AT, 256, ("y", "z0", "z1", "x")),
    "down0": (DOWN_AT, 256, ("z0", "y", "z1", "x")),
    "down1": (DOWN_AT + 256, 256, ("y", "z1", "z0", "x")),
    "gate0": (GATE_AT, 256, ("x", "z1", "z0", "y")),
    "gate1": (GATE_AT + 256, 256, ("x", "z0", "z1", "y")),
    "up0": (UP_AT, 256, ("z1", "y", "z0", "x")),
    "up1": (UP_AT + 256, 256, ("y", "z0", "z1", "x")),
}
QUERY_REDUCE = {"query0": ("y", "z1", "z0"), "query1": ("z0", "y", "z1")}
REDUCE_POINTS = {
    0: ("down0", "down1"),
    2: ("up1", "up0"),
    3: ("down0", "down1", "out"),
    5: ("gate0",),
    6: ("gate1",),
    7: ("up1",),
    9: ("gate0",),
    10: ("out",),
    11: ("down1",),
    12: ("down0",),
    14: ("up1", "up0"),
    15: ("gate1",),
    16: ("gate0", "out", "up0"),
    22: ("gate1",),
    23: ("query1", "query0"),
    26: ("out", "up0", "query0"),
    27: ("down1", "query1"),
    28: ("gate0", "gate1"),
    29: ("down0", "up1", "query1", "query0"),
}
FULL = slice(None)


class Place:
    def __init__(self):
        self.w = lax.axis_index("wide")
        self.n = lax.axis_index("narrow")
        self.c = lax.rem(self.n, 2)
        self.x = lax.div(self.n, 2)
        y, z0, z1 = [lax.rem(lax.div(self.w, 2**k), 2) for k in range(3)]
        self.spot = {"x": self.x, "z1": z1, "z0": z0, "y": y}
        self.core_n = self.n + 1 - 2 * self.c
        self.cross_n = self.n + 2 - 4 * self.x
        self.diag_n = 3 - self.n
        self.core = (self.w, self.core_n)
        self.cross = (self.w, self.cross_n)
        self.diag = (self.w, self.diag_n)
        self.to = {
            "x": self.cross,
            "y": (self.w + 1 - 2 * y, self.n),
            "z0": (self.w + 2 - 4 * z0, self.n),
            "z1": (self.w + 4 - 8 * z1, self.n),
        }


def enter(devices):
    barrier = pltpu.get_barrier_semaphore()
    for device in devices:
        pl.semaphore_signal(barrier, inc=1, device_id=device, device_id_type=MESH)
    pl.semaphore_wait(barrier, len(devices))


class Links:
    def __init__(self, send, recv):
        self.send, self.recv = send, recv
        self.sent = 0

    def remote(self, source, target, device):
        i = self.sent
        self.sent += 1
        return pltpu.make_async_remote_copy(
            src_ref=source,
            dst_ref=target,
            send_sem=self.send.at[i],
            recv_sem=self.recv.at[i],
            device_id=device,
            device_id_type=MESH,
        )


class Gather:
    def __init__(self, links, me, room, axes, order, lead=(), tail=()):
        self.transfers = []
        known = set()
        for axis in order:
            spot = room.at[(*lead, *(FULL if a in known else me.spot[a] for a in axes), *tail)]
            self.transfers.append(links.remote(spot, spot, me.to[axis]))
            known.add(axis)
        self.at = 0

    def step(self):
        if self.at > 0:
            self.transfers[self.at - 1].wait()
        if self.at < len(self.transfers):
            self.transfers[self.at].start()
        self.at += 1

    def finish(self):
        while self.at <= len(self.transfers):
            self.step()


class Reduce:
    def __init__(self, links, me, start, rooms, axes, order, lead=(), tail=()):
        self.values, self.stages = [start, *rooms], []
        axes = list(axes)
        for room, axis in zip(rooms, order):
            before = (FULL,) * axes.index(axis)
            after = ((FULL,) * (len(axes) - 1 - len(before)) + tail) if not self.stages else ()
            theirs = (*lead, *before, 1 - me.spot[axis], *after)
            mine = (*lead, *before, me.spot[axis], *after)
            source = self.values[len(self.stages)]
            self.stages.append((links.remote(source.at[theirs], room, me.to[axis]), mine))
            axes.remove(axis)
        self.at = 0

    def take(self):
        copy, mine = self.stages[self.at - 1]
        copy.wait()
        before, into = self.values[self.at - 1 : self.at + 1]
        return into[...].astype(jnp.float32) + before[mine].astype(jnp.float32)

    def step(self):
        if self.at > 0:
            into = self.values[self.at]
            into[...] = self.take().astype(into.dtype)
        self.stages[self.at][0].start()
        self.at += 1

    def close(self):
        while self.at < len(self.stages):
            self.step()
        return self.take()


def reduce_rooms(order, axes, lead, part, lanes):
    left, shapes = list(axes), []
    for axis in order:
        left.remove(axis)
        shapes.append((*lead, *(2,) * len(left), part, lanes))
    return shapes


def norm_rows(rows):
    scale = lax.rsqrt(jnp.mean(rows * rows, axis=-1, keepdims=True) + norm_eps)
    return scale, rows * scale


def layer_kernel(
    length_ref, tok_ref, cot_ref, qkv_ref, gateup_ref, down_ref, out_ref, gains_ref,
    layer_out, dtok_out, red_out, redq_out, gsum_out,
    rows_ref, wq_ref, gain_ref, w_ref, wo_ref, k_ref, q_ref, v_ref, wide_ref, lse_ref, turned_ref, mixed_ref,
    xs_ref, ds_ref, got_ref, dxb_ref, do_ref, cross_ref, gsend, ggot, *rest,
):
    *rooms, send, recv = rest
    me = Place()
    links = Links(send, recv)
    rows, width = tok_ref.shape
    heads = qkv_ref.shape[2] // HD
    head_width = heads * HD
    slot = 4 * rows
    half = rows // 2
    part = qkv_ref.shape[1]
    cut = part // 2
    wide_axes = AXES[1:]
    low = jnp.bfloat16
    length = length_ref[0]
    own_w = tuple(me.spot[a] for a in wide_axes)
    step_rows = 256

    def rows_of(block):
        return pl.ds(pl.multiple_of(block * rows, rows), rows)

    def weight(x, name, count=None):
        start, lanes = SPANS[name]
        lanes = lanes if count is None else count
        return w_ref[x, :, :, :, :, start : start + lanes].reshape(width, lanes)

    def other_out(x):
        return wo_ref[x, :, :, :, :, :head_width].reshape(width, head_width)

    wq_ref[(FULL, *own_w)] = qkv_ref[...].astype(low)
    gain_ref[own_w] = jnp.zeros((8, 128), jnp.float32)
    gain_ref[(*own_w, slice(0, 2), slice(0, part))] = gains_ref[...]
    own = (me.x, *own_w, FULL)
    w_ref[(*own, slice(GATE_AT, UP_AT))] = gateup_ref[0].astype(low)
    w_ref[(*own, slice(UP_AT, DOWN_AT))] = gateup_ref[1].astype(low)
    w_ref[(*own, slice(DOWN_AT, OUT_AT))] = down_ref[...].astype(low)
    pad = jnp.zeros((part, ALL_AT - OUT_AT - head_width), jnp.float32)
    w_ref[(*own, slice(OUT_AT, ALL_AT))] = jnp.concatenate([out_ref[...].T, pad], axis=1).astype(low)
    enter([me.core, me.cross, me.diag, me.to["y"], me.to["z0"], me.to["z1"]])
    cross_rows, core_rows, forward_rows = [], [], []
    for i in range(2):
        piece = pl.ds(i * half, half)
        cross_rows.append(links.remote(tok_ref.at[piece], rows_ref.at[me.n, piece], me.cross))
        core_rows.append(links.remote(tok_ref.at[piece], rows_ref.at[me.n, piece], me.core))
        there = rows_ref.at[me.cross_n, piece]
        forward_rows.append(links.remote(there, there, me.core))
    cross_rows[0].start()
    core_rows[0].start()
    core_rows[1].start()
    chains = {"gain": Gather(links, me, gain_ref, wide_axes, GATHER["gain"])}
    for i in range(2):
        name = "query%d" % i
        chains[name] = Gather(links, me, wq_ref, wide_axes, GATHER[name], (FULL,), (pl.ds(i * cut, cut),))
    for name, span in SPANS.items():
        chains[name] = Gather(links, me, w_ref, AXES, GATHER[name], (), (FULL, pl.ds(*span)))

    def gather_point(i):
        for name in GATHER_POINTS.get(i, ()):
            chains[name].step()

    gather_point(0)
    cross_rows[1].start()
    out_lanes = (FULL,) * 5 + (pl.ds(*SPANS["out"]),)
    to_core_out = links.remote(w_ref.at[out_lanes], wo_ref, me.core)
    to_core_cot = links.remote(cot_ref, ds_ref, me.core)
    to_core_tok = links.remote(tok_ref, xs_ref, me.core)

    gather_point(1)
    gather_point(2)
    gather_point(3)
    chains["gain"].finish()
    gain_row = jnp.zeros((8, width), jnp.float32)
    for w in range(8):
        lane = lax.broadcasted_iota(jnp.int32, (128, width), 0)
        column = lax.broadcasted_iota(jnp.int32, (128, width), 1)
        select = jnp.where((column == lane + w * part) & (lane < part), 1.0, 0.0)
        gain_row = gain_row + dot(gain_ref[w >> 2, (w >> 1) & 1, w & 1].astype(low), select.astype(low), NN)
    gain_one, gain_two = gain_row[0:1], gain_row[1:2]

    def normalize(block, source=None):
        held = rows_ref[block] if source is None else source[...]
        values = norm_rows(held.astype(jnp.float32))[1] * gain_one
        normed = values.astype(low)
        rows_ref[block] = normed
        turned_ref[:, rows_of(block)] = normed.T

    normalize(me.n, tok_ref)
    for copy in core_rows:
        copy.wait()
    normalize(me.core_n)
    to_core_cot.start()
    to_core_tok.start()
    gather_point(4)
    cross_rows[0].wait()
    forward_rows[0].start()
    gather_point(5)
    cross_rows[1].wait()
    forward_rows[1].start()
    gather_point(6)
    for copy in forward_rows:
        copy.wait()
    normalize(me.cross_n)
    normalize(me.diag_n)
    chains["query0"].finish()
    chains["query1"].finish()
    gather_point(7)

    def attention(proj_ref, qa_ref, vt_ref, s_ref, own_mixed):
        @pl.loop(0, 4)
        def _(block):
            normed = rows_ref[block]
            for s in range(3):
                weights = wq_ref[s].reshape(width, head_width)
                proj_ref[s, rows_of(block), :] = dot(normed, weights, NN).astype(low)

        gather_point(8)
        for head in range(heads):
            span = slice(head * HD, (head + 1) * HD)
            query = proj_ref[0, :, span]
            value = proj_ref[2, :, span]
            k_ref[head] = key_columns(proj_ref[1, :, span], length)
            q_ref[head] = query
            qa_ref[head] = query_columns(query, None)
            lane = lax.broadcasted_iota(jnp.int32, (slot, HD), 1)
            ones = jnp.where(lane < 3, 1.0, 0.0).astype(low)
            v_ref[head] = jnp.concatenate([value, ones], axis=1)
            place = lax.broadcasted_iota(jnp.int32, (16, slot), 0)
            ones = jnp.where(place == 0, 1.0, 0.0).astype(low)
            vt_ref[head] = jnp.concatenate([value.T, ones], axis=0)
        gather_point(9)

        to_cross = [
            links.remote(own_mixed.at[0], mixed_ref.at[me.n, me.c], me.cross),
            links.remote(own_mixed.at[1], mixed_ref.at[me.n, 1 - me.c], me.cross),
        ]
        to_core = [
            links.remote(own_mixed.at[2], mixed_ref.at[me.n, 1 - me.c], me.core),
            links.remote(own_mixed.at[3], mixed_ref.at[me.n, me.c], me.core),
        ]
        arrived = mixed_ref.at[me.cross_n]
        pass_on = links.remote(arrived, arrived, me.core)

        def attend_head(at_rows, head):
            query = qa_ref[head, at_rows, :]
            peak = None
            for at in range(0, slot, KEY_ROWS):
                score = dot(k_ref[head, pl.ds(at, KEY_ROWS), :], query, NT)
                s_ref[pl.ds(at, KEY_ROWS), :] = score
                most = jnp.max(score.reshape(KEY_ROWS // 8, 8, rows), axis=0)
                peak = most if peak is None else jnp.maximum(peak, most)
            peak = jnp.max(peak, axis=0, keepdims=True)
            total = None
            for at in range(0, slot, KEY_ROWS):
                soft = jnp.exp2(s_ref[pl.ds(at, KEY_ROWS), :] - peak).astype(low)
                share = dot(vt_ref[head, :, pl.ds(at, KEY_ROWS)], soft, NN)
                total = share if total is None else total + share
            row_sum = total[HD : HD + 1]
            wide = total[:HD] / row_sum
            wide_ref[head, :, at_rows] = wide
            lse_ref[head, :, at_rows] = peak + jnp.log2(row_sum)
            return wide

        @pl.loop(0, 4)
        def _(turn):
            other = 1 - lax.div(turn, 2)
            flip = lax.rem(lax.rem(turn, 2) + lax.div(turn, 2), 2)
            block = 2 * (me.x + (1 - 2 * me.x) * other) + me.c + (1 - 2 * me.c) * flip
            wides = []
            for head in range(heads):
                for at in range(4):
                    point = 9 + 3 * at + head
                    if point > 9 and point in GATHER_POINTS:
                        pl.when(turn == at)(functools.partial(gather_point, point))
                wides.append(attend_head(rows_of(block), head))
            own_mixed[turn] = jnp.concatenate(wides, axis=0).T.astype(low)
            pl.when(turn == 0)(to_cross[0].start)
            pl.when(turn == 1)(to_cross[1].start)
            pl.when(turn == 2)(to_core[0].start)
            pl.when(turn == 3)(to_core[1].start)

        chains["out"].finish()
        to_core_out.start()
        mixed_ref[me.n, 1 - me.c] = own_mixed[2]
        mixed_ref[me.n, me.c] = own_mixed[3]
        for copy in to_cross:
            copy.wait()
        pass_on.start()
        for copy in to_core + [to_core_out, to_core_cot, to_core_tok, pass_on]:
            copy.wait()

    pl.run_scoped(
        attention,
        VMEM((3, slot, head_width), low),
        VMEM((heads, slot, 4 * HD), low),
        VMEM((heads, HD + 16, slot), low),
        VMEM((slot, rows), jnp.float32),
        VMEM((4, rows, head_width), low),
    )

    at_room = 0
    reduces = {}
    for name, (start, lanes, order) in REDUCE.items():
        tail = (FULL, pl.ds(start, lanes))
        reduces[name] = Reduce(links, me, w_ref, rooms[at_room : at_room + 4], AXES, order, (), tail)
        at_room += 4

    def reduce_point(i):
        for name in REDUCE_POINTS.get(i, ()):
            reduces[name].step()

    def reduce_points(first, step, head):
        for at in range(2):
            point = first + 3 * at + head
            if point in REDUCE_POINTS:
                pl.when(step == at)(functools.partial(reduce_point, point))

    def middle(h_ref, dg_ref, du_ref, x1_ref, dh2_ref, mlp_ref, own_do, turn_ref):
        send_dh2, send_mlp = rows_ref.at[2], rows_ref.at[3]
        to_core_dh2 = links.remote(send_dh2, got_ref.at[0], me.core)
        to_core_mlp = links.remote(send_mlp, got_ref.at[1], me.core)
        to_core_dx = links.remote(dxb_ref.at[1], dxb_ref.at[0], me.core)
        to_grads = [
            links.remote(own_do.at[me.cross_n], do_ref.at[me.n], me.cross),
            links.remote(own_do.at[me.diag_n], do_ref.at[me.n], me.diag),
            links.remote(own_do.at[me.core_n], do_ref.at[me.n], me.core),
        ]

        @pl.loop(0, 4)
        def _(step):
            own = lax.div(step, 2)
            side = me.c + (1 - 2 * me.c) * (1 - own)
            at = pl.ds(pl.multiple_of(lax.rem(step, 2) * step_rows, step_rows), step_rows)
            attn = jnp.zeros((step_rows, width), jnp.float32)
            for x in range(2):
                attn += dot(mixed_ref[2 * x + me.c, side, at, :], weight(x, "out", head_width), NT)
                attn += dot(mixed_ref[2 * x + 1 - me.c, side, at, :], other_out(x), NT)

            @pl.when(own == 0)
            def _():
                x1 = xs_ref[at, :].astype(jnp.float32) + attn
                rows_ref[own, at, :] = (norm_rows(x1)[1] * gain_two).astype(low)

            @pl.when(own == 1)
            def _():
                x1 = tok_ref[at, :].astype(jnp.float32) + attn
                x1_ref[at, :] = x1
                rows_ref[own, at, :] = (norm_rows(x1)[1] * gain_two).astype(low)

        for name in ("gate", "up", "down"):
            chains[name].finish()

        def feed(own):
            @pl.loop(0, rows // step_rows)
            def _(step):
                at = pl.ds(pl.multiple_of(step * step_rows, step_rows), step_rows)
                at_all = pl.ds(pl.multiple_of(own * rows + step * step_rows, step_rows), step_rows)
                h2 = rows_ref[own, at, :]
                dy = (cot_ref if own else ds_ref)[at, :]
                dh2 = jnp.zeros((step_rows, width), jnp.float32)
                mlp = jnp.zeros((step_rows, width), jnp.float32)
                for x in range(2):
                    gate = dot(h2, weight(x, "gate"), NN)
                    up = dot(h2, weight(x, "up"), NN)
                    dh = dot(dy, weight(x, "down"), NN)
                    square = gate * gate
                    turn = jnp.tanh(gate * (0.7978845608028654 + 0.035677408136300125 * square))
                    share = 0.5 + 0.5 * turn
                    gelu = gate * share
                    slope = share + 0.5 * gate * (1.0 - turn * turn) * (
                        0.7978845608028654 + 0.10703222440890037 * square
                    )
                    h = (gelu * up).astype(low)
                    dup = (dh * gelu).astype(low)
                    dgate = (dh * up * slope).astype(low)
                    h_ref[x, at_all, :] = h
                    du_ref[x, at_all, :] = dup
                    dg_ref[x, at_all, :] = dgate
                    mlp += dot(h, weight(x, "down"), NT)
                    dh2 += dot(dgate, weight(x, "gate"), NT)
                    dh2 += dot(dup, weight(x, "up"), NT)
                if own:
                    dh2_ref[at, :] = dh2
                    mlp_ref[at, :] = mlp
                else:
                    send_dh2[at, :] = dh2.astype(low)
                    send_mlp[at, :] = mlp.astype(low)

        feed(0)
        to_core_dh2.start()
        to_core_mlp.start()
        feed(1)

        def weight_grad(name, right):
            start, lanes = SPANS[name]

            @pl.loop(0, 4)
            def _(step):
                tile = 2 * part
                left = turn_ref[pl.ds(pl.multiple_of(step * tile, tile), tile), :]
                for x in range(2):
                    value = dot(left, right(x), NN).astype(low).reshape(2, part, lanes)
                    w_ref[x, lax.div(step, 2), lax.rem(step, 2), :, :, start : start + lanes] = value

        turn_ref[:, :rows] = ds_ref[...].T
        turn_ref[:, rows:] = cot_ref[...].T
        weight_grad("down", lambda x: h_ref[x])
        reduce_point(0)
        to_core_dh2.wait()
        to_core_mlp.wait()
        gsend[0] = jnp.zeros_like(gsend[0])

        @pl.loop(0, rows // step_rows)
        def _(step):
            at = pl.ds(pl.multiple_of(step * step_rows, step_rows), step_rows)
            x1 = x1_ref[at, :]
            layer_out[at, :] = (x1 + mlp_ref[at, :] + got_ref[1, at, :].astype(jnp.float32)).astype(low)
            dh2 = dh2_ref[at, :] + got_ref[0, at, :].astype(jnp.float32)
            scale, n2 = norm_rows(x1)
            gsend[0, 1:2, :] += jnp.sum(dh2 * n2, axis=0, keepdims=True)
            e2 = dh2 * gain_two
            dx = cot_ref[at, :].astype(jnp.float32) + scale * (
                e2 - n2 * jnp.mean(e2 * n2, axis=-1, keepdims=True)
            )
            dtok_out[at, :] = dx
            dx_low = dx.astype(low)
            dxb_ref[1, at, :] = dx_low
            for x in range(2):
                own_do[2 * x + me.c, at, :] = dot(dx_low, weight(x, "out", head_width), NN).astype(low)
                own_do[2 * x + 1 - me.c, at, :] = dot(dx_low, other_out(x), NN).astype(low)

        for copy in to_grads:
            copy.start()
        to_core_dx.start()
        do_ref[me.n] = own_do[me.n]
        for i in range(2):
            turn_ref[:, i * rows : (i + 1) * rows] = rows_ref[i].T
        weight_grad("gate", lambda x: dg_ref[x])
        reduce_point(1)
        weight_grad("up", lambda x: du_ref[x])
        reduce_point(2)
        to_core_dx.wait()
        for i in range(2):
            turn_ref[:, i * rows : (i + 1) * rows] = dxb_ref[i].T

        @pl.loop(0, 4)
        def _(step):
            tile = 2 * part
            at = pl.ds(pl.multiple_of(step * tile, tile), tile)
            for x in range(2):
                value = dot(turn_ref[at, :rows], mixed_ref[2 * x + me.c, 1 - me.c], NN)
                value += dot(turn_ref[at, rows:], mixed_ref[2 * x + me.c, me.c], NN)
                value = value.astype(low).reshape(2, part, head_width)
                w_ref[x, lax.div(step, 2), lax.rem(step, 2), :, :, OUT_AT : OUT_AT + head_width] = value

        reduce_point(3)
        for copy in to_grads:
            copy.wait()

    hidden = UP_AT - GATE_AT
    pl.run_scoped(
        middle,
        VMEM((2, 2 * rows, hidden), low),
        VMEM((2, 2 * rows, hidden), low),
        VMEM((2, 2 * rows, hidden), low),
        VMEM((rows, width), jnp.float32),
        VMEM((rows, width), jnp.float32),
        VMEM((rows, width), jnp.float32),
        VMEM((4, rows, head_width), low),
        VMEM((width, 2 * rows), low),
    )

    def back(t_ref, qw_ref, gw_ref, dkv_ref, dp_ref, dq_ref):
        pair_ref = rows_ref
        for head in range(heads):
            t_ref[head] = k_ref[head, :, :HD].T
        dkv_ref[...] = jnp.zeros_like(dkv_ref)
        far = [me.cross_n, me.diag_n]
        near = [me.core_n, me.n]

        def prepare(block):
            at_rows = rows_of(block)
            grads = do_ref[block]
            grads_turned = grads.astype(jnp.float32).T
            for head in range(heads):
                span = slice(head * HD, (head + 1) * HD)
                delta = jnp.sum(grads_turned[span] * wide_ref[head, :, at_rows], axis=0, keepdims=True)
                qw_ref[head, at_rows, :] = query_columns(q_ref[head, at_rows, :], lse_ref[head, :, at_rows])
                gw_ref[head, at_rows, :] = jnp.concatenate([grads[:, span], row_columns(-delta, None)], axis=1)

        def attend_back_rows(at_rows, blocks, first, step):
            totals = []
            for head in range(heads):
                query_wide = qw_ref[head, at_rows, :]
                grad_wide = gw_ref[head, at_rows, :]
                query = q_ref[head, at_rows, :]
                grad = grad_wide[:, :HD]
                blank = jnp.zeros_like(query)
                right = jnp.concatenate(
                    [jnp.concatenate([query, blank], axis=1), jnp.concatenate([blank, grad], axis=1)], axis=0
                )
                total = None
                for block in blocks:
                    keys = rows_of(block)
                    soft = jnp.exp2(dot(k_ref[head, keys, :], query_wide, NT))
                    soft_grad = dot(v_ref[head, keys, :], grad_wide, NT)
                    score_grad = (soft * soft_grad).astype(low)
                    left = jnp.concatenate([score_grad, soft.astype(low)], axis=1)
                    dkv_ref[head, keys, :] += dot(left, right, NN)
                    share = dot(t_ref[head, :, keys], score_grad, NN)
                    total = share if total is None else total + share
                totals.append(total)
                reduce_points(first, step, head)
            return jnp.concatenate(totals, axis=0)

        def pick(pair, step):
            return pair[0] + (pair[1] - pair[0]) * step

        def close_keys(blocks):
            for block in blocks:
                at = rows_of(block)
                for head in range(heads):
                    span = slice(head * HD, (head + 1) * HD)
                    dkv = dkv_ref[head, at, :]
                    dp_ref[1, at, span] = (dkv[:, :HD] * HD ** (-0.5)).astype(low)
                    dp_ref[2, at, span] = dkv[:, HD:].astype(low)

        def input_grad(block):
            at = rows_of(block)
            total = jnp.zeros((rows, width), jnp.float32)
            for s in range(3):
                total += dot(dp_ref[s, at, :], wq_ref[s].reshape(width, head_width), NT)
            return total

        @pl.loop(0, 2)
        def _(step):
            block = pick(far, step)
            prepare(block)
            total = attend_back_rows(rows_of(block), far + near, 4, step) * HD ** (-0.5)
            dp_ref[0, rows_of(block), :] = total.T.astype(low)

        @pl.loop(0, 2)
        def _(step):
            block = pick(near, step)
            prepare(block)
            total = attend_back_rows(rows_of(block), far, 10, step)
            wide_ref[:, :, rows_of(block)] = total.reshape(heads, HD, rows)

        to_core = [links.remote(pair_ref.at[i], got_ref.at[i], me.core) for i in range(2)]
        to_cross = links.remote(pair_ref.at[2], cross_ref, me.cross)
        close_keys(far)
        pair_ref[0] = input_grad(me.diag_n).astype(low)
        to_core[0].start()
        kept = input_grad(me.cross_n)
        to_core[0].wait()
        pair_ref[2] = (kept + got_ref[0].astype(jnp.float32)).astype(low)
        to_cross.start()
        reduce_point(16)

        @pl.loop(0, 2)
        def _(step):
            at = rows_of(pick(near, step))
            total = wide_ref[:, :, at].reshape(head_width, rows) + attend_back_rows(at, near, 17, step)
            total = total * HD ** (-0.5)
            dp_ref[0, at, :] = total.T.astype(low)

        close_keys(near)
        gain_sum = jnp.zeros((width, 1), jnp.float32)
        for s in range(3):
            total = dot(turned_ref[...], dp_ref[s], NN)
            weights = wq_ref[s].reshape(width, head_width).astype(jnp.float32)
            gain_sum += jnp.sum(total * weights, axis=-1, keepdims=True)
            dq_ref[s] = total.astype(low).reshape(dq_ref.shape[1:])
        for i, (name, order) in enumerate(QUERY_REDUCE.items()):
            at = at_room + 3 * i
            tail = (pl.ds(i * cut, cut),)
            reduces[name] = Reduce(links, me, dq_ref, rooms[at : at + 3], wide_axes, order, (FULL,), tail)
        reduce_point(23)
        gain_place = lax.broadcasted_iota(jnp.int32, (width, 128), 1)
        gsend[0] = gsend[0] + jnp.where(gain_place == 0, gain_sum, 0.0).T[0:8]
        hops = [me.core, me.cross, me.to["y"], me.to["z0"], me.to["z1"]]
        gains = [links.remote(gsend.at[i], ggot.at[i], device) for i, device in enumerate(hops)]

        def gain_step(i):
            gains[i].wait()
            gsend[i + 1] = gsend[i] + ggot[i]
            if i + 1 < len(gains):
                gains[i + 1].start()

        gains[0].start()
        pair_ref[1] = input_grad(me.core_n).astype(low)
        to_core[1].start()
        reduce_point(24)
        gain_step(0)
        pair_ref[3] = input_grad(me.n).astype(low)
        reduce_point(25)
        gain_step(1)
        reduce_point(26)
        gain_step(2)
        reduce_point(27)
        to_core[1].wait()
        to_cross.wait()

        @pl.loop(0, rows // step_rows)
        def _(step):
            at = pl.ds(pl.multiple_of(step * step_rows, step_rows), step_rows)
            dh1 = pair_ref[3, at, :].astype(jnp.float32) + got_ref[1, at, :].astype(jnp.float32)
            dh1 += cross_ref[at, :].astype(jnp.float32)
            scale, n1 = norm_rows(tok_ref[at, :].astype(jnp.float32))
            e1 = dh1 * gain_one
            dtok_out[at, :] += scale * (e1 - n1 * jnp.mean(e1 * n1, axis=-1, keepdims=True))

        reduce_point(28)
        gain_step(3)
        reduce_point(29)
        for name, (start, lanes, _) in REDUCE.items():
            red_out[:, start : start + lanes] = reduces[name].close()
        gain_step(4)
        redq_out[:, :cut] = reduces["query0"].close()
        redq_out[:, cut:] = reduces["query1"].close()
        own_lane = lax.broadcasted_iota(jnp.int32, (width, 128), 0) == gain_place + me.w * part
        select = jnp.where(own_lane & (gain_place < part), 1.0, 0.0).astype(low)
        held = jnp.zeros((8, 128), jnp.float32)
        for piece in pieces(gsend[len(gains)]):
            held += dot(piece, select, NN)
        gsum_out[...] = held

    pl.run_scoped(
        back,
        VMEM((heads, HD, slot), low),
        VMEM((heads, slot, 4 * HD), low),
        VMEM((heads, slot, 2 * HD), low),
        VMEM((heads, slot, 2 * HD), jnp.float32),
        VMEM((3, slot, head_width), low),
        VMEM((3, 2, 2, 2, part, head_width), low),
    )


def update_kernel(
    red_ref, redq_ref, gsum_ref,
    qkv_w, out_w, gateup_w, down_w, gains_w,
    qkv_m, qkv_s, out_m, out_s, gateup_m, gateup_s, down_m, down_s, gains_m, gains_s,
    *outs,
):
    def put(at, weight, mean, square, gradient, rate, decay):
        results = adam_update(weight[...], mean[...], square[...], gradient, rate, decay)
        for ref, value in zip(outs[3 * at : 3 * at + 3], results):
            ref[...] = value

    slice_rows = red_ref.shape[0]
    put(0, qkv_w, qkv_m, qkv_s, redq_ref[...], D ** (-0.5), decay_rate)
    heads_width = out_w.shape[0]
    put(1, out_w, out_m, out_s, red_ref[:, OUT_AT : OUT_AT + heads_width].T, OUT_FAN ** (-0.5), decay_rate)
    both = jnp.stack([red_ref[:, GATE_AT:UP_AT], red_ref[:, UP_AT:DOWN_AT]])
    put(2, gateup_w, gateup_m, gateup_s, both, D ** (-0.5), decay_rate)
    put(3, down_w, down_m, down_s, red_ref[:, DOWN_AT:OUT_AT], FF ** (-0.5), decay_rate)
    gain = gains_w[...].astype(jnp.bfloat16).astype(jnp.float32)
    gain_grad = gsum_ref[0:2, :slice_rows]
    row = lax.broadcasted_iota(jnp.int32, gain.shape, 0)
    gain_grad = jnp.where(row == 0, gain_grad / gain, gain_grad)
    put(4, gains_w, gains_m, gains_s, gain_grad, gain_rate, 0.0)


IN_VMEM = pl.BlockSpec(memory_space=pltpu.VMEM)
IN_SMEM = pl.BlockSpec(memory_space=pltpu.SMEM)


def shards_fast(
    tokens, lengths, qkv_weight, out_weight, gateup_weight, down_weight, norm_gains,
    qkv_mean, qkv_square, out_mean, out_square, gateup_mean, gateup_square, down_mean, down_square,
    gains_mean, gains_square, cotangent,
):
    low, wide_type = jnp.bfloat16, jnp.float32
    shape = jax.ShapeDtypeStruct
    rows, width = tokens.shape
    slot = 4 * rows
    part = qkv_weight.shape[1]
    heads = qkv_weight.shape[2] // HD
    head_width = heads * HD
    tail = ALL_AT - OUT_AT
    wide_bits = (2, 2, 2)

    rooms = []
    for _, lanes, order in REDUCE.values():
        rooms += reduce_rooms(order, AXES, (), part, lanes)
    for order in QUERY_REDUCE.values():
        rooms += reduce_rooms(order, AXES[1:], (3,), part // 2, head_width)
    layer_out, dtok, red, redq, gsum = pl.pallas_call(
        layer_kernel,
        out_shape=(
            shape((rows, width), low),
            shape((rows, width), wide_type),
            shape((part, ALL_AT), wide_type),
            shape((3, part, head_width), wide_type),
            shape((8, 128), wide_type),
        ),
        in_specs=[IN_SMEM] + [IN_VMEM] * 7,
        out_specs=(IN_VMEM,) * 5,
        scratch_shapes=[
            VMEM((4, rows, width), low),
            VMEM((3, *wide_bits, part, head_width), low),
            VMEM((*wide_bits, 8, 128), wide_type),
            VMEM((2, *wide_bits, part, ALL_AT), low),
            VMEM((2, *wide_bits, part, tail), low),
            VMEM((heads, slot, 4 * HD), low),
            VMEM((heads, slot, HD), low),
            VMEM((heads, slot, 2 * HD), low),
            VMEM((heads, HD, slot), wide_type),
            VMEM((heads, 1, slot), wide_type),
            VMEM((width, slot), low),
            VMEM((4, 2, rows, head_width), low),
            VMEM((rows, width), low),
            VMEM((rows, width), low),
            VMEM((2, rows, width), low),
            VMEM((2, rows, width), low),
            VMEM((4, rows, head_width), low),
            VMEM((rows, width), low),
            VMEM((6, 8, width), wide_type),
            VMEM((5, 8, width), wide_type),
            *[VMEM(room, low) for room in rooms],
            pltpu.SemaphoreType.DMA((96,)),
            pltpu.SemaphoreType.DMA((96,)),
        ],
        compiler_params=pltpu.CompilerParams(
            collective_id=1, has_side_effects=True, vmem_limit_bytes=KERNEL_BYTES
        ),
    )(lengths, tokens, cotangent, qkv_weight, gateup_weight, down_weight.T, out_weight, norm_gains)

    weights = (qkv_weight, out_weight, gateup_weight, down_weight.T, norm_gains)
    moments = (
        qkv_mean, qkv_square, out_mean, out_square, gateup_mean, gateup_square, down_mean.T, down_square.T,
        gains_mean, gains_square,
    )
    updated = pl.pallas_call(
        update_kernel,
        out_shape=tuple(shape(w.shape, wide_type) for w in weights for _ in range(3)),
        in_specs=[IN_VMEM] * 18,
        out_specs=(IN_VMEM,) * 15,
        compiler_params=pltpu.CompilerParams(vmem_limit_bytes=KERNEL_BYTES),
    )(red, redq, gsum, *weights, *moments)
    down_updated = [value.T for value in updated[9:12]]
    return (layer_out, dtok, *updated[:9], *down_updated, *updated[12:])


def shards(
    tokens,
    lengths,
    qkv_weight,
    out_weight,
    gateup_weight,
    down_weight,
    norm_gains,
    qkv_mean,
    qkv_square,
    out_mean,
    out_square,
    gateup_mean,
    gateup_square,
    down_mean,
    down_square,
    gains_mean,
    gains_square,
    cotangent,
):
    lowered = (
        qkv_weight.astype(jnp.bfloat16),
        out_weight.astype(jnp.bfloat16),
        gateup_weight.astype(jnp.bfloat16),
        down_weight.astype(jnp.bfloat16),
        norm_gains.astype(jnp.bfloat16),
    )
    qkv_full, out_full, gateup_full, down_full, gains_full = (
        lax.all_gather(lowered[0], "wide", axis=1, tiled=True),
        lax.all_gather(lowered[1], "wide", axis=1, tiled=True),
        lax.all_gather(lowered[2], "wide", axis=1, tiled=True),
        lax.all_gather(lowered[3], "wide", axis=1, tiled=True),
        lax.all_gather(lowered[4], "wide", axis=1, tiled=True),
    )
    gain_values = gains_full.astype(jnp.float32)
    rows_full = lax.all_gather(tokens, "narrow", axis=0, tiled=True)
    rows_float = rows_full.astype(jnp.float32)
    normed_one = rms_scale(rows_float, gain_values[0]).astype(jnp.bfloat16)
    projected = jnp.einsum(
        "td,sde->ste", normed_one, qkv_full, preferred_element_type=jnp.float32
    ).astype(jnp.bfloat16)
    mixed, mixed_wide, row_lse = attend(lengths, projected)
    attn_partial = jnp.dot(mixed, out_full, preferred_element_type=jnp.float32)
    own_float = tokens.astype(jnp.float32)
    attn_own = lax.psum_scatter(attn_partial, "narrow", scatter_dimension=0, tiled=True)
    residual_own = own_float + attn_own
    residual_full = lax.all_gather(residual_own, "narrow", axis=0, tiled=True)
    normed_two = rms_scale(residual_full, gain_values[1]).astype(jnp.bfloat16)
    gateup = jnp.einsum("td,sdf->stf", normed_two, gateup_full, preferred_element_type=jnp.float32)
    hidden = gelu_product(gateup[0], gateup[1]).astype(jnp.bfloat16)
    mlp_own = lax.psum_scatter(
        jnp.dot(hidden, down_full, preferred_element_type=jnp.float32).astype(jnp.bfloat16),
        "narrow",
        scatter_dimension=0,
        tiled=True,
    ).astype(jnp.float32)
    layer_out = (residual_own + mlp_own).astype(jnp.bfloat16)
    grad_full = lax.all_gather(cotangent, "narrow", axis=0, tiled=True)
    down_grad = jnp.einsum("tf,td->fd", hidden, grad_full, preferred_element_type=jnp.float32)
    hidden_grad = jnp.einsum("td,fd->tf", grad_full, down_full, preferred_element_type=jnp.float32)
    primal_out, gelu_back = jax.vjp(gelu_product, gateup[0], gateup[1])
    gate_grad, up_grad = gelu_back(hidden_grad)
    gateup_rows = jnp.stack([gate_grad, up_grad]).astype(jnp.bfloat16)
    gateup_grad = jnp.einsum(
        "td,stf->sdf", normed_two, gateup_rows, preferred_element_type=jnp.float32
    )
    normed_two_part = jnp.einsum(
        "stf,sdf->td", gateup_rows, gateup_full, preferred_element_type=jnp.float32
    )
    normed_two_grad = lax.psum_scatter(
        normed_two_part.astype(jnp.bfloat16), "narrow", scatter_dimension=0, tiled=True
    ).astype(jnp.float32)
    primal_two, norm_two_back = jax.vjp(rms_scale, residual_own, gain_values[1])
    residual_part, gain_two_grad = norm_two_back(normed_two_grad)
    residual_grad = cotangent.astype(jnp.float32) + residual_part
    residual_low = lax.all_gather(residual_grad.astype(jnp.bfloat16), "narrow", axis=0, tiled=True)
    out_grad = jnp.einsum("te,td->ed", mixed, residual_low, preferred_element_type=jnp.float32)
    mixed_grad = jnp.einsum(
        "td,ed->te", residual_low, out_full, preferred_element_type=jnp.float32
    ).astype(jnp.bfloat16)
    qkv_rows = attend_back(lengths, projected, mixed_grad, mixed_wide, row_lse)
    qkv_grad = jnp.einsum("td,ste->sde", normed_one, qkv_rows, preferred_element_type=jnp.float32)
    normed_one_part = jnp.einsum(
        "ste,sde->td", qkv_rows, qkv_full, preferred_element_type=jnp.float32
    )
    normed_one_grad = lax.psum_scatter(
        normed_one_part.astype(jnp.bfloat16), "narrow", scatter_dimension=0, tiled=True
    ).astype(jnp.float32)
    primal_one, norm_one_back = jax.vjp(rms_scale, own_float, gain_values[0])
    tokens_part, gain_one_grad = norm_one_back(normed_one_grad)
    tokens_grad = residual_grad + tokens_part
    gains_grad = lax.psum(jnp.stack([gain_one_grad, gain_two_grad]), "narrow")
    reduced_qkv, reduced_out, reduced_gateup, reduced_down, reduced_gains = (
        lax.psum_scatter(qkv_grad, "wide", scatter_dimension=1, tiled=True),
        lax.psum_scatter(out_grad, "wide", scatter_dimension=1, tiled=True),
        lax.psum_scatter(gateup_grad, "wide", scatter_dimension=1, tiled=True),
        lax.psum_scatter(down_grad, "wide", scatter_dimension=1, tiled=True),
        lax.psum_scatter(gains_grad, "wide", scatter_dimension=1, tiled=True),
    )
    qkv_master, qkv_first, qkv_second = adam_update(
        qkv_weight, qkv_mean, qkv_square, reduced_qkv, D ** (-0.5), decay_rate
    )
    out_master, out_first, out_second = adam_update(
        out_weight, out_mean, out_square, reduced_out, OUT_FAN ** (-0.5), decay_rate
    )
    gateup_master, gateup_first, gateup_second = adam_update(
        gateup_weight, gateup_mean, gateup_square, reduced_gateup, D ** (-0.5), decay_rate
    )
    down_master, down_first, down_second = adam_update(
        down_weight, down_mean, down_square, reduced_down, FF ** (-0.5), decay_rate
    )
    gains_master, gains_first, gains_second = adam_update(
        norm_gains, gains_mean, gains_square, reduced_gains, gain_rate, 0.0
    )
    return (
        layer_out,
        tokens_grad,
        qkv_master,
        qkv_first,
        qkv_second,
        out_master,
        out_first,
        out_second,
        gateup_master,
        gateup_first,
        gateup_second,
        down_master,
        down_first,
        down_second,
        gains_master,
        gains_first,
        gains_second,
    )


def solution(mesh):
    part = D // mesh.shape["wide"]
    fits = mesh.shape["narrow"] == 4 and mesh.shape["wide"] == 8 and part % 32 == 0
    return jax.shard_map(
        shards_fast if fits else shards,
        mesh=mesh,
        in_specs=(
            P(("wide", "narrow"), None),
            P("wide"),
            P(None, "wide", "narrow"),
            P("narrow", "wide"),
            P(None, "wide", "narrow"),
            P("narrow", "wide"),
            P(None, "wide"),
            P(None, "wide", "narrow"),
            P(None, "wide", "narrow"),
            P("narrow", "wide"),
            P("narrow", "wide"),
            P(None, "wide", "narrow"),
            P(None, "wide", "narrow"),
            P("narrow", "wide"),
            P("narrow", "wide"),
            P(None, "wide"),
            P(None, "wide"),
            P(("wide", "narrow"), None),
        ),
        out_specs=(
            P(("wide", "narrow"), None),
            P(("wide", "narrow"), None),
            P(None, "wide", "narrow"),
            P(None, "wide", "narrow"),
            P(None, "wide", "narrow"),
            P("narrow", "wide"),
            P("narrow", "wide"),
            P("narrow", "wide"),
            P(None, "wide", "narrow"),
            P(None, "wide", "narrow"),
            P(None, "wide", "narrow"),
            P("narrow", "wide"),
            P("narrow", "wide"),
            P("narrow", "wide"),
            P(None, "wide"),
            P(None, "wide"),
            P(None, "wide"),
        ),
        check_vma=False,
    )
```

```python
import functools

import jax
import jax.numpy as jnp
from jax import lax
from jax.experimental import pallas as pl
from jax.experimental.pallas import tpu as pltpu
from jax.sharding import PartitionSpec as P

D = 768
HEADS = 12
HD = 64
FF = 2048
SLOT = 2048
STEP_COUNT = 5
OUT_FAN = 1


norm_eps = 1e-06
adam_eps = 1e-08
beta_first = 0.5
beta_second = 0.5
decay_rate = 0.01
gain_rate = 0.3
masked_score = -1e30


def rms_scale(rows, gain):
    return rows * lax.rsqrt(jnp.mean(rows * rows, axis=-1, keepdims=True) + norm_eps) * gain


def gelu_product(gate_part, up_part):
    return jax.nn.gelu(gate_part, approximate=True) * up_part


def adam_update(weight, mean_old, square_old, gradient, rate, decay):
    mean_new = beta_first * mean_old + (1.0 - beta_first) * gradient
    square_new = beta_second * square_old + (1.0 - beta_second) * gradient * gradient
    mean_hat = mean_new / (1.0 - beta_first**STEP_COUNT)
    square_hat = square_new / (1.0 - beta_second**STEP_COUNT)
    weight_new = weight - rate * (mean_hat / (jnp.sqrt(square_hat) + adam_eps) + decay * weight)
    return (weight_new, mean_new, square_new)


LOG2E = 1.4426950408889634
NN = (((1,), (0,)), ((), ()))
NT = (((1,), (1,)), ((), ()))
QUERY_ROWS = 512
KEY_ROWS = 512


def pieces(value):
    high = value.astype(jnp.bfloat16)
    rest = value - high.astype(jnp.float32)
    mid = rest.astype(jnp.bfloat16)
    low = (rest - mid.astype(jnp.float32)).astype(jnp.bfloat16)
    return high, mid, low


def dot(left, right, dims):
    return lax.dot_general(left, right, dims, preferred_element_type=jnp.float32)


def key_columns(key_rows, length):
    rows = key_rows.shape[0]
    lane = lax.broadcasted_iota(jnp.int32, (rows, HD), 1)
    row = lax.broadcasted_iota(jnp.int32, (rows, HD), 0)
    mask = jnp.where(row < length, 0.0, masked_score)
    extra = jnp.where(lane == 0, mask, jnp.where(lane < 4, 1.0, 0.0)).astype(jnp.bfloat16)
    return jnp.concatenate([key_rows, key_rows, key_rows, extra], axis=1)


def query_columns(query_rows, shift):
    scaled = query_rows.astype(jnp.float32) * (LOG2E * HD ** (-0.5))
    if shift is None:
        lane = lax.broadcasted_iota(jnp.int32, query_rows.shape, 1)
        extra = jnp.where(lane == 0, 1.0, 0.0).astype(jnp.bfloat16)
    else:
        extra = row_columns(-shift, 1.0)
    return jnp.concatenate([*pieces(scaled), extra], axis=1)


def row_columns(row_value, first):
    count = row_value.shape[1]
    high, mid, low = [piece.astype(jnp.float32) for piece in pieces(row_value)]
    place = lax.broadcasted_iota(jnp.int32, (HD, count), 0)
    if first is None:
        held = jnp.where(place == 0, high, jnp.where(place == 1, mid, jnp.where(place == 2, low, 0.0)))
    else:
        held = jnp.where(place == 1, high, jnp.where(place == 2, mid, jnp.where(place == 3, low, 0.0)))
        held = jnp.where(place == 0, first, held)
    return held.T.astype(jnp.bfloat16)


def attend_kernel(length_ref, proj_ref, out_ref, wide_ref, lse_ref, q_ref, k_ref, v_ref, s_ref):
    slot = proj_ref.shape[1]
    heads = proj_ref.shape[2] // HD
    length = length_ref[0]
    for head in range(heads):
        span = slice(head * HD, (head + 1) * HD)
        k_ref[head] = key_columns(proj_ref[1, :, span], length)
        q_ref[head] = query_columns(proj_ref[0, :, span], None)
        turned = proj_ref[2, :, span].astype(jnp.float32).T.astype(jnp.bfloat16)
        place = lax.broadcasted_iota(jnp.int32, (16, slot), 0)
        ones = jnp.where(place == 0, 1.0, 0.0).astype(jnp.bfloat16)
        v_ref[head] = jnp.concatenate([turned, ones], axis=0)

    @pl.loop(0, slot // QUERY_ROWS)
    def _(block):
        start = pl.multiple_of(block * QUERY_ROWS, QUERY_ROWS)
        turned = []
        for head in range(heads):
            query = q_ref[head, pl.ds(start, QUERY_ROWS), :]
            peak = None
            for at in range(0, slot, KEY_ROWS):
                score = dot(k_ref[head, pl.ds(at, KEY_ROWS), :], query, NT)
                s_ref[pl.ds(at, KEY_ROWS), :] = score
                most = jnp.max(score.reshape(KEY_ROWS // 8, 8, QUERY_ROWS), axis=0)
                peak = most if peak is None else jnp.maximum(peak, most)
            peak = jnp.max(peak, axis=0, keepdims=True)
            total = None
            for at in range(0, slot, KEY_ROWS):
                soft = jnp.exp2(s_ref[pl.ds(at, KEY_ROWS), :] - peak).astype(jnp.bfloat16)
                part = dot(v_ref[head, :, pl.ds(at, KEY_ROWS)], soft, NN)
                total = part if total is None else total + part
            row_sum = total[HD : HD + 1]
            wide = total[:HD] / row_sum
            wide_ref[head, :, pl.ds(start, QUERY_ROWS)] = wide
            lse_ref[head, :, pl.ds(start, QUERY_ROWS)] = peak + jnp.log2(row_sum)
            turned.append(wide)
        joined = jnp.concatenate(turned, axis=0)
        out_ref[pl.ds(start, QUERY_ROWS), :] = joined.T.astype(jnp.bfloat16)


def attend_back_kernel(
    length_ref, proj_ref, grad_ref, wide_ref, lse_ref, out_ref, q_ref, k_ref, t_ref, v_ref, dk_ref, dv_ref
):
    slot = proj_ref.shape[1]
    heads = proj_ref.shape[2] // HD
    length = length_ref[0]
    key_turned = proj_ref[1].astype(jnp.float32).T.astype(jnp.bfloat16)
    for head in range(heads):
        span = slice(head * HD, (head + 1) * HD)
        k_ref[head] = key_columns(proj_ref[1, :, span], length)
        q_ref[head] = proj_ref[0, :, span]
        t_ref[head] = key_turned[span]
        lane = lax.broadcasted_iota(jnp.int32, (slot, HD), 1)
        ones = jnp.where(lane < 3, 1.0, 0.0).astype(jnp.bfloat16)
        v_ref[head] = jnp.concatenate([proj_ref[2, :, span], ones], axis=1)
    dk_ref[...] = jnp.zeros_like(dk_ref)
    dv_ref[...] = jnp.zeros_like(dv_ref)

    @pl.loop(0, slot // QUERY_ROWS)
    def _(block):
        start = pl.multiple_of(block * QUERY_ROWS, QUERY_ROWS)
        rows = pl.ds(start, QUERY_ROWS)
        turned = []
        grads = grad_ref[rows, :]
        grads_turned = grads.astype(jnp.float32).T
        for head in range(heads):
            span = slice(head * HD, (head + 1) * HD)
            query = q_ref[head, rows, :]
            grad = grads[:, span]
            delta = jnp.sum(grads_turned[span] * wide_ref[head, :, rows], axis=0, keepdims=True)
            query_wide = query_columns(query, lse_ref[head, :, rows])
            grad_wide = jnp.concatenate([grad, row_columns(-delta, None)], axis=1)
            total = None
            for at in range(0, slot, KEY_ROWS):
                keys = pl.ds(at, KEY_ROWS)
                soft = jnp.exp2(dot(k_ref[head, keys, :], query_wide, NT))
                soft_grad = dot(v_ref[head, keys, :], grad_wide, NT)
                soft_low = soft.astype(jnp.bfloat16)
                score_grad = (soft * soft_grad).astype(jnp.bfloat16)
                dv_ref[head, keys, :] += dot(soft_low, grad, NN)
                dk_ref[head, keys, :] += dot(score_grad, query, NN)
                part = dot(t_ref[head, :, keys], score_grad, NN)
                total = part if total is None else total + part
            turned.append(total * HD ** (-0.5))
        joined = jnp.concatenate(turned, axis=0)
        out_ref[0, rows, :] = joined.T.astype(jnp.bfloat16)

    for head in range(heads):
        span = slice(head * HD, (head + 1) * HD)
        out_ref[1, :, span] = (dk_ref[head] * HD ** (-0.5)).astype(jnp.bfloat16)
        out_ref[2, :, span] = dv_ref[head].astype(jnp.bfloat16)


VMEM = pltpu.VMEM
KERNEL_BYTES = 62 * 2**20


def attend(lengths, proj):
    _, slot, width = proj.shape
    heads = width // HD
    return pl.pallas_call(
        attend_kernel,
        out_shape=(
            jax.ShapeDtypeStruct((slot, width), jnp.bfloat16),
            jax.ShapeDtypeStruct((heads, HD, slot), jnp.float32),
            jax.ShapeDtypeStruct((heads, 1, slot), jnp.float32),
        ),
        in_specs=[pl.BlockSpec(memory_space=pltpu.SMEM), pl.BlockSpec(memory_space=VMEM)],
        out_specs=(pl.BlockSpec(memory_space=VMEM),) * 3,
        scratch_shapes=[
            VMEM((heads, slot, 4 * HD), jnp.bfloat16),
            VMEM((heads, slot, 4 * HD), jnp.bfloat16),
            VMEM((heads, HD + 16, slot), jnp.bfloat16),
            VMEM((slot, QUERY_ROWS), jnp.float32),
        ],
        compiler_params=pltpu.CompilerParams(vmem_limit_bytes=KERNEL_BYTES),
    )(lengths, proj)


def attend_back(lengths, proj, grad, wide, lse):
    _, slot, width = proj.shape
    heads = width // HD
    return pl.pallas_call(
        attend_back_kernel,
        out_shape=jax.ShapeDtypeStruct((3, slot, width), jnp.bfloat16),
        in_specs=[pl.BlockSpec(memory_space=pltpu.SMEM)] + [pl.BlockSpec(memory_space=VMEM)] * 4,
        out_specs=pl.BlockSpec(memory_space=VMEM),
        scratch_shapes=[
            VMEM((heads, slot, HD), jnp.bfloat16),
            VMEM((heads, slot, 4 * HD), jnp.bfloat16),
            VMEM((heads, HD, slot), jnp.bfloat16),
            VMEM((heads, slot, 2 * HD), jnp.bfloat16),
            VMEM((heads, slot, HD), jnp.float32),
            VMEM((heads, slot, HD), jnp.float32),
        ],
        compiler_params=pltpu.CompilerParams(vmem_limit_bytes=KERNEL_BYTES),
    )(lengths, proj, grad, wide, lse)


MESH = pl.DeviceIdType.MESH
GATE_AT, UP_AT, DOWN_AT, OUT_AT, ALL_AT = 0, 512, 1024, 1536, 1792
AXES = ("x", "z1", "z0", "y")
SPANS = {
    "out": (OUT_AT, ALL_AT - OUT_AT),
    "gate": (GATE_AT, UP_AT - GATE_AT),
    "up": (UP_AT, DOWN_AT - UP_AT),
    "down": (DOWN_AT, OUT_AT - DOWN_AT),
}
GATHER = {
    "gain": ("z1", "z0", "y"),
    "query0": ("z1", "z0", "y"),
    "query1": ("z1", "y", "z0"),
}
GATHER_PIECES = {
    "out": (OUT_AT, 256, ("z0", "z1", "x", "y")),
    "gate0": (GATE_AT, 256, ("z1", "y", "x", "z0")),
    "gate1": (GATE_AT + 256, 256, ("y", "x", "z1", "z0")),
    "up0": (UP_AT, 256, ("z1", "x", "z0", "y")),
    "up1": (UP_AT + 256, 256, ("z1", "z0", "y", "x")),
    "down0": (DOWN_AT, 256, ("z1", "z0", "y", "x")),
    "down1": (DOWN_AT + 256, 256, ("x", "z1", "z0", "y")),
}
GATHER_POINTS = {
    0: ("gain", "query0", "query1", "gate0",),
    1: ("down1",),
    2: ("gain", "out", "gate1", "gate1", "down0",),
    3: ("gain", "query0", "query1",),
    4: ("query0", "query1",),
    5: ("up0",),
    6: ("up1", "down0",),
    7: ("out", "gate0",),
    8: ("up0",),
    9: ("gate0",),
    10: ("up1", "gate1", "down0", "down1",),
    12: ("out", "up0", "up1",),
    16: ("out", "up1", "gate1",),
    18: ("up0", "down1",),
    20: ("down0",),
    22: ("down1", "gate0",),
}
REDUCE = {
    "out": (OUT_AT, 256, ("y", "z1", "z0", "x")),
    "down0": (DOWN_AT, 256, ("x", "y", "z0", "z1")),
    "down1": (DOWN_AT + 256, 256, ("y", "x", "z1", "z0")),
    "gate0": (GATE_AT, 256, ("z0", "y", "z1", "x")),
    "gate1": (GATE_AT + 256, 256, ("z1", "x", "z0", "y")),
    "up0": (UP_AT, 256, ("y", "z1", "x", "z0")),
    "up1": (UP_AT + 256, 256, ("x", "y", "z1", "z0")),
}
QUERY_REDUCE = {"query0": ("y", "z1", "z0"), "query1": ("z0", "y", "z1")}
REDUCE_POINTS = {
    0: ("down1",),
    1: ("gate1",),
    2: ("down0", "up0", "up1",),
    3: ("out", "gate0",),
    4: ("down1",),
    7: ("up0",),
    8: ("down0",),
    11: ("up1", "out",),
    13: ("gate1",),
    14: ("down0", "gate0",),
    15: ("up1",),
    16: ("down1",),
    17: ("gate0",),
    18: ("out",),
    19: ("down0",),
    21: ("gate1",),
    23: ("query1", "query0",),
    24: ("down1",),
    25: ("up0", "query0",),
    26: ("query1", "gate0",),
    27: ("up1",),
    29: ("query1", "up0", "out", "gate1", "query0",),
}
FULL = slice(None)


class Place:
    def __init__(self):
        self.w = lax.axis_index("wide")
        self.n = lax.axis_index("narrow")
        self.c = lax.rem(self.n, 2)
        self.x = lax.div(self.n, 2)
        y, z0, z1 = [lax.rem(lax.div(self.w, 2**k), 2) for k in range(3)]
        self.spot = {"x": self.x, "z1": z1, "z0": z0, "y": y}
        self.core_n = self.n + 1 - 2 * self.c
        self.cross_n = self.n + 2 - 4 * self.x
        self.diag_n = 3 - self.n
        self.core = (self.w, self.core_n)
        self.cross = (self.w, self.cross_n)
        self.diag = (self.w, self.diag_n)
        self.to = {
            "x": self.cross,
            "y": (self.w + 1 - 2 * y, self.n),
            "z0": (self.w + 2 - 4 * z0, self.n),
            "z1": (self.w + 4 - 8 * z1, self.n),
        }


def enter(devices):
    barrier = pltpu.get_barrier_semaphore()
    for device in devices:
        pl.semaphore_signal(barrier, inc=1, device_id=device, device_id_type=MESH)
    pl.semaphore_wait(barrier, len(devices))


class Links:
    def __init__(self, send, recv):
        self.send, self.recv = send, recv
        self.sent = 0

    def remote(self, source, target, device):
        i = self.sent
        self.sent += 1
        return pltpu.make_async_remote_copy(
            src_ref=source,
            dst_ref=target,
            send_sem=self.send.at[i],
            recv_sem=self.recv.at[i],
            device_id=device,
            device_id_type=MESH,
        )


class Gather:
    def __init__(self, links, me, room, axes, order, lead=(), tail=()):
        self.transfers = []
        known = set()
        for axis in order:
            spot = room.at[(*lead, *(FULL if a in known else me.spot[a] for a in axes), *tail)]
            self.transfers.append(links.remote(spot, spot, me.to[axis]))
            known.add(axis)

    def step(self, at):
        if at > 0:
            self.transfers[at - 1].wait()
        if at < len(self.transfers):
            self.transfers[at].start()


class Reduce:
    def __init__(self, links, me, start, rooms, axes, order, lead=(), tail=()):
        self.values, self.stages = [start, *rooms], []
        axes = list(axes)
        for room, axis in zip(rooms, order):
            before = (FULL,) * axes.index(axis)
            after = ((FULL,) * (len(axes) - 1 - len(before)) + tail) if not self.stages else ()
            theirs = (*lead, *before, 1 - me.spot[axis], *after)
            mine = (*lead, *before, me.spot[axis], *after)
            source = self.values[len(self.stages)]
            self.stages.append((links.remote(source.at[theirs], room, me.to[axis]), mine))
            axes.remove(axis)

    def take(self, at):
        copy, mine = self.stages[at - 1]
        copy.wait()
        before, into = self.values[at - 1 : at + 1]
        return into[...].astype(jnp.float32) + before[mine].astype(jnp.float32)

    def step(self, at):
        if at > 0:
            into = self.values[at]
            into[...] = self.take(at).astype(into.dtype)
        self.stages[at][0].start()

    def close(self):
        return self.take(len(self.stages))


def numbered(points):
    seen, steps = {}, {}
    for point in sorted(points):
        steps[point] = []
        for name in points[point]:
            steps[point].append((name, seen.get(name, 0)))
            seen[name] = seen.get(name, 0) + 1
    return steps


def reduce_rooms(order, axes, lead, part, lanes):
    left, shapes = list(axes), []
    for axis in order:
        left.remove(axis)
        shapes.append((*lead, *(2,) * len(left), part, lanes))
    return shapes


def norm_rows(rows):
    scale = lax.rsqrt(jnp.mean(rows * rows, axis=-1, keepdims=True) + norm_eps)
    return scale, rows * scale


def layer_kernel(
    length_ref, tok_ref, cot_ref, qkv_ref, gateup_ref, down_ref, out_ref, gains_ref,
    layer_out, dtok_out, red_out, redq_out, gsum_out,
    rows_ref, wq_ref, gain_ref, w_ref, wo_ref, k_ref, q_ref, v_ref, wide_ref, lse_ref, turned_ref, mixed_ref,
    xs_ref, ds_ref, got_ref, dxb_ref, do_ref, cross_ref, gsend, ggot, *rest,
):
    *rooms, send, recv = rest
    me = Place()
    links = Links(send, recv)
    rows, width = tok_ref.shape
    heads = qkv_ref.shape[2] // HD
    head_width = heads * HD
    slot = 4 * rows
    half = rows // 2
    part = qkv_ref.shape[1]
    cut = part // 2
    wide_axes = AXES[1:]
    low = jnp.bfloat16
    length = length_ref[0]
    own_w = tuple(me.spot[a] for a in wide_axes)
    step_rows = 256
    feed_rows = 512

    def rows_of(block):
        return pl.ds(pl.multiple_of(block * rows, rows), rows)

    def weight(x, name, count=None):
        start, lanes = SPANS[name]
        lanes = lanes if count is None else count
        return w_ref[x, :, :, :, :, start : start + lanes].reshape(width, lanes)

    def other_out(x):
        return wo_ref[x, :, :, :, :, :head_width].reshape(width, head_width)

    wq_ref[(FULL, *own_w)] = qkv_ref[...].astype(low)
    gain_ref[own_w] = jnp.zeros((8, 128), jnp.float32)
    gain_ref[(*own_w, slice(0, 2), slice(0, part))] = gains_ref[...]
    own = (me.x, *own_w, FULL)
    w_ref[(*own, slice(GATE_AT, UP_AT))] = gateup_ref[0].astype(low)
    w_ref[(*own, slice(UP_AT, DOWN_AT))] = gateup_ref[1].astype(low)
    w_ref[(*own, slice(DOWN_AT, OUT_AT))] = down_ref[...].astype(low)
    pad = jnp.zeros((part, ALL_AT - OUT_AT - head_width), jnp.float32)
    w_ref[(*own, slice(OUT_AT, ALL_AT))] = jnp.concatenate([out_ref[...].T, pad], axis=1).astype(low)
    enter([me.core, me.cross, me.diag, me.to["y"], me.to["z0"], me.to["z1"]])
    cross_rows, core_rows, forward_rows = [], [], []
    for i in range(2):
        piece = pl.ds(i * half, half)
        cross_rows.append(links.remote(tok_ref.at[piece], rows_ref.at[me.n, piece], me.cross))
        core_rows.append(links.remote(tok_ref.at[piece], rows_ref.at[me.n, piece], me.core))
        there = rows_ref.at[me.cross_n, piece]
        forward_rows.append(links.remote(there, there, me.core))
    cross_rows[0].start()
    core_rows[0].start()
    core_rows[1].start()
    chains = {"gain": Gather(links, me, gain_ref, wide_axes, GATHER["gain"])}
    for i in range(2):
        name = "query%d" % i
        chains[name] = Gather(links, me, wq_ref, wide_axes, GATHER[name], (FULL,), (pl.ds(i * cut, cut),))
    for name, (start, lanes, order) in GATHER_PIECES.items():
        chains[name] = Gather(links, me, w_ref, AXES, order, (), (FULL, pl.ds(start, lanes)))

    gather_steps, reduce_steps = numbered(GATHER_POINTS), numbered(REDUCE_POINTS)

    def gather_point(i):
        for name, at in gather_steps.get(i, ()):
            chains[name].step(at)

    def gather_end(name):
        chains[name].step(len(chains[name].transfers))

    gather_point(0)
    cross_rows[1].start()
    out_lanes = (FULL,) * 5 + (pl.ds(*SPANS["out"]),)
    to_core_out = links.remote(w_ref.at[out_lanes], wo_ref, me.core)
    to_core_cot = links.remote(cot_ref, ds_ref, me.core)
    to_core_tok = links.remote(tok_ref, xs_ref, me.core)
    for i in range(1, 4):
        gather_point(i)
    gather_end("gain")
    gain_row = jnp.zeros((8, width), jnp.float32)
    for w in range(8):
        lane = lax.broadcasted_iota(jnp.int32, (128, width), 0)
        column = lax.broadcasted_iota(jnp.int32, (128, width), 1)
        select = jnp.where((column == lane + w * part) & (lane < part), 1.0, 0.0)
        gain_row = gain_row + dot(gain_ref[w >> 2, (w >> 1) & 1, w & 1].astype(low), select.astype(low), NN)
    gain_one, gain_two = gain_row[0:1], gain_row[1:2]

    whole, halves = pl.ds(0, rows), [pl.ds(0, half), pl.ds(half, half)]

    def normalize(block, piece, source=None):
        held = rows_ref[block, piece, :] if source is None else source[...]
        rows_ref[block, piece, :] = (norm_rows(held.astype(jnp.float32))[1] * gain_one).astype(low)

    def attention(qa_ref, vt_ref, s_ref, own_mixed):
        place = lax.broadcasted_iota(jnp.int32, (heads, 16, slot), 1)
        vt_ref[:, HD:, :] = jnp.where(place == 0, 1.0, 0.0).astype(low)

        def project(block, piece):
            normed = rows_ref[block, piece, :]
            first = pl.multiple_of(block * rows + piece.start, half)
            at = pl.ds(first, piece.size)
            turned_ref[:, at] = normed.T
            query, key, value = [
                dot(normed, wq_ref[s].reshape(width, head_width), NN).astype(low) for s in range(3)
            ]
            lane = lax.broadcasted_iota(jnp.int32, (piece.size, HD), 1)
            ones = jnp.where(lane < 3, 1.0, 0.0).astype(low)
            value_turned = value.T
            for head in range(heads):
                span = slice(head * HD, (head + 1) * HD)
                k_ref[head, at, :] = key_columns(key[:, span], length - first)
                q_ref[head, at, :] = query[:, span]
                qa_ref[head, at, :] = query_columns(query[:, span], None)
                v_ref[head, at, :] = jnp.concatenate([value[:, span], ones], axis=1)
                vt_ref[head, :HD, at] = value_turned[span]

        normalize(me.n, whole, tok_ref)
        gather_point(4)
        for copy in core_rows:
            copy.wait()
        normalize(me.core_n, whole)
        gather_point(5)
        cross_rows[0].wait()
        forward_rows[0].start()
        to_core_cot.start()
        to_core_tok.start()
        gather_point(6)
        forward_rows[0].wait()
        normalize(me.cross_n, halves[0])
        normalize(me.diag_n, halves[0])
        gather_end("query0")
        gather_end("query1")
        gather_point(7)
        project(me.n, whole)
        project(me.core_n, whole)
        gather_point(8)
        cross_rows[1].wait()
        forward_rows[1].start()
        project(me.cross_n, halves[0])
        project(me.diag_n, halves[0])
        gather_point(9)
        forward_rows[1].wait()
        normalize(me.cross_n, halves[1])
        normalize(me.diag_n, halves[1])
        project(me.cross_n, halves[1])
        project(me.diag_n, halves[1])

        to_cross = [links.remote(own_mixed.at[0, i], mixed_ref.at[me.n, i], me.cross) for i in range(2)]
        to_core = [links.remote(own_mixed.at[1, i], mixed_ref.at[me.n, i], me.core) for i in range(2)]
        pass_on = links.remote(mixed_ref.at[me.cross_n], mixed_ref.at[me.cross_n], me.core)

        def attend_head(at_rows, head):
            query = qa_ref[head, at_rows, :]
            peak = None
            for at in range(0, slot, KEY_ROWS):
                score = dot(k_ref[head, pl.ds(at, KEY_ROWS), :], query, NT)
                s_ref[pl.ds(at, KEY_ROWS), :] = score
                most = jnp.max(score.reshape(KEY_ROWS // 8, 8, rows), axis=0)
                peak = most if peak is None else jnp.maximum(peak, most)
            peak = jnp.max(peak, axis=0, keepdims=True)
            total = None
            for at in range(0, slot, KEY_ROWS):
                soft = jnp.exp2(s_ref[pl.ds(at, KEY_ROWS), :] - peak).astype(low)
                share = dot(vt_ref[head, :, pl.ds(at, KEY_ROWS)], soft, NN)
                total = share if total is None else total + share
            row_sum = total[HD : HD + 1]
            wide = total[:HD] / row_sum
            wide_ref[head, :, at_rows] = wide
            lse_ref[head, :, at_rows] = peak + jnp.log2(row_sum)
            return wide

        def hand_on():
            for copy in to_cross:
                copy.wait()
            pass_on.start()

        @pl.loop(0, 4)
        def _(turn):
            near, side = lax.div(turn, 2), lax.rem(turn, 2)
            chip = me.x + (1 - 2 * me.x) * (1 - near)
            at_rows = rows_of(2 * chip + side)
            wides = []
            for head in range(heads):
                for at in range(4):
                    point = 10 + 3 * at + head
                    if point in GATHER_POINTS:
                        pl.when(turn == at)(functools.partial(gather_point, point))
                if head == 1:
                    pl.when(turn == 3)(hand_on)
                wides.append(attend_head(at_rows, head))
            own_mixed[near, side] = jnp.concatenate(wides, axis=0).T.astype(low)
            for at, copy in enumerate(to_cross + to_core):
                pl.when(turn == at)(copy.start)

        gather_point(22)
        mixed_ref[me.n] = own_mixed[1]
        gather_end("out")
        to_core_out.start()
        for copy in to_core + [to_core_out, to_core_cot, to_core_tok, pass_on]:
            copy.wait()

    pl.run_scoped(
        attention,
        VMEM((heads, slot, 4 * HD), low),
        VMEM((heads, HD + 16, slot), low),
        VMEM((slot, rows), jnp.float32),
        VMEM((2, 2, rows, head_width), low),
    )

    at_room = 0
    reduces = {}
    for name, (start, lanes, order) in REDUCE.items():
        tail = (FULL, pl.ds(start, lanes))
        reduces[name] = Reduce(links, me, w_ref, rooms[at_room : at_room + 4], AXES, order, (), tail)
        at_room += 4

    def reduce_point(i):
        for name, at in reduce_steps.get(i, ()):
            reduces[name].step(at)

    def reduce_points(first, step, head):
        for at in range(2):
            point = first + 3 * at + head
            if point in REDUCE_POINTS:
                pl.when(step == at)(functools.partial(reduce_point, point))

    def middle(h_ref, dg_ref, du_ref, x1_ref, dh2_ref, mlp_ref, own_do, turn_ref):
        send_dh2, send_mlp = rows_ref.at[2], rows_ref.at[3]
        to_core_dh2 = links.remote(send_dh2, got_ref.at[0], me.core)
        to_core_mlp = links.remote(send_mlp, got_ref.at[1], me.core)
        to_core_dx = links.remote(dxb_ref.at[1], dxb_ref.at[0], me.core)
        to_grads = [
            links.remote(own_do.at[me.cross_n], do_ref.at[me.n], me.cross),
            links.remote(own_do.at[me.diag_n], do_ref.at[me.n], me.diag),
            links.remote(own_do.at[me.core_n], do_ref.at[me.n], me.core),
        ]

        @pl.loop(0, 4)
        def _(step):
            own = lax.div(step, 2)
            side = me.c + (1 - 2 * me.c) * (1 - own)
            at = pl.ds(pl.multiple_of(lax.rem(step, 2) * step_rows, step_rows), step_rows)
            attn = jnp.zeros((step_rows, width), jnp.float32)
            for x in range(2):
                attn += dot(mixed_ref[2 * x + me.c, side, at, :], weight(x, "out", head_width), NT)
                attn += dot(mixed_ref[2 * x + 1 - me.c, side, at, :], other_out(x), NT)

            @pl.when(own == 0)
            def _():
                x1 = xs_ref[at, :].astype(jnp.float32) + attn
                rows_ref[own, at, :] = (norm_rows(x1)[1] * gain_two).astype(low)

            @pl.when(own == 1)
            def _():
                x1 = tok_ref[at, :].astype(jnp.float32) + attn
                x1_ref[at, :] = x1
                rows_ref[own, at, :] = (norm_rows(x1)[1] * gain_two).astype(low)

            for at in range(4):
                if 23 + at in GATHER_POINTS:
                    pl.when(step == at)(functools.partial(gather_point, 23 + at))

        for name in GATHER_PIECES:
            if name != "out":
                gather_end(name)

        def feed(own):
            @pl.loop(0, rows // feed_rows)
            def _(step):
                at = pl.ds(pl.multiple_of(step * feed_rows, feed_rows), feed_rows)
                at_all = pl.ds(pl.multiple_of(own * rows + step * feed_rows, feed_rows), feed_rows)
                h2 = rows_ref[own, at, :]
                dy = (cot_ref if own else ds_ref)[at, :]
                dh2 = jnp.zeros((feed_rows, width), jnp.float32)
                mlp = jnp.zeros((feed_rows, width), jnp.float32)
                for x in range(2):
                    gate = dot(h2, weight(x, "gate"), NN)
                    up = dot(h2, weight(x, "up"), NN)
                    dh = dot(dy, weight(x, "down"), NN)
                    square = gate * gate
                    turn = jnp.tanh(gate * (0.7978845608028654 + 0.035677408136300125 * square))
                    share = 0.5 + 0.5 * turn
                    gelu = gate * share
                    slope = share + 0.5 * gate * (1.0 - turn * turn) * (
                        0.7978845608028654 + 0.10703222440890037 * square
                    )
                    h = (gelu * up).astype(low)
                    dup = (dh * gelu).astype(low)
                    dgate = (dh * up * slope).astype(low)
                    h_ref[x, at_all, :] = h
                    du_ref[x, at_all, :] = dup
                    dg_ref[x, at_all, :] = dgate
                    mlp += dot(h, weight(x, "down"), NT)
                    dh2 += dot(dgate, weight(x, "gate"), NT)
                    dh2 += dot(dup, weight(x, "up"), NT)
                if own:
                    dh2_ref[at, :] = dh2
                    mlp_ref[at, :] = mlp
                else:
                    send_dh2[at, :] = dh2.astype(low)
                    send_mlp[at, :] = mlp.astype(low)

        feed(0)
        to_core_dh2.start()
        to_core_mlp.start()
        feed(1)

        def weight_grad(name, right):
            start, lanes = SPANS[name]

            @pl.loop(0, 4)
            def _(step):
                tile = 2 * part
                left = turn_ref[pl.ds(pl.multiple_of(step * tile, tile), tile), :]
                for x in range(2):
                    value = dot(left, right(x), NN).astype(low).reshape(2, part, lanes)
                    w_ref[x, lax.div(step, 2), lax.rem(step, 2), :, :, start : start + lanes] = value

        to_core_dh2.wait()
        to_core_mlp.wait()
        gsend[0] = jnp.zeros_like(gsend[0])

        @pl.loop(0, rows // step_rows)
        def _(step):
            at = pl.ds(pl.multiple_of(step * step_rows, step_rows), step_rows)
            x1 = x1_ref[at, :]
            layer_out[at, :] = (x1 + mlp_ref[at, :] + got_ref[1, at, :].astype(jnp.float32)).astype(low)
            dh2 = dh2_ref[at, :] + got_ref[0, at, :].astype(jnp.float32)
            scale, n2 = norm_rows(x1)
            gsend[0, 1:2, :] += jnp.sum(dh2 * n2, axis=0, keepdims=True)
            e2 = dh2 * gain_two
            dx = cot_ref[at, :].astype(jnp.float32) + scale * (
                e2 - n2 * jnp.mean(e2 * n2, axis=-1, keepdims=True)
            )
            dtok_out[at, :] = dx
            dx_low = dx.astype(low)
            dxb_ref[1, at, :] = dx_low
            for x in range(2):
                own_do[2 * x + me.c, at, :] = dot(dx_low, weight(x, "out", head_width), NN).astype(low)
                own_do[2 * x + 1 - me.c, at, :] = dot(dx_low, other_out(x), NN).astype(low)

        for copy in to_grads:
            copy.start()
        to_core_dx.start()
        do_ref[me.n] = own_do[me.n]
        turn_ref[:, :rows] = ds_ref[...].T
        turn_ref[:, rows:] = cot_ref[...].T
        weight_grad("down", lambda x: h_ref[x])
        reduce_point(0)
        for i in range(2):
            turn_ref[:, i * rows : (i + 1) * rows] = rows_ref[i].T
        weight_grad("gate", lambda x: dg_ref[x])
        reduce_point(1)
        weight_grad("up", lambda x: du_ref[x])
        reduce_point(2)
        to_core_dx.wait()
        for i in range(2):
            turn_ref[:, i * rows : (i + 1) * rows] = dxb_ref[i].T

        @pl.loop(0, 4)
        def _(step):
            tile = 2 * part
            at = pl.ds(pl.multiple_of(step * tile, tile), tile)
            for x in range(2):
                value = dot(turn_ref[at, :rows], mixed_ref[2 * x + me.c, 1 - me.c], NN)
                value += dot(turn_ref[at, rows:], mixed_ref[2 * x + me.c, me.c], NN)
                value = value.astype(low).reshape(2, part, head_width)
                w_ref[x, lax.div(step, 2), lax.rem(step, 2), :, :, OUT_AT : OUT_AT + head_width] = value

        reduce_point(3)
        for copy in to_grads:
            copy.wait()

    hidden = UP_AT - GATE_AT
    pl.run_scoped(
        middle,
        VMEM((2, 2 * rows, hidden), low),
        VMEM((2, 2 * rows, hidden), low),
        VMEM((2, 2 * rows, hidden), low),
        VMEM((rows, width), jnp.float32),
        VMEM((rows, width), jnp.float32),
        VMEM((rows, width), jnp.float32),
        VMEM((4, rows, head_width), low),
        VMEM((width, 2 * rows), low),
    )

    def back(t_ref, qw_ref, gw_ref, dkv_ref, dp_ref, dq_ref):
        pair_ref = rows_ref
        for head in range(heads):
            t_ref[head] = k_ref[head, :, :HD].T
        dkv_ref[...] = jnp.zeros_like(dkv_ref)
        far = [me.cross_n, me.diag_n]
        near = [me.core_n, me.n]

        def prepare(block):
            at_rows = rows_of(block)
            grads = do_ref[block]
            grads_turned = grads.astype(jnp.float32).T
            for head in range(heads):
                span = slice(head * HD, (head + 1) * HD)
                delta = jnp.sum(grads_turned[span] * wide_ref[head, :, at_rows], axis=0, keepdims=True)
                qw_ref[head, at_rows, :] = query_columns(q_ref[head, at_rows, :], lse_ref[head, :, at_rows])
                gw_ref[head, at_rows, :] = jnp.concatenate([grads[:, span], row_columns(-delta, None)], axis=1)

        def attend_back_rows(at_rows, blocks, first, step):
            totals = []
            for head in range(heads):
                query_wide = qw_ref[head, at_rows, :]
                grad_wide = gw_ref[head, at_rows, :]
                query = q_ref[head, at_rows, :]
                grad = grad_wide[:, :HD]
                blank = jnp.zeros_like(query)
                right = jnp.concatenate(
                    [jnp.concatenate([query, blank], axis=1), jnp.concatenate([blank, grad], axis=1)], axis=0
                )
                total = None
                for block in blocks:
                    keys = rows_of(block)
                    soft = jnp.exp2(dot(k_ref[head, keys, :], query_wide, NT))
                    soft_grad = dot(v_ref[head, keys, :], grad_wide, NT)
                    score_grad = (soft * soft_grad).astype(low)
                    left = jnp.concatenate([score_grad, soft.astype(low)], axis=1)
                    dkv_ref[head, keys, :] += dot(left, right, NN)
                    share = dot(t_ref[head, :, keys], score_grad, NN)
                    total = share if total is None else total + share
                totals.append(total)
                reduce_points(first, step, head)
            return jnp.concatenate(totals, axis=0)

        def pick(pair, step):
            return pair[0] + (pair[1] - pair[0]) * step

        def close_keys(blocks):
            for block in blocks:
                at = rows_of(block)
                for head in range(heads):
                    span = slice(head * HD, (head + 1) * HD)
                    dkv = dkv_ref[head, at, :]
                    dp_ref[1, at, span] = (dkv[:, :HD] * HD ** (-0.5)).astype(low)
                    dp_ref[2, at, span] = dkv[:, HD:].astype(low)

        def input_grad(block):
            at = rows_of(block)
            total = jnp.zeros((rows, width), jnp.float32)
            for s in range(3):
                total += dot(dp_ref[s, at, :], wq_ref[s].reshape(width, head_width), NT)
            return total

        @pl.loop(0, 2)
        def _(step):
            block = pick(far, step)
            prepare(block)
            total = attend_back_rows(rows_of(block), far + near, 4, step) * HD ** (-0.5)
            dp_ref[0, rows_of(block), :] = total.T.astype(low)

        @pl.loop(0, 2)
        def _(step):
            block = pick(near, step)
            prepare(block)
            total = attend_back_rows(rows_of(block), far, 10, step)
            wide_ref[:, :, rows_of(block)] = total.reshape(heads, HD, rows)

        to_core = [links.remote(pair_ref.at[i], got_ref.at[i], me.core) for i in range(2)]
        to_cross = links.remote(pair_ref.at[2], cross_ref, me.cross)
        close_keys(far)
        pair_ref[0] = input_grad(me.diag_n).astype(low)
        to_core[0].start()
        kept = input_grad(me.cross_n)
        to_core[0].wait()
        pair_ref[2] = (kept + got_ref[0].astype(jnp.float32)).astype(low)
        to_cross.start()
        reduce_point(16)

        @pl.loop(0, 2)
        def _(step):
            at = rows_of(pick(near, step))
            total = wide_ref[:, :, at].reshape(head_width, rows) + attend_back_rows(at, near, 17, step)
            total = total * HD ** (-0.5)
            dp_ref[0, at, :] = total.T.astype(low)

        close_keys(near)
        gain_sum = jnp.zeros((width, 1), jnp.float32)
        for s in range(3):
            total = dot(turned_ref[...], dp_ref[s], NN)
            weights = wq_ref[s].reshape(width, head_width).astype(jnp.float32)
            gain_sum += jnp.sum(total * weights, axis=-1, keepdims=True)
            dq_ref[s] = total.astype(low).reshape(dq_ref.shape[1:])
        for i, (name, order) in enumerate(QUERY_REDUCE.items()):
            at = at_room + 3 * i
            tail = (pl.ds(i * cut, cut),)
            reduces[name] = Reduce(links, me, dq_ref, rooms[at : at + 3], wide_axes, order, (FULL,), tail)
        reduce_point(23)
        gain_place = lax.broadcasted_iota(jnp.int32, (width, 128), 1)
        gsend[0] = gsend[0] + jnp.where(gain_place == 0, gain_sum, 0.0).T[0:8]
        hops = [me.core, me.cross, me.to["y"], me.to["z0"], me.to["z1"]]
        gains = [links.remote(gsend.at[i], ggot.at[i], device) for i, device in enumerate(hops)]

        def gain_step(i):
            gains[i].wait()
            gsend[i + 1] = gsend[i] + ggot[i]
            if i + 1 < len(gains):
                gains[i + 1].start()

        gains[0].start()
        pair_ref[1] = input_grad(me.core_n).astype(low)
        to_core[1].start()
        reduce_point(24)
        gain_step(0)
        pair_ref[3] = input_grad(me.n).astype(low)
        reduce_point(25)
        gain_step(1)
        reduce_point(26)
        gain_step(2)
        reduce_point(27)
        to_core[1].wait()
        to_cross.wait()

        @pl.loop(0, rows // step_rows)
        def _(step):
            at = pl.ds(pl.multiple_of(step * step_rows, step_rows), step_rows)
            dh1 = pair_ref[3, at, :].astype(jnp.float32) + got_ref[1, at, :].astype(jnp.float32)
            dh1 += cross_ref[at, :].astype(jnp.float32)
            scale, n1 = norm_rows(tok_ref[at, :].astype(jnp.float32))
            e1 = dh1 * gain_one
            dtok_out[at, :] += scale * (e1 - n1 * jnp.mean(e1 * n1, axis=-1, keepdims=True))

        reduce_point(28)
        gain_step(3)
        reduce_point(29)
        for name, (start, lanes, _) in REDUCE.items():
            red_out[:, start : start + lanes] = reduces[name].close()
        gain_step(4)
        redq_out[:, :cut] = reduces["query0"].close()
        redq_out[:, cut:] = reduces["query1"].close()
        own_lane = lax.broadcasted_iota(jnp.int32, (width, 128), 0) == gain_place + me.w * part
        select = jnp.where(own_lane & (gain_place < part), 1.0, 0.0).astype(low)
        held = jnp.zeros((8, 128), jnp.float32)
        for piece in pieces(gsend[len(gains)]):
            held += dot(piece, select, NN)
        gsum_out[...] = held

    pl.run_scoped(
        back,
        VMEM((heads, HD, slot), low),
        VMEM((heads, slot, 4 * HD), low),
        VMEM((heads, slot, 2 * HD), low),
        VMEM((heads, slot, 2 * HD), jnp.float32),
        VMEM((3, slot, head_width), low),
        VMEM((3, 2, 2, 2, part, head_width), low),
    )


def update_kernel(
    red_ref, redq_ref, gsum_ref,
    qkv_w, out_w, gateup_w, down_w, gains_w,
    qkv_m, qkv_s, out_m, out_s, gateup_m, gateup_s, down_m, down_s, gains_m, gains_s, layer_ref, dtok_ref,
    *outs,
):
    def put(at, weight, mean, square, gradient, rate, decay):
        results = adam_update(weight[...], mean[...], square[...], gradient, rate, decay)
        for ref, value in zip(outs[3 * at : 3 * at + 3], results):
            ref[...] = value

    outs[15][...] = layer_ref[...]
    outs[16][...] = dtok_ref[...]
    slice_rows = red_ref.shape[0]
    put(0, qkv_w, qkv_m, qkv_s, redq_ref[...], D ** (-0.5), decay_rate)
    heads_width = out_w.shape[0]
    put(1, out_w, out_m, out_s, red_ref[:, OUT_AT : OUT_AT + heads_width].T, OUT_FAN ** (-0.5), decay_rate)
    both = jnp.stack([red_ref[:, GATE_AT:UP_AT], red_ref[:, UP_AT:DOWN_AT]])
    put(2, gateup_w, gateup_m, gateup_s, both, D ** (-0.5), decay_rate)
    put(3, down_w, down_m, down_s, red_ref[:, DOWN_AT:OUT_AT], FF ** (-0.5), decay_rate)
    gain = gains_w[...].astype(jnp.bfloat16).astype(jnp.float32)
    gain_grad = gsum_ref[0:2, :slice_rows]
    row = lax.broadcasted_iota(jnp.int32, gain.shape, 0)
    gain_grad = jnp.where(row == 0, gain_grad / gain, gain_grad)
    put(4, gains_w, gains_m, gains_s, gain_grad, gain_rate, 0.0)


IN_VMEM = pl.BlockSpec(memory_space=pltpu.VMEM)
IN_SMEM = pl.BlockSpec(memory_space=pltpu.SMEM)


def shards_fast(
    tokens, lengths, qkv_weight, out_weight, gateup_weight, down_weight, norm_gains,
    qkv_mean, qkv_square, out_mean, out_square, gateup_mean, gateup_square, down_mean, down_square,
    gains_mean, gains_square, cotangent,
):
    low, wide_type = jnp.bfloat16, jnp.float32
    shape = jax.ShapeDtypeStruct
    rows, width = tokens.shape
    slot = 4 * rows
    part = qkv_weight.shape[1]
    heads = qkv_weight.shape[2] // HD
    head_width = heads * HD
    tail = ALL_AT - OUT_AT
    wide_bits = (2, 2, 2)

    rooms = []
    for _, lanes, order in REDUCE.values():
        rooms += reduce_rooms(order, AXES, (), part, lanes)
    for order in QUERY_REDUCE.values():
        rooms += reduce_rooms(order, AXES[1:], (3,), part // 2, head_width)
    layer_out, dtok, red, redq, gsum = pl.pallas_call(
        layer_kernel,
        out_shape=(
            shape((rows, width), low),
            shape((rows, width), wide_type),
            shape((part, ALL_AT), wide_type),
            shape((3, part, head_width), wide_type),
            shape((8, 128), wide_type),
        ),
        in_specs=[IN_SMEM] + [IN_VMEM] * 7,
        out_specs=(IN_VMEM,) * 5,
        scratch_shapes=[
            VMEM((4, rows, width), low),
            VMEM((3, *wide_bits, part, head_width), low),
            VMEM((*wide_bits, 8, 128), wide_type),
            VMEM((2, *wide_bits, part, ALL_AT), low),
            VMEM((2, *wide_bits, part, tail), low),
            VMEM((heads, slot, 4 * HD), low),
            VMEM((heads, slot, HD), low),
            VMEM((heads, slot, 2 * HD), low),
            VMEM((heads, HD, slot), wide_type),
            VMEM((heads, 1, slot), wide_type),
            VMEM((width, slot), low),
            VMEM((4, 2, rows, head_width), low),
            VMEM((rows, width), low),
            VMEM((rows, width), low),
            VMEM((2, rows, width), low),
            VMEM((2, rows, width), low),
            VMEM((4, rows, head_width), low),
            VMEM((rows, width), low),
            VMEM((6, 8, width), wide_type),
            VMEM((5, 8, width), wide_type),
            *[VMEM(room, low) for room in rooms],
            pltpu.SemaphoreType.DMA((100,)),
            pltpu.SemaphoreType.DMA((100,)),
        ],
        compiler_params=pltpu.CompilerParams(
            collective_id=1, has_side_effects=True, vmem_limit_bytes=KERNEL_BYTES
        ),
    )(lengths, tokens, cotangent, qkv_weight, gateup_weight, down_weight.T, out_weight, norm_gains)

    weights = (qkv_weight, out_weight, gateup_weight, down_weight.T, norm_gains)
    moments = (
        qkv_mean, qkv_square, out_mean, out_square, gateup_mean, gateup_square, down_mean.T, down_square.T,
        gains_mean, gains_square,
    )
    updated = pl.pallas_call(
        update_kernel,
        out_shape=(
            *[shape(w.shape, wide_type) for w in weights for _ in range(3)],
            shape((rows, width), low),
            shape((rows, width), wide_type),
        ),
        in_specs=[IN_VMEM] * 20,
        out_specs=(IN_VMEM,) * 17,
        compiler_params=pltpu.CompilerParams(vmem_limit_bytes=KERNEL_BYTES),
    )(red, redq, gsum, *weights, *moments, layer_out, dtok)
    down_updated = [value.T for value in updated[9:12]]
    return (*updated[15:], *updated[:9], *down_updated, *updated[12:15])


def shards(
    tokens,
    lengths,
    qkv_weight,
    out_weight,
    gateup_weight,
    down_weight,
    norm_gains,
    qkv_mean,
    qkv_square,
    out_mean,
    out_square,
    gateup_mean,
    gateup_square,
    down_mean,
    down_square,
    gains_mean,
    gains_square,
    cotangent,
):
    lowered = (
        qkv_weight.astype(jnp.bfloat16),
        out_weight.astype(jnp.bfloat16),
        gateup_weight.astype(jnp.bfloat16),
        down_weight.astype(jnp.bfloat16),
        norm_gains.astype(jnp.bfloat16),
    )
    qkv_full, out_full, gateup_full, down_full, gains_full = (
        lax.all_gather(lowered[0], "wide", axis=1, tiled=True),
        lax.all_gather(lowered[1], "wide", axis=1, tiled=True),
        lax.all_gather(lowered[2], "wide", axis=1, tiled=True),
        lax.all_gather(lowered[3], "wide", axis=1, tiled=True),
        lax.all_gather(lowered[4], "wide", axis=1, tiled=True),
    )
    gain_values = gains_full.astype(jnp.float32)
    rows_full = lax.all_gather(tokens, "narrow", axis=0, tiled=True)
    rows_float = rows_full.astype(jnp.float32)
    normed_one = rms_scale(rows_float, gain_values[0]).astype(jnp.bfloat16)
    projected = jnp.einsum(
        "td,sde->ste", normed_one, qkv_full, preferred_element_type=jnp.float32
    ).astype(jnp.bfloat16)
    mixed, mixed_wide, row_lse = attend(lengths, projected)
    attn_partial = jnp.dot(mixed, out_full, preferred_element_type=jnp.float32)
    own_float = tokens.astype(jnp.float32)
    attn_own = lax.psum_scatter(attn_partial, "narrow", scatter_dimension=0, tiled=True)
    residual_own = own_float + attn_own
    residual_full = lax.all_gather(residual_own, "narrow", axis=0, tiled=True)
    normed_two = rms_scale(residual_full, gain_values[1]).astype(jnp.bfloat16)
    gateup = jnp.einsum("td,sdf->stf", normed_two, gateup_full, preferred_element_type=jnp.float32)
    hidden = gelu_product(gateup[0], gateup[1]).astype(jnp.bfloat16)
    mlp_own = lax.psum_scatter(
        jnp.dot(hidden, down_full, preferred_element_type=jnp.float32).astype(jnp.bfloat16),
        "narrow",
        scatter_dimension=0,
        tiled=True,
    ).astype(jnp.float32)
    layer_out = (residual_own + mlp_own).astype(jnp.bfloat16)
    grad_full = lax.all_gather(cotangent, "narrow", axis=0, tiled=True)
    down_grad = jnp.einsum("tf,td->fd", hidden, grad_full, preferred_element_type=jnp.float32)
    hidden_grad = jnp.einsum("td,fd->tf", grad_full, down_full, preferred_element_type=jnp.float32)
    primal_out, gelu_back = jax.vjp(gelu_product, gateup[0], gateup[1])
    gate_grad, up_grad = gelu_back(hidden_grad)
    gateup_rows = jnp.stack([gate_grad, up_grad]).astype(jnp.bfloat16)
    gateup_grad = jnp.einsum(
        "td,stf->sdf", normed_two, gateup_rows, preferred_element_type=jnp.float32
    )
    normed_two_part = jnp.einsum(
        "stf,sdf->td", gateup_rows, gateup_full, preferred_element_type=jnp.float32
    )
    normed_two_grad = lax.psum_scatter(
        normed_two_part.astype(jnp.bfloat16), "narrow", scatter_dimension=0, tiled=True
    ).astype(jnp.float32)
    primal_two, norm_two_back = jax.vjp(rms_scale, residual_own, gain_values[1])
    residual_part, gain_two_grad = norm_two_back(normed_two_grad)
    residual_grad = cotangent.astype(jnp.float32) + residual_part
    residual_low = lax.all_gather(residual_grad.astype(jnp.bfloat16), "narrow", axis=0, tiled=True)
    out_grad = jnp.einsum("te,td->ed", mixed, residual_low, preferred_element_type=jnp.float32)
    mixed_grad = jnp.einsum(
        "td,ed->te", residual_low, out_full, preferred_element_type=jnp.float32
    ).astype(jnp.bfloat16)
    qkv_rows = attend_back(lengths, projected, mixed_grad, mixed_wide, row_lse)
    qkv_grad = jnp.einsum("td,ste->sde", normed_one, qkv_rows, preferred_element_type=jnp.float32)
    normed_one_part = jnp.einsum(
        "ste,sde->td", qkv_rows, qkv_full, preferred_element_type=jnp.float32
    )
    normed_one_grad = lax.psum_scatter(
        normed_one_part.astype(jnp.bfloat16), "narrow", scatter_dimension=0, tiled=True
    ).astype(jnp.float32)
    primal_one, norm_one_back = jax.vjp(rms_scale, own_float, gain_values[0])
    tokens_part, gain_one_grad = norm_one_back(normed_one_grad)
    tokens_grad = residual_grad + tokens_part
    gains_grad = lax.psum(jnp.stack([gain_one_grad, gain_two_grad]), "narrow")
    reduced_qkv, reduced_out, reduced_gateup, reduced_down, reduced_gains = (
        lax.psum_scatter(qkv_grad, "wide", scatter_dimension=1, tiled=True),
        lax.psum_scatter(out_grad, "wide", scatter_dimension=1, tiled=True),
        lax.psum_scatter(gateup_grad, "wide", scatter_dimension=1, tiled=True),
        lax.psum_scatter(down_grad, "wide", scatter_dimension=1, tiled=True),
        lax.psum_scatter(gains_grad, "wide", scatter_dimension=1, tiled=True),
    )
    qkv_master, qkv_first, qkv_second = adam_update(
        qkv_weight, qkv_mean, qkv_square, reduced_qkv, D ** (-0.5), decay_rate
    )
    out_master, out_first, out_second = adam_update(
        out_weight, out_mean, out_square, reduced_out, OUT_FAN ** (-0.5), decay_rate
    )
    gateup_master, gateup_first, gateup_second = adam_update(
        gateup_weight, gateup_mean, gateup_square, reduced_gateup, D ** (-0.5), decay_rate
    )
    down_master, down_first, down_second = adam_update(
        down_weight, down_mean, down_square, reduced_down, FF ** (-0.5), decay_rate
    )
    gains_master, gains_first, gains_second = adam_update(
        norm_gains, gains_mean, gains_square, reduced_gains, gain_rate, 0.0
    )
    return (
        layer_out,
        tokens_grad,
        qkv_master,
        qkv_first,
        qkv_second,
        out_master,
        out_first,
        out_second,
        gateup_master,
        gateup_first,
        gateup_second,
        down_master,
        down_first,
        down_second,
        gains_master,
        gains_first,
        gains_second,
    )


def solution(mesh):
    part = D // mesh.shape["wide"]
    fits = mesh.shape["narrow"] == 4 and mesh.shape["wide"] == 8 and part % 32 == 0
    return jax.shard_map(
        shards_fast if fits else shards,
        mesh=mesh,
        in_specs=(
            P(("wide", "narrow"), None),
            P("wide"),
            P(None, "wide", "narrow"),
            P("narrow", "wide"),
            P(None, "wide", "narrow"),
            P("narrow", "wide"),
            P(None, "wide"),
            P(None, "wide", "narrow"),
            P(None, "wide", "narrow"),
            P("narrow", "wide"),
            P("narrow", "wide"),
            P(None, "wide", "narrow"),
            P(None, "wide", "narrow"),
            P("narrow", "wide"),
            P("narrow", "wide"),
            P(None, "wide"),
            P(None, "wide"),
            P(("wide", "narrow"), None),
        ),
        out_specs=(
            P(("wide", "narrow"), None),
            P(("wide", "narrow"), None),
            P(None, "wide", "narrow"),
            P(None, "wide", "narrow"),
            P(None, "wide", "narrow"),
            P("narrow", "wide"),
            P("narrow", "wide"),
            P("narrow", "wide"),
            P(None, "wide", "narrow"),
            P(None, "wide", "narrow"),
            P(None, "wide", "narrow"),
            P("narrow", "wide"),
            P("narrow", "wide"),
            P("narrow", "wide"),
            P(None, "wide"),
            P(None, "wide"),
            P(None, "wide"),
        ),
        check_vma=False,
    )
```
